128 devices in a mesh: ctx: 16 (over y, x_lo, core), pb: 8 (over z, x_hi).
Axes of the slice: x: 4 (x_hi: 2, x_lo: 2; x = x_hi * 2 + x_lo), y: 4, z: 4, core: 2. Of those that a mesh axis runs over, the one named last changes fastest.
Arguments:
- embed_prev: bfloat16 [4096, 2048], P('ctx'), may hold values from -16 to 16
- w_query: bfloat16 [2048, 2048], P(None, 'pb'), may hold values from -1 to 1
- w_key: bfloat16 [2048, 2048], P(None, 'pb'), may hold values from -1 to 1
- w_value: bfloat16 [2048, 2048], P(None, 'pb'), may hold values from -0.125 to 0.125
- w_out: bfloat16 [2048, 2048], P('pb'), may hold values from -1 to 1
- byte_ids: int32 [4096, 8], P(('ctx', 'pb')), may hold values from 0 to 255
- pad_embed: bfloat16 [512], replicated, may hold values from -3 to 3
- byte_table: bfloat16 [256, 512], replicated, may hold values from -5 to 5
- w_link: bfloat16 [256, 512], replicated, may hold values from -0.375 to 0.375
- w_local_qkv: bfloat16 [512, 1536], replicated, may hold values from -1 to 1
- w_local_out: bfloat16 [512, 512], replicated, may hold values from -0.25 to 0.25
- w_vocab: bfloat16 [512, 256], replicated, may hold values from -3 to 3
Outputs:
- grad_query: bfloat16 [2048, 2048], P('ctx', 'pb')
- grad_key: bfloat16 [2048, 2048], P('ctx', 'pb')
- grad_value: bfloat16 [2048, 2048], P('ctx', 'pb')
- grad_out: bfloat16 [2048, 2048], P('pb', 'ctx')
The draws below stay inside these ranges and needn't reach their ends.
All inputs are finite; a program needn't handle non-finite values.
Results may differ from the reference program's by a relative error of at most 0.035.
Values may be sent and summed in bfloat16 or wider, within the bound.
A program may use at most 128 MiB of HBM per device.

```python
import math
import jax
import jax.numpy as jnp
import numpy as np
from jax import lax

DG = 2048
HD = 128
HG = 16
PATCH = 8
BW = 256
DL = 512
LHD = 64
LH = 8
VOCAB = 256
NP = 4096


def global_axes(key):
    base = jax.random.fold_in(key, 501)
    first, second, third = jax.random.split(base, 3)
    sign_dir = jax.random.rademacher(first, (DG,), jnp.float32)
    head_dir = jax.random.rademacher(second, (HG, HD), jnp.float32)
    head_gain = jax.random.uniform(third, (HG,), jnp.float32, 1.0, 1.4)
    return (sign_dir, head_dir, head_gain)


def local_axes(key):
    base = jax.random.fold_in(key, 502)
    first, second, third, fourth = jax.random.split(base, 4)
    sign_local = jax.random.rademacher(first, (DL,), jnp.float32)
    local_dir = jax.random.rademacher(second, (LH, LHD), jnp.float32)
    local_gain = jax.random.uniform(third, (LH,), jnp.float32, 2.0, 2.4)
    vocab_gain = jax.random.uniform(fourth, (), jnp.float32, 9.5, 11.5)
    return (sign_local, local_dir, local_gain, vocab_gain)


def projection_with(key, sign_dir, head_dir, head_gain):
    random_part = jnp.clip(jax.random.normal(key, (DG, DG), jnp.float32), -4.0, 4.0) * DG ** (-0.5)
    column = (head_dir * head_gain[:, None]).reshape(DG)
    return random_part + sign_dir[:, None] * column[None, :] * (DG * HD) ** (-0.5)


def draw_embed_prev(key, part):
    sign_dir, head_dir, head_gain = global_axes(key)
    key = jax.random.fold_in(key, 11)
    first, second, third, fourth = jax.random.split(key, 4)
    noise = jnp.clip(jax.random.normal(first, (NP, DG), jnp.float32), -4.0, 4.0)
    row_scale = jnp.exp(jax.random.uniform(second, (NP, 1), jnp.float32, math.log(0.5), math.log(4.0)))
    chosen = jax.random.randint(third, (NP, 1), 0, 64) == 0
    strength = jax.random.uniform(fourth, (NP, 1), jnp.float32, 0.7, 0.97)
    aligned = jnp.where(chosen, strength, 0.0)
    return (row_scale * (aligned * sign_dir[None, :] + jnp.sqrt(1.0 - aligned * aligned) * noise)).astype(jnp.bfloat16)


def draw_w_query(key, part):
    sign_dir, head_dir, head_gain = global_axes(key)
    key = jax.random.fold_in(key, 12)
    return projection_with(key, sign_dir, head_dir, head_gain).astype(jnp.bfloat16)


def draw_w_key(key, part):
    sign_dir, head_dir, head_gain = global_axes(key)
    key = jax.random.fold_in(key, 13)
    return projection_with(key, sign_dir, head_dir, head_gain).astype(jnp.bfloat16)


def draw_byte_table(key, part):
    sign_local, local_dir, local_gain, vocab_gain = local_axes(key)
    key = jax.random.fold_in(key, 21)
    first, second, third = jax.random.split(key, 3)
    random_part = jnp.clip(jax.random.normal(first, (VOCAB, DL), jnp.float32) * 0.25, -1.0, 1.0)
    chosen = jax.random.randint(second, (VOCAB, 1), 0, 4) == 0
    strength = jax.random.uniform(third, (VOCAB, 1), jnp.float32, 2.0, 4.0)
    return (random_part + jnp.where(chosen, strength, 0.0) * sign_local[None, :]).astype(jnp.bfloat16)


def draw_w_local_qkv(key, part):
    sign_local, local_dir, local_gain, vocab_gain = local_axes(key)
    key = jax.random.fold_in(key, 22)
    random_part = jnp.clip(jax.random.normal(key, (DL, 3 * DL), jnp.float32), -4.0, 4.0) * DL ** (-0.5)
    column = (local_dir * local_gain[:, None]).reshape(DL)
    zeros_block = jnp.zeros((DL,), jnp.float32)
    columns = jnp.concatenate([column, column, zeros_block], axis=0)
    return (random_part + sign_local[:, None] * columns[None, :] * (DL * LHD) ** (-0.5)).astype(jnp.bfloat16)


def draw_w_vocab(key, part):
    sign_local, local_dir, local_gain, vocab_gain = local_axes(key)
    key = jax.random.fold_in(key, 23)
    first, second, third = jax.random.split(key, 3)
    random_part = jnp.clip(jax.random.normal(first, (DL, VOCAB), jnp.float32), -4.0, 4.0) * DL ** (-0.5)
    column_one = jax.random.randint(second, (), 0, VOCAB)
    column_two = (column_one + 1 + jax.random.randint(third, (), 0, VOCAB - 1)) % VOCAB
    indices = lax.iota(jnp.int32, VOCAB)
    gains = jnp.where(indices == column_one, vocab_gain, 0.0) + jnp.where(indices == column_two, vocab_gain + 0.1, 0.0)
    return (random_part + sign_local[:, None] * gains[None, :] * DL ** (-0.5)).astype(jnp.bfloat16)


def place_ends(entries, own_key, low, high):
    spot = [jax.random.randint(jax.random.fold_in(own_key, axis), (), 0, length) for axis, length in enumerate(entries.shape)]
    longest = entries.shape.index(max(entries.shape))
    beside = spot[:longest] + [(spot[longest] + 1) % entries.shape[longest]] + spot[longest + 1:]
    return entries.at[tuple(spot)].set(low).at[tuple(beside)].set(high)


def block_levels(own_key, shape, cuts, least, top_value):
    def one(dim, blocks):
        draws = jax.random.uniform(jax.random.fold_in(jax.random.fold_in(own_key, 6), dim), (blocks,), jnp.float32, least / len(cuts), top_value / len(cuts))
        return jnp.repeat(jnp.exp(draws), shape[dim] // blocks).reshape((-1,) + (1,) * (len(shape) - dim - 1))

    level = one(*cuts[0])
    for cut in cuts[1:]:
        level = level * one(*cut)
    return level


def rank_bounds(amount, skew):
    weights = [(1 << 20) // math.isqrt(standing ** skew) + 1 for standing in range(1, amount + 1)]
    scale = 1 + sum(weights) // (1 << 30)
    return np.cumsum(np.array([max(1, weight // scale) for weight in weights]))


def ranked(stream_key, extent, count, slope):
    listing = rank_bounds(count, slope)
    lot = jax.random.randint(jax.random.fold_in(stream_key, 1), extent, 0, int(listing[count - 1]))
    standing = jnp.searchsorted(jnp.asarray(listing, jnp.int32), lot, side="right")
    return jax.random.permutation(jax.random.fold_in(stream_key, 2), count)[standing].astype(jnp.int32)


def scatter_about(own_key, dims, deviation, bound, shards=(), held_as=jnp.bfloat16):
    values = deviation * jax.random.normal(own_key, dims, jnp.float32)
    if shards:
        values = values * block_levels(own_key, dims, shards, -0.22, 0.18)
    return jnp.clip(values, -bound, bound).astype(held_as)


def setup_inputs(seed: int = 0) -> dict:
    streams_of = jax.random.split(jax.random.key(seed), 13)
    embed_prev = draw_embed_prev(jax.random.fold_in(streams_of[12], 71), 0)
    w_query = draw_w_query(jax.random.fold_in(streams_of[12], 71), 0)
    w_key = draw_w_key(jax.random.fold_in(streams_of[12], 71), 0)
    w_value = scatter_about(streams_of[3], (DG, DG), DG ** -0.5, 0.125, ((1, 8),))
    w_out = scatter_about(streams_of[4], (DG, DG), (DG // 64) ** -0.5, 1.0, ((0, 8),))
    byte_ids = place_ends(ranked(streams_of[5], (NP, PATCH), VOCAB, 2), jax.random.fold_in(streams_of[5], 3), 0, VOCAB - 1).astype(jnp.int32)
    pad_embed = scatter_about(streams_of[6], (DL,), 0.5, 3.0)
    byte_table = draw_byte_table(jax.random.fold_in(streams_of[12], 71), 0)
    w_link = scatter_about(streams_of[8], (BW, DL), BW ** -0.5, 0.375)
    w_local_qkv = draw_w_local_qkv(jax.random.fold_in(streams_of[12], 71), 0)
    w_local_out = scatter_about(streams_of[10], (DL, DL), DL ** -0.5, 0.25)
    w_vocab = draw_w_vocab(jax.random.fold_in(streams_of[12], 71), 0)
    return {"embed_prev": embed_prev, "w_query": w_query, "w_key": w_key, "w_value": w_value, "w_out": w_out, "byte_ids": byte_ids, "pad_embed": pad_embed, "byte_table": byte_table, "w_link": w_link, "w_local_qkv": w_local_qkv, "w_local_out": w_local_out, "w_vocab": w_vocab}


epsilon = 1e-06
masked_value = -1e+30

def rounded(values):
    return lax.optimization_barrier(values.astype(jnp.bfloat16)).astype(jnp.float32)

def rms_round(values):
    return (values * lax.rsqrt(lax.optimization_barrier(jnp.mean(values * values, axis=1, keepdims=True)) + epsilon)).astype(jnp.bfloat16)

def local_loss(glob, byte_ids, pad_embed, byte_table, w_link, w_local_qkv, w_local_out, w_vocab, total_bytes):
    patches, patch = byte_ids.shape
    count_rows = patches * patch
    width = w_link.shape[1]
    heads = width // LHD
    pieces = glob.reshape(count_rows, glob.shape[1] // patch)
    earlier = jnp.concatenate([jnp.zeros((patches, 1), jnp.int32), byte_ids[:, :-1]], axis=1).reshape(count_rows, 1)
    leading = (lax.broadcasted_iota(jnp.int32, (patches, patch), 1) == 0).reshape(count_rows, 1)
    symbols = lax.broadcasted_iota(jnp.int32, (1, byte_table.shape[0]), 1)
    table_hot = jnp.logical_and(earlier == symbols, jnp.logical_not(leading)).astype(jnp.bfloat16)
    embedded = jnp.dot(table_hot, byte_table, preferred_element_type=jnp.float32)
    hidden_state = embedded + jnp.where(leading, pad_embed.astype(jnp.float32)[None, :], 0.0)
    hidden_state = hidden_state + jnp.dot(pieces, w_link, preferred_element_type=jnp.float32)
    mixed = jnp.dot(rms_round(hidden_state), w_local_qkv, preferred_element_type=jnp.float32)
    mixed = rounded(mixed).reshape(patches, patch, 3, heads, LHD)
    queries = mixed[:, :, 0]
    keys = mixed[:, :, 1]
    values = mixed[:, :, 2]
    scores = jnp.einsum('rphd,rqhd->rhpq', queries, keys) * LHD ** (-0.5)
    causal = lax.broadcasted_iota(jnp.int32, (patch, patch), 0) >= lax.broadcasted_iota(jnp.int32, (patch, patch), 1)
    scores = jnp.where(causal, scores, masked_value)
    weights = rounded(jax.nn.softmax(scores, axis=-1))
    attended = jnp.einsum('rhpq,rqhd->rphd', weights, values).astype(jnp.bfloat16).reshape(count_rows, width)
    hidden_state = hidden_state + jnp.dot(attended, w_local_out, preferred_element_type=jnp.float32)
    logits = jnp.dot(rms_round(hidden_state), w_vocab, preferred_element_type=jnp.float32)
    highest = lax.stop_gradient(lax.optimization_barrier(jnp.max(logits, axis=1, keepdims=True)))
    log_norm = highest[:, 0] + jnp.log(lax.optimization_barrier(jnp.sum(jnp.exp(logits - highest), axis=1)))
    target_hot = byte_ids.reshape(count_rows, 1) == lax.broadcasted_iota(jnp.int32, (1, logits.shape[1]), 1)
    picked = lax.optimization_barrier(jnp.sum(jnp.where(target_hot, logits, 0.0), axis=1))
    return jnp.sum(log_norm - picked) / total_bytes

def split_heads(values):
    return lax.optimization_barrier(values).astype(jnp.float32).reshape(NP, DG // HD, HD).transpose(1, 0, 2)

def merge_heads(values):
    return values.transpose(1, 0, 2).reshape(NP, DG)

def reference(embed_prev, w_query, w_key, w_value, w_out, byte_ids, pad_embed, byte_table, w_link, w_local_qkv, w_local_out, w_vocab):
    scale = HD ** (-0.5)
    block = min(512, NP)
    starts = lax.iota(jnp.int32, NP // block) * block
    every_pos = lax.iota(jnp.int32, NP)
    widened = embed_prev.astype(jnp.float32)
    normed = rms_round(widened)
    query = jnp.dot(normed, w_query, preferred_element_type=jnp.float32).astype(jnp.bfloat16)
    key = jnp.dot(normed, w_key, preferred_element_type=jnp.float32).astype(jnp.bfloat16)
    value = jnp.dot(normed, w_value, preferred_element_type=jnp.float32).astype(jnp.bfloat16)

    def head_forward(operands):
        queries, keys, values = operands

        def query_block(start):
            block_q = lax.dynamic_slice_in_dim(queries, start, block, 0)
            block_pos = start + lax.iota(jnp.int32, block)
            scores = jnp.dot(block_q, keys.T) * scale
            allowed = every_pos[None, :] <= block_pos[:, None]
            scores = jnp.where(allowed, scores, masked_value)
            highest = lax.optimization_barrier(jnp.max(scores, axis=1, keepdims=True))
            weights = jnp.where(allowed, jnp.exp(scores - highest), 0.0)
            totals = lax.optimization_barrier(jnp.sum(weights, axis=1, keepdims=True))
            attended = (jnp.dot(rounded(weights), values) / totals).astype(jnp.bfloat16)
            return (attended, (highest + jnp.log(totals))[:, 0])
        attended, log_total = lax.map(query_block, starts)
        return (attended.reshape(NP, HD), log_total.reshape(NP))
    heads_q = split_heads(query)
    heads_k = split_heads(key)
    heads_v = split_heads(value)
    attended, log_total = lax.map(head_forward, (heads_q, heads_k, heads_v))
    attended = merge_heads(attended)
    glob = jnp.dot(attended, w_out, preferred_element_type=jnp.float32).astype(jnp.bfloat16)
    loss_value, pullback = jax.vjp(lambda inner: local_loss(inner, byte_ids, pad_embed, byte_table, w_link, w_local_qkv, w_local_out, w_vocab, NP * PATCH), glob)
    glob_grad = pullback(jnp.ones_like(loss_value))[0]
    attended_grad = jnp.dot(glob_grad, w_out.T, preferred_element_type=jnp.float32).astype(jnp.bfloat16)
    row_dots = lax.optimization_barrier(jnp.sum((attended_grad.astype(jnp.float32) * attended.astype(jnp.float32)).reshape(NP, DG // HD, HD), axis=2)).T
    heads_g = split_heads(attended_grad)

    def head_backward(operands):
        queries, keys, values, grads, log_total_h, dots_h = operands

        def query_block(start):
            block_q = lax.dynamic_slice_in_dim(queries, start, block, 0)
            block_g = lax.dynamic_slice_in_dim(grads, start, block, 0)
            block_l = lax.dynamic_slice_in_dim(log_total_h, start, block, 0)
            block_d = lax.dynamic_slice_in_dim(dots_h, start, block, 0)
            block_pos = start + lax.iota(jnp.int32, block)
            scores = jnp.dot(block_q, keys.T) * scale
            allowed = every_pos[None, :] <= block_pos[:, None]
            probs = jnp.where(allowed, jnp.exp(scores - block_l[:, None]), 0.0)
            prob_grads = jnp.dot(block_g, values.T)
            score_grad = rounded(probs * (prob_grads - block_d[:, None]) * scale)
            return jnp.dot(score_grad, keys).astype(jnp.bfloat16)

        def key_block(start):
            block_k = lax.dynamic_slice_in_dim(keys, start, block, 0)
            block_v = lax.dynamic_slice_in_dim(values, start, block, 0)
            block_pos = start + lax.iota(jnp.int32, block)
            scores = jnp.dot(queries, block_k.T) * scale
            allowed = block_pos[None, :] <= every_pos[:, None]
            probs = jnp.where(allowed, jnp.exp(scores - log_total_h[:, None]), 0.0)
            prob_grads = jnp.dot(grads, block_v.T)
            score_grad = rounded(probs * (prob_grads - dots_h[:, None]) * scale)
            key_grad = jnp.dot(score_grad.T, queries).astype(jnp.bfloat16)
            value_grad = jnp.dot(rounded(probs).T, grads).astype(jnp.bfloat16)
            return (key_grad, value_grad)
        query_grad = lax.map(query_block, starts).reshape(NP, HD)
        key_grad, value_grad = lax.map(key_block, starts)
        return (query_grad, key_grad.reshape(NP, HD), value_grad.reshape(NP, HD))
    query_grad, key_grad, value_grad = lax.map(head_backward, (heads_q, heads_k, heads_v, heads_g, log_total, row_dots))
    contract = (((0,), (0,)), ((), ()))
    grad_query = lax.dot_general(normed, merge_heads(query_grad), contract, preferred_element_type=jnp.float32).astype(jnp.bfloat16)
    grad_key = lax.dot_general(normed, merge_heads(key_grad), contract, preferred_element_type=jnp.float32).astype(jnp.bfloat16)
    grad_value = lax.dot_general(normed, merge_heads(value_grad), contract, preferred_element_type=jnp.float32).astype(jnp.bfloat16)
    grad_out = lax.dot_general(attended, glob_grad, contract, preferred_element_type=jnp.float32).astype(jnp.bfloat16)
    return (grad_query, grad_key, grad_value, grad_out)
```

```python
import functools

import jax
import jax.numpy as jnp
from jax import lax
from jax.experimental import pallas as pl
from jax.experimental.pallas import tpu as pltpu
from jax.sharding import PartitionSpec as P

HD = 128
LHD = 64
PATCH = 8
EPSILON = 1e-06
MASKED = -1e30
MESH = pl.DeviceIdType.MESH
BF = jnp.bfloat16
F32 = jnp.float32


def nn(left, right):
    return lax.dot_general(left, right, (((1,), (0,)), ((), ())), preferred_element_type=F32)


def nt(left, right):
    return lax.dot_general(left, right, (((1,), (1,)), ((), ())), preferred_element_type=F32)


def tn(left, right):
    return lax.dot_general(left, right, (((0,), (0,)), ((), ())), preferred_element_type=F32)


def loop(low, high, body):
    def step(index, unused):
        body(index)
        return unused

    lax.fori_loop(low, high, step, 0)


def row_form(column, rows):
    return jnp.transpose(jnp.broadcast_to(column, (rows, HD)))[0:8]


def rms_inverse(values):
    return lax.rsqrt(jnp.mean(values * values, axis=1, keepdims=True) + EPSILON)


def rms_back(values, inverse, grad):
    width = values.shape[1]
    dots = jnp.sum(grad * values, axis=1, keepdims=True)
    return inverse * grad - values * (inverse * inverse * inverse * dots * (1.0 / width))


def step_kernel(
    sizes,
    embed,
    w_query,
    w_key,
    w_value,
    w_out,
    ids,
    pad_embed,
    table,
    w_link,
    w_mix,
    w_local_out,
    w_vocab,
    grad_query,
    grad_key,
    grad_value,
    grad_out,
    normed,
    kv_send,
    kv_all,
    q_send,
    q_all,
    run_max,
    run_sum,
    run_out,
    att_head,
    att_pair,
    lse_col,
    lse_all,
    glob_part,
    glob_in,
    hidden,
    mixed,
    weights,
    d_mixed,
    grad_all,
    da_send,
    da_all,
    dots_send,
    dots_all,
    dq_acc,
    dk_acc,
    dv_acc,
    wq_send,
    wo_send,
    wkv_send,
    wq_in,
    wo_in,
    wkv_in,
    kv_s,
    kv_r,
    q_s,
    q_r,
    da_s,
    da_r,
    dots_s,
    dots_r,
    wq_s,
    wq_r,
    wo_s,
    wo_r,
    wkv_s,
    wkv_r,
    lse_s,
    lse_r,
    glob_s,
    glob_r,
    grad_s,
    grad_r,
    norm_s,
    norm_r,
    att_s,
    att_r,
    full_s,
    full_r,
):
    nctx, npb = sizes
    chips = nctx // 2
    rows, wide = embed.shape
    patches = rows // npb
    bytes_here = patches * PATCH
    scale = HD ** (-0.5)
    place = lax.axis_index("ctx")
    part = lax.axis_index("pb")
    chip = place // 2
    core = place % 2
    other = place + 1 - 2 * core

    def ctx_copy(src, dst, send, recv, peer):
        return pltpu.make_async_remote_copy(
            src_ref=src,
            dst_ref=dst,
            send_sem=send,
            recv_sem=recv,
            device_id=(peer, part),
            device_id_type=MESH,
        )

    def pb_copy(src, dst, send, recv, peer):
        return pltpu.make_async_remote_copy(
            src_ref=src,
            dst_ref=dst,
            send_sem=send,
            recv_sem=recv,
            device_id=(place, peer),
            device_id_type=MESH,
        )

    def each_peer(wanted, action):
        def one(step):
            peer = (place + step) % nctx

            @pl.when(wanted(peer // 2))
            def _():
                action(peer)

        loop(1, nctx, one)

    def each_part(action):
        loop(1, npb, lambda step: action((part + step) % npb))

    later = lambda at: at >= chip
    earlier = lambda at: at <= chip
    anyone = lambda at: at >= 0

    barrier = pltpu.get_barrier_semaphore()

    def greet_ctx(peer):
        pl.semaphore_signal(barrier, inc=1, device_id=(peer, part), device_id_type=MESH)

    def greet_part(peer):
        pl.semaphore_signal(barrier, inc=1, device_id=(place, peer), device_id_type=MESH)

    each_peer(anyone, greet_ctx)
    each_part(greet_part)

    tile_rows = min(32, rows)

    def norm_rows(step):
        here = pl.ds(pl.multiple_of(step * tile_rows, tile_rows), tile_rows)
        values = embed[here, :].astype(F32)
        normed[core, here, :] = (values * rms_inverse(values)).astype(BF)

    loop(0, rows // tile_rows, norm_rows)
    own_normed = normed[core]
    for slot, weight in ((0, w_key), (1, w_value)):
        product = nn(own_normed, weight[...]).astype(BF)
        kv_send[0, slot] = product[:, :HD]
        kv_send[1, slot] = product[:, HD:]
    pl.semaphore_wait(barrier, nctx + npb - 2)

    def kv_copy(peer):
        return ctx_copy(
            kv_send.at[peer % 2], kv_all.at[:, place], kv_s.at[peer], kv_r.at[place], peer
        )

    each_peer(later, lambda peer: kv_copy(peer).start())
    kv_all[:, place] = kv_send[core]
    product = nn(own_normed, w_query[...]).astype(BF)
    q_send[0] = product[:, :HD]
    q_send[1] = product[:, HD:]

    def q_copy(peer):
        return ctx_copy(q_send.at[peer % 2], q_all.at[place], q_s.at[peer], q_r.at[place], peer)

    q_copy(other).start()
    q_all[place] = q_send[core]

    def norm_copy(index):
        return ctx_copy(normed.at[index], normed.at[index], norm_s, norm_r, other)

    norm_copy(core).start()
    strictly_earlier = lambda at: at < chip
    each_peer(strictly_earlier, lambda peer: q_copy(peer).start())

    def kv_wait(peer):
        ctx_copy(kv_send.at[0], kv_all.at[:, peer], kv_s.at[peer], kv_r.at[peer], peer).wait_recv()

    def q_wait(peer):
        ctx_copy(q_send.at[0], q_all.at[peer], q_s.at[peer], q_r.at[peer], peer).wait_recv()

    first = 2 * chip
    pair_rows = 2 * rows

    def keys_of(at):
        return kv_all[0, pl.ds(2 * at, 2)].reshape(pair_rows, HD)

    def values_of(at):
        return kv_all[1, pl.ds(2 * at, 2)].reshape(pair_rows, HD)

    def diagonal(half, keys_down):
        shape = (rows, pair_rows)
        here = lax.broadcasted_iota(jnp.int32, shape, 0) + half * rows
        there = lax.broadcasted_iota(jnp.int32, shape, 1)
        return (there >= here) if keys_down else (there <= here)

    run_max[...] = jnp.full(run_max.shape, MASKED, F32)
    run_sum[...] = jnp.zeros(run_sum.shape, F32)
    run_out[...] = jnp.zeros(run_out.shape, F32)

    def attend(half, at, on_diagonal):
        scores = nt(q_all[first + half], keys_of(at)) * scale
        if on_diagonal:
            scores = jnp.where(diagonal(half, False), scores, MASKED)
        before = run_max[half, :, 0:1]
        highest = jnp.maximum(before, jnp.max(scores, axis=1, keepdims=True))
        exps = jnp.exp(scores - highest)
        factor = jnp.exp(before - highest)
        total = run_sum[half, :, 0:1] * factor + jnp.sum(exps, axis=1, keepdims=True)
        run_out[half] = run_out[half] * factor + nn(exps.astype(BF), values_of(at))
        run_max[half] = jnp.broadcast_to(highest, (rows, HD))
        run_sum[half] = jnp.broadcast_to(total, (rows, HD))

    kv_wait(other)
    q_wait(other)
    for half in (0, 1):
        attend(half, chip, True)

    def attend_earlier(step):
        at = chip - step
        kv_wait(2 * at)
        kv_wait(2 * at + 1)
        for half in (0, 1):
            attend(half, at, False)

    loop(1, chip + 1, attend_earlier)
    for half in (0, 1):
        att_head[half] = (run_out[half] / run_sum[half]).astype(BF)
        log_total = run_max[half] + jnp.log(run_sum[half])
        lse_col[half] = log_total
        lse_all[chip, half] = jnp.transpose(log_total)[0:8]

    def att_copy():
        return ctx_copy(att_head.at[1 - core], att_pair.at[core], att_s, att_r, other)

    att_copy().start()
    att_pair[core] = att_head[core]

    def lse_copy(at):
        return ctx_copy(
            lse_all.at[chip], lse_all.at[chip], lse_s.at[at], lse_r.at[chip], 2 * at + core
        )

    loop(0, chip, lambda at: lse_copy(at).start())
    ctx_copy(att_head.at[0], att_pair.at[1 - core], att_s, att_r, other).wait_recv()

    both_heads = jnp.concatenate([att_pair[0], att_pair[1]], axis=1)
    out_tile = min(512, wide)

    def out_columns(step):
        here = pl.ds(pl.multiple_of(step * out_tile, out_tile), out_tile)
        product = nn(both_heads, w_out[:, here]).astype(BF)
        glob_part[:, :, here] = product.reshape(npb, patches, out_tile)

    loop(0, wide // out_tile, out_columns)

    def glob_copy(peer):
        return pb_copy(
            glob_part.at[peer], glob_in.at[part], glob_s.at[peer], glob_r.at[part], peer
        )

    each_part(lambda peer: glob_copy(peer).start())
    glob_in[part] = glob_part[part]

    ids_here = ids[...]
    targets = jnp.concatenate([ids_here[:, b : b + 1] for b in range(PATCH)], axis=0)
    nothing = jnp.full((patches, 1), -1, jnp.int32)
    preceding = jnp.concatenate(
        [nothing] + [ids_here[:, b : b + 1] for b in range(PATCH - 1)], axis=0
    )
    symbols = lax.broadcasted_iota(jnp.int32, (bytes_here, table.shape[0]), 1)
    table_hot = (preceding == symbols).astype(BF)
    leading = preceding < 0
    hidden[...] = nn(table_hot, table[...]) + jnp.where(
        leading, pad_embed[...].astype(F32), 0.0
    )

    def glob_wait(peer):
        pb_copy(
            glob_part.at[0], glob_in.at[peer], glob_s.at[peer], glob_r.at[peer], peer
        ).wait_recv()

    each_part(glob_wait)
    glob = glob_in[0].astype(F32)
    for index in range(1, npb):
        glob = glob + glob_in[index].astype(F32)
    glob = glob.astype(BF)
    byte_wide = wide // PATCH
    pieces = jnp.concatenate(
        [glob[:, b * byte_wide : (b + 1) * byte_wide] for b in range(PATCH)], axis=0
    )
    hidden[...] += nn(pieces, w_link[...])
    hidden_one = hidden[...]
    inverse_one = rms_inverse(hidden_one)
    mixed[...] = nn((hidden_one * inverse_one).astype(BF), w_mix[...]).astype(BF)
    local_wide = w_link.shape[1]
    row_index = lax.broadcasted_iota(jnp.int32, (bytes_here, bytes_here), 0)
    column_index = lax.broadcasted_iota(jnp.int32, (bytes_here, bytes_here), 1)
    same = jnp.logical_and(
        lax.rem(row_index, patches) == lax.rem(column_index, patches), column_index <= row_index
    )
    lane = lax.broadcasted_iota(jnp.int32, (bytes_here, 2 * LHD), 1)
    halves = (lane < LHD, lane >= LHD)
    pairs = local_wide // (2 * LHD)

    def pair_of(block, pair):
        low = block * local_wide + pair * 2 * LHD
        return mixed[:, low : low + 2 * LHD]

    def kept(values, side):
        return jnp.where(halves[side], values, jnp.zeros_like(values))

    local_att = []
    for pair in range(pairs):
        summed = None
        for side in (0, 1):
            scores = nt(kept(pair_of(0, pair), side), pair_of(1, pair)) * LHD ** (-0.5)
            scores = jnp.where(same, scores, MASKED)
            exps = jnp.exp(scores - jnp.max(scores, axis=1, keepdims=True))
            soft = exps / jnp.sum(exps, axis=1, keepdims=True)
            weights[2 * pair + side] = soft
            term = nn(soft.astype(BF), kept(pair_of(2, pair), side))
            summed = term if summed is None else summed + term
        local_att.append(summed.astype(BF))
    hidden_two = hidden[...] + nn(jnp.concatenate(local_att, axis=1), w_local_out[...])
    inverse_two = rms_inverse(hidden_two)
    logits = nn((hidden_two * inverse_two).astype(BF), w_vocab[...])
    exps = jnp.exp(logits - jnp.max(logits, axis=1, keepdims=True))
    soft = exps / jnp.sum(exps, axis=1, keepdims=True)
    d_logits = (soft - jnp.where(targets == symbols, 1.0, 0.0)) * (
        1.0 / (rows * nctx * PATCH)
    )
    d_normed_two = nt(d_logits.astype(BF), w_vocab[...]).astype(BF).astype(F32)
    d_hidden = rms_back(hidden_two, inverse_two, d_normed_two)
    d_local_att = nt(d_hidden.astype(BF), w_local_out[...]).astype(BF)
    for pair in range(pairs):
        low = pair * 2 * LHD
        d_att = d_local_att[:, low : low + 2 * LHD]
        d_query = d_key = d_value = None
        for side in (0, 1):
            soft = weights[2 * pair + side]
            d_side = kept(d_att, side)
            d_soft = nt(d_side, pair_of(2, pair)).astype(BF).astype(F32)
            dots = jnp.sum(d_soft * soft, axis=1, keepdims=True)
            d_scores = (soft * (d_soft - dots) * LHD ** (-0.5)).astype(BF)
            value_term = tn(soft.astype(BF), d_side)
            query_term = nn(d_scores, kept(pair_of(1, pair), side))
            key_term = tn(d_scores, kept(pair_of(0, pair), side))
            if side == 0:
                d_query, d_key, d_value = query_term, key_term, value_term
            else:
                d_query, d_key, d_value = (
                    d_query + query_term,
                    d_key + key_term,
                    d_value + value_term,
                )
        for block, term in enumerate((d_query, d_key, d_value)):
            at = block * local_wide + low
            d_mixed[:, at : at + 2 * LHD] = term.astype(BF)
    d_normed_one = nt(d_mixed[...], w_mix[...]).astype(BF).astype(F32)
    d_hidden = d_hidden + rms_back(hidden[...], rms_inverse(hidden[...]), d_normed_one)
    d_pieces = nt(d_hidden.astype(BF), w_link[...]).astype(BF)
    for b in range(PATCH):
        grad_all[core, part, :, b * byte_wide : (b + 1) * byte_wide] = d_pieces[
            b * patches : (b + 1) * patches
        ]

    def grad_copy(peer):
        mine = grad_all.at[core, part]
        return pb_copy(mine, mine, grad_s.at[peer], grad_r.at[part], peer)

    def grad_wait(peer):
        theirs = grad_all.at[core, peer]
        pb_copy(theirs, theirs, grad_s.at[peer], grad_r.at[peer], peer).wait_recv()

    each_part(lambda peer: grad_copy(peer).start())
    each_part(grad_wait)

    def full_copy(index):
        return ctx_copy(grad_all.at[index], grad_all.at[index], full_s, full_r, other)

    full_copy(core).start()
    product = nt(grad_all[core].reshape(rows, wide), w_out[...]).astype(BF)
    for head in (0, 1):
        d_att = product[:, head * HD : (head + 1) * HD]
        da_send[head] = d_att
        dots = jnp.sum(d_att.astype(F32) * att_pair[head].astype(F32), axis=1, keepdims=True)
        dots_send[head] = row_form(dots, rows)

    def da_copy(peer):
        return ctx_copy(
            da_send.at[peer % 2], da_all.at[place], da_s.at[peer], da_r.at[place], peer
        )

    def dots_copy(peer):
        return ctx_copy(
            dots_send.at[peer % 2], dots_all.at[place], dots_s.at[peer], dots_r.at[place], peer
        )

    def da_start(peer):
        da_copy(peer).start()
        dots_copy(peer).start()

    def da_wait(peer):
        ctx_copy(da_send.at[0], da_all.at[peer], da_s.at[peer], da_r.at[peer], peer).wait_recv()
        ctx_copy(
            dots_send.at[0], dots_all.at[peer], dots_s.at[peer], dots_r.at[peer], peer
        ).wait_recv()

    each_peer(earlier, da_start)
    da_all[place] = da_send[core]
    dots_all[place] = dots_send[core]
    da_wait(other)

    dq_acc[...] = jnp.zeros(dq_acc.shape, F32)

    def query_back(half, at, on_diagonal):
        scores = nt(q_all[first + half], keys_of(at)) * scale
        probs = jnp.exp(scores - lse_col[half, :, 0:1])
        if on_diagonal:
            probs = jnp.where(diagonal(half, False), probs, 0.0)
        d_probs = nt(da_all[first + half], values_of(at))
        d_scores = (probs * (d_probs - run_sum[half, :, 0:1]) * scale).astype(BF)
        dq_acc[half] += nn(d_scores, keys_of(at))

    for half in (0, 1):
        dots = jnp.sum(
            da_all[first + half].astype(F32) * att_head[half].astype(F32), axis=1, keepdims=True
        )
        run_sum[half] = jnp.broadcast_to(dots, (rows, HD))
    for half in (0, 1):
        query_back(half, chip, True)

    def query_earlier(step):
        for half in (0, 1):
            query_back(half, chip - step, False)

    loop(1, chip + 1, query_earlier)

    block_wide = wide // nctx

    def turned(values):
        return jnp.transpose(values.reshape(pair_rows, HD).astype(F32)).astype(BF)

    def normed_block(owner):
        here = pl.ds(pl.multiple_of(owner * block_wide, block_wide), block_wide)
        return normed[:, :, here].reshape(pair_rows, block_wide)

    def wq_copy(peer):
        return ctx_copy(wq_send.at[peer], wq_in.at[place], wq_s.at[peer], wq_r.at[place], peer)

    def wo_copy(peer):
        return ctx_copy(wo_send.at[peer], wo_in.at[place], wo_s.at[peer], wo_r.at[place], peer)

    def wkv_copy(peer):
        return ctx_copy(wkv_send.at[peer], wkv_in.at[place], wkv_s.at[peer], wkv_r.at[place], peer)

    norm_copy(1 - core).wait_recv()
    dq_turned = turned(dq_acc[...].astype(BF))

    def wq_block(owner):
        wq_send[owner] = nn(dq_turned, normed_block(owner)).astype(BF)

    loop(0, nctx, wq_block)
    each_peer(anyone, lambda peer: wq_copy(peer).start())
    wq_in[place] = wq_send[place]

    full_copy(1 - core).wait_recv()
    att_turned = turned(att_head[...])

    def wo_block(owner):
        here = pl.ds(pl.multiple_of(owner * block_wide, block_wide), block_wide)
        wo_send[owner] = nn(
            att_turned, grad_all[:, :, :, here].reshape(pair_rows, block_wide)
        ).astype(BF)

    loop(0, nctx, wo_block)
    each_peer(anyone, lambda peer: wo_copy(peer).start())
    wo_in[place] = wo_send[place]

    dk_acc[...] = jnp.zeros(dk_acc.shape, F32)
    dv_acc[...] = jnp.zeros(dv_acc.shape, F32)

    def key_back(half, at, on_diagonal):
        queries = q_all[pl.ds(2 * at, 2)].reshape(pair_rows, HD)
        grads = da_all[pl.ds(2 * at, 2)].reshape(pair_rows, HD)
        log_total = jnp.concatenate([lse_all[at, 0, 0:1, :], lse_all[at, 1, 0:1, :]], axis=1)
        dots = jnp.concatenate([dots_all[2 * at, 0:1, :], dots_all[2 * at + 1, 0:1, :]], axis=1)
        scores = nt(kv_all[0, first + half], queries) * scale
        probs = jnp.exp(scores - log_total)
        if on_diagonal:
            probs = jnp.where(diagonal(half, True), probs, 0.0)
        d_probs = nt(kv_all[1, first + half], grads)
        d_scores = (probs * (d_probs - dots) * scale).astype(BF)
        dv_acc[half] += nn(probs.astype(BF), grads)
        dk_acc[half] += nn(d_scores, queries)

    for half in (0, 1):
        key_back(half, chip, True)

    def key_later(at):
        for peer in (2 * at, 2 * at + 1):
            q_wait(peer)
            da_wait(peer)
        ctx_copy(
            lse_all.at[at], lse_all.at[at], lse_s.at[at], lse_r.at[at], 2 * at + core
        ).wait_recv()
        for half in (0, 1):
            key_back(half, at, False)

    loop(chip + 1, chips, key_later)
    dk_turned = turned(dk_acc[...].astype(BF))
    dv_turned = turned(dv_acc[...].astype(BF))

    def wkv_block(owner):
        block = normed_block(owner)
        wkv_send[owner, 0] = nn(dk_turned, block).astype(BF)
        wkv_send[owner, 1] = nn(dv_turned, block).astype(BF)

    loop(0, nctx, wkv_block)
    each_peer(anyone, lambda peer: wkv_copy(peer).start())
    wkv_in[place] = wkv_send[place]

    def total_of(pick, head):
        total = pick(head).astype(F32)
        for index in range(1, chips):
            total = total + pick(2 * index + head).astype(F32)
        return total

    def wq_wait(peer):
        ctx_copy(wq_send.at[0], wq_in.at[peer], wq_s.at[peer], wq_r.at[peer], peer).wait_recv()

    def wo_wait(peer):
        ctx_copy(wo_send.at[0], wo_in.at[peer], wo_s.at[peer], wo_r.at[peer], peer).wait_recv()

    def wkv_wait(peer):
        ctx_copy(wkv_send.at[0], wkv_in.at[peer], wkv_s.at[peer], wkv_r.at[peer], peer).wait_recv()

    each_peer(anyone, wq_wait)
    for head in (0, 1):
        total = total_of(lambda index: wq_in[index], head)
        grad_query[:, head * HD : (head + 1) * HD] = jnp.transpose(total).astype(BF)
    each_peer(anyone, wo_wait)
    for head in (0, 1):
        total = total_of(lambda index: wo_in[index], head)
        grad_out[head * HD : (head + 1) * HD, :] = total.astype(BF)
    each_peer(anyone, wkv_wait)
    for head in (0, 1):
        total = total_of(lambda index: wkv_in[index, 0], head)
        grad_key[:, head * HD : (head + 1) * HD] = jnp.transpose(total).astype(BF)
        total = total_of(lambda index: wkv_in[index, 1], head)
        grad_value[:, head * HD : (head + 1) * HD] = jnp.transpose(total).astype(BF)

    each_peer(later, lambda peer: kv_copy(peer).wait_send())

    def sent_earlier(peer):
        q_copy(peer).wait_send()
        da_copy(peer).wait_send()
        dots_copy(peer).wait_send()

    each_peer(earlier, sent_earlier)
    loop(0, chip, lambda at: lse_copy(at).wait_send())
    norm_copy(core).wait_send()
    att_copy().wait_send()
    full_copy(core).wait_send()

    def sent_part(peer):
        glob_copy(peer).wait_send()
        grad_copy(peer).wait_send()

    each_part(sent_part)

    def sent_all(peer):
        wq_copy(peer).wait_send()
        wo_copy(peer).wait_send()
        wkv_copy(peer).wait_send()

    each_peer(anyone, sent_all)


def per_device(nctx, npb, *args):
    embed, w_query, w_key, w_value, w_out, ids, pad_embed, table, w_link, w_mix, w_lo, w_vocab = args
    rows, wide = embed.shape
    patches = rows // npb
    local_rows = patches * PATCH
    local_wide = w_link.shape[1]
    chips = nctx // 2
    block = wide // nctx
    vmem = pltpu.VMEM
    dma = pltpu.SemaphoreType.DMA
    scratch = [
        vmem((2, rows, wide), BF),
        vmem((2, 2, rows, HD), BF),
        vmem((2, nctx, rows, HD), BF),
        vmem((2, rows, HD), BF),
        vmem((nctx, rows, HD), BF),
        vmem((2, rows, HD), F32),
        vmem((2, rows, HD), F32),
        vmem((2, rows, HD), F32),
        vmem((2, rows, HD), BF),
        vmem((2, rows, HD), BF),
        vmem((2, rows, HD), F32),
        vmem((chips, 2, 8, rows), F32),
        vmem((npb, patches, wide), BF),
        vmem((npb, patches, wide), BF),
        vmem((local_rows, local_wide), F32),
        vmem((local_rows, 3 * local_wide), BF),
        vmem((local_wide // LHD, local_rows, local_rows), F32),
        vmem((local_rows, 3 * local_wide), BF),
        vmem((2, npb, patches, wide), BF),
        vmem((2, rows, HD), BF),
        vmem((nctx, rows, HD), BF),
        vmem((2, 8, rows), F32),
        vmem((nctx, 8, rows), F32),
        vmem((2, rows, HD), F32),
        vmem((2, rows, HD), F32),
        vmem((2, rows, HD), F32),
        vmem((nctx, HD, block), BF),
        vmem((nctx, HD, block), BF),
        vmem((nctx, 2, HD, block), BF),
        vmem((nctx, HD, block), BF),
        vmem((nctx, HD, block), BF),
        vmem((nctx, 2, HD, block), BF),
    ]
    scratch += [dma((nctx,))] * 14
    scratch += [dma((chips,))] * 2
    scratch += [dma((npb,))] * 4
    scratch += [dma] * 6
    whole = pl.BlockSpec(memory_space=pltpu.VMEM)
    tall = jax.ShapeDtypeStruct((block, 2 * HD), BF)
    return pl.pallas_call(
        functools.partial(step_kernel, (nctx, npb)),
        out_shape=(tall, tall, tall, jax.ShapeDtypeStruct((2 * HD, block), BF)),
        in_specs=[whole] * 12,
        out_specs=(whole,) * 4,
        scratch_shapes=scratch,
        compiler_params=pltpu.CompilerParams(
            collective_id=0, has_side_effects=True, vmem_limit_bytes=56 * 1024 * 1024
        ),
        name="step",
    )(
        embed, w_query, w_key, w_value, w_out, ids, pad_embed[None, :], table, w_link, w_mix,
        w_lo, w_vocab,
    )


def solution(mesh):
    in_specs = (
        P("ctx", None),
        P(None, "pb"),
        P(None, "pb"),
        P(None, "pb"),
        P("pb", None),
        P(("ctx", "pb"), None),
        P(),
        P(),
        P(),
        P(),
        P(),
        P(),
    )
    out_specs = (P("ctx", "pb"), P("ctx", "pb"), P("ctx", "pb"), P("pb", "ctx"))
    return jax.shard_map(
        functools.partial(per_device, mesh.shape["ctx"], mesh.shape["pb"]),
        mesh=mesh,
        in_specs=in_specs,
        out_specs=out_specs,
        check_vma=False,
    )
```

```python
import functools

import jax
import jax.numpy as jnp
from jax import lax
from jax.experimental import pallas as pl
from jax.experimental.pallas import tpu as pltpu
from jax.sharding import PartitionSpec as P

HD = 128
LHD = 64
PATCH = 8
EPSILON = 1e-06
MASKED = -1e30
MESH = pl.DeviceIdType.MESH
BF = jnp.bfloat16
F32 = jnp.float32


def nn(left, right):
    return lax.dot_general(left, right, (((1,), (0,)), ((), ())), preferred_element_type=F32)


def nt(left, right):
    return lax.dot_general(left, right, (((1,), (1,)), ((), ())), preferred_element_type=F32)


def tn(left, right):
    return lax.dot_general(left, right, (((0,), (0,)), ((), ())), preferred_element_type=F32)


def loop(low, high, body):
    def step(index, unused):
        body(index)
        return unused

    lax.fori_loop(low, high, step, 0)


def row_form(column, rows):
    return jnp.transpose(jnp.broadcast_to(column, (rows, HD)))[0:8]


def rms_inverse(values):
    return lax.rsqrt(jnp.mean(values * values, axis=1, keepdims=True) + EPSILON)


def rms_back(values, inverse, grad):
    width = values.shape[1]
    dots = jnp.sum(grad * values, axis=1, keepdims=True)
    return inverse * grad - values * (inverse * inverse * inverse * dots * (1.0 / width))


def step_kernel(
    sizes,
    embed_far,
    w_query_far,
    w_key_far,
    w_value_far,
    w_out_far,
    ids,
    pad_embed,
    table_far,
    w_link_far,
    w_mix_far,
    w_local_out_far,
    w_vocab_far,
    tall_sums,
    wide_sums,
    embed,
    w_query,
    w_key,
    w_value,
    w_out,
    table,
    w_link,
    w_mix,
    w_local_out,
    w_vocab,
    load_s,
    normed,
    normed_turned,
    kv_send,
    kv_all,
    q_send,
    q_all,
    run_max,
    run_sum,
    run_out,
    att_head,
    att_pair,
    lse_col,
    lse_all,
    glob_part,
    glob_in,
    hidden,
    mixed,
    weights,
    d_mixed,
    ids_wide,
    targets_all,
    grad_all,
    da_send,
    da_all,
    dq_acc,
    dk_acc,
    dv_acc,
    wqo_send,
    wkv_send,
    wqo_in,
    wkv_in,
    kv_s,
    kv_r,
    q_s,
    q_r,
    da_s,
    da_r,
    wqo_s,
    wqo_r,
    wkv_s,
    wkv_r,
    lse_s,
    lse_r,
    glob_s,
    glob_r,
    grad_s,
    grad_r,
    norm_s,
    norm_r,
    att_s,
    att_r,
    full_s,
    full_r,
):
    nctx, npb = sizes
    chips = nctx // 2
    rows, wide = embed.shape
    patches = rows // npb
    bytes_here = patches * PATCH
    scale = HD ** (-0.5)
    place = lax.axis_index("ctx")
    part = lax.axis_index("pb")
    chip = place // 2
    core = place % 2
    other = place + 1 - 2 * core

    def ctx_copy(src, dst, send, recv, peer):
        return pltpu.make_async_remote_copy(
            src_ref=src,
            dst_ref=dst,
            send_sem=send,
            recv_sem=recv,
            device_id=(peer, part),
            device_id_type=MESH,
        )

    def pb_copy(src, dst, send, recv, peer):
        return pltpu.make_async_remote_copy(
            src_ref=src,
            dst_ref=dst,
            send_sem=send,
            recv_sem=recv,
            device_id=(place, peer),
            device_id_type=MESH,
        )

    def each_peer(wanted, action):
        def one(step):
            peer = (place + nctx - step) % nctx

            @pl.when(wanted(peer // 2))
            def _():
                action(peer)

        loop(1, nctx, one)

    def each_part(action):
        loop(1, npb, lambda step: action((part + step) % npb))

    pairs_in = (
        (embed_far, embed),
        (w_key_far, w_key),
        (w_value_far, w_value),
        (w_query_far, w_query),
        (w_out_far, w_out),
        (table_far, table),
        (w_link_far, w_link),
        (w_mix_far, w_mix),
        (w_local_out_far, w_local_out),
        (w_vocab_far, w_vocab),
    )
    loads = [
        pltpu.make_async_copy(far, near, load_s.at[index])
        for index, (far, near) in enumerate(pairs_in)
    ]
    for load in loads:
        load.start()

    later = lambda at: at >= chip
    earlier = lambda at: at <= chip
    anyone = lambda at: at >= 0

    barrier = pltpu.get_barrier_semaphore()

    def greet_ctx(peer):
        pl.semaphore_signal(barrier, inc=1, device_id=(peer, part), device_id_type=MESH)

    def greet_part(peer):
        pl.semaphore_signal(barrier, inc=1, device_id=(place, peer), device_id_type=MESH)

    each_peer(anyone, greet_ctx)
    each_part(greet_part)

    tile_rows = min(32, rows)
    loads[0].wait()
    for low in range(0, rows, tile_rows):
        values = embed[low : low + tile_rows, :].astype(F32)
        normed[core, low : low + tile_rows, :] = (values * rms_inverse(values)).astype(BF)
    own_normed = normed[core]
    for slot, weight in ((0, w_key), (1, w_value)):
        loads[1 + slot].wait()
        product = nn(own_normed, weight[...]).astype(BF)
        kv_send[0, slot] = product[:, :HD]
        kv_send[1, slot] = product[:, HD:]
    pl.semaphore_wait(barrier, nctx + npb - 2)

    def kv_copy(peer):
        return ctx_copy(
            kv_send.at[peer % 2], kv_all.at[:, place], kv_s.at[peer], kv_r.at[place], peer
        )

    each_peer(later, lambda peer: kv_copy(peer).start())
    kv_all[:, place] = kv_send[core]
    loads[3].wait()
    product = nn(own_normed, w_query[...]).astype(BF)
    q_send[0] = product[:, :HD]
    q_send[1] = product[:, HD:]

    def q_copy(peer):
        return ctx_copy(q_send.at[peer % 2], q_all.at[place], q_s.at[peer], q_r.at[place], peer)

    q_copy(other).start()
    q_all[place] = q_send[core]

    def norm_copy(index):
        return ctx_copy(normed.at[index], normed.at[index], norm_s, norm_r, other)

    norm_copy(core).start()
    strictly_earlier = lambda at: at < chip
    each_peer(strictly_earlier, lambda peer: q_copy(peer).start())

    def kv_wait(peer):
        ctx_copy(kv_send.at[0], kv_all.at[:, peer], kv_s.at[peer], kv_r.at[peer], peer).wait_recv()

    def q_wait(peer):
        ctx_copy(q_send.at[0], q_all.at[peer], q_s.at[peer], q_r.at[peer], peer).wait_recv()

    first = 2 * chip
    pair_rows = 2 * rows

    def keys_of(at):
        return kv_all[0, pl.ds(2 * at, 2)].reshape(pair_rows, HD)

    def values_of(at):
        return kv_all[1, pl.ds(2 * at, 2)].reshape(pair_rows, HD)

    def diagonal(half, keys_down):
        shape = (rows, pair_rows)
        here = lax.broadcasted_iota(jnp.int32, shape, 0) + half * rows
        there = lax.broadcasted_iota(jnp.int32, shape, 1)
        return (there >= here) if keys_down else (there <= here)

    run_max[...] = jnp.full(run_max.shape, MASKED, F32)
    run_sum[...] = jnp.zeros(run_sum.shape, F32)
    run_out[...] = jnp.zeros(run_out.shape, F32)

    def attend(half, at, on_diagonal):
        scores = nt(q_all[first + half], keys_of(at)) * scale
        if on_diagonal:
            scores = jnp.where(diagonal(half, False), scores, MASKED)
        before = run_max[half, :, 0:1]
        highest = jnp.maximum(before, jnp.max(scores, axis=1, keepdims=True))
        exps = jnp.exp(scores - highest)
        factor = jnp.exp(before - highest)
        total = run_sum[half, :, 0:1] * factor + jnp.sum(exps, axis=1, keepdims=True)
        run_out[half] = run_out[half] * factor + nn(exps.astype(BF), values_of(at))
        run_max[half] = jnp.broadcast_to(highest, (rows, HD))
        run_sum[half] = jnp.broadcast_to(total, (rows, HD))

    kv_wait(other)
    q_wait(other)
    for half in (0, 1):
        attend(half, chip, True)
    norm_copy(1 - core).wait_recv()
    turn_tile = min(128, wide)

    def turn_columns(step):
        here = pl.ds(pl.multiple_of(step * turn_tile, turn_tile), turn_tile)
        block = normed[:, :, here].reshape(pair_rows, turn_tile)
        normed_turned[here, :] = jnp.transpose(block.astype(F32)).astype(BF)

    loop(0, wide // turn_tile, turn_columns)
    for load in loads[4:]:
        load.wait()

    def attend_earlier(step):
        at = chip - step
        kv_wait(2 * at)
        kv_wait(2 * at + 1)
        for half in (0, 1):
            attend(half, at, False)

    loop(1, chip + 1, attend_earlier)
    for half in (0, 1):
        att_head[half] = (run_out[half] / run_sum[half]).astype(BF)
        log_total = run_max[half] + jnp.log(run_sum[half])
        lse_col[half] = log_total
        lse_all[chip, half] = jnp.transpose(log_total)[0:8]

    def att_copy():
        return ctx_copy(att_head.at[1 - core], att_pair.at[core], att_s, att_r, other)

    att_copy().start()
    att_pair[core] = att_head[core]

    def lse_copy(at):
        return ctx_copy(
            lse_all.at[chip], lse_all.at[chip], lse_s.at[at], lse_r.at[chip], 2 * at + core
        )

    loop(0, chip, lambda at: lse_copy(at).start())
    ctx_copy(att_head.at[0], att_pair.at[1 - core], att_s, att_r, other).wait_recv()

    both_heads = jnp.concatenate([att_pair[0], att_pair[1]], axis=1)
    out_tile = min(512, wide)

    def out_columns(step):
        here = pl.ds(pl.multiple_of(step * out_tile, out_tile), out_tile)
        product = nn(both_heads, w_out[:, here]).astype(BF)
        glob_part[:, :, here] = product.reshape(npb, patches, out_tile)

    loop(0, wide // out_tile, out_columns)

    groups = 2
    share = patches // groups

    def glob_copy(group, peer):
        here = pl.ds(pl.multiple_of(group * share, share), share)
        return pb_copy(
            glob_part.at[peer, here],
            glob_in.at[part, here],
            glob_s.at[group, peer],
            glob_r.at[group, part],
            peer,
        )

    def glob_wait(group, peer):
        here = pl.ds(pl.multiple_of(group * share, share), share)
        pb_copy(
            glob_part.at[0, here],
            glob_in.at[peer, here],
            glob_s.at[group, peer],
            glob_r.at[group, peer],
            peer,
        ).wait_recv()

    for group in range(groups):
        each_part(lambda peer: glob_copy(group, peer).start())
    glob_in[part] = glob_part[part]

    count = share * PATCH
    byte_wide = wide // PATCH
    local_wide = w_link.shape[1]
    pairs = local_wide // (2 * LHD)
    symbols = lax.broadcasted_iota(jnp.int32, (count, table.shape[0]), 1)
    nothing = jnp.full((share, 1), -1, jnp.int32)
    ids_wide[:, 0:patches] = ids[...]
    for group in range(groups):
        columns = []
        for b in range(PATCH):
            line = jnp.broadcast_to(ids_wide[b : b + 1, :], (HD, HD))
            columns.append(jnp.transpose(line)[group * share : (group + 1) * share, 0:1])
        preceding = jnp.concatenate([nothing] + columns[:-1], axis=0)
        targets_all[group] = jnp.broadcast_to(jnp.concatenate(columns, axis=0), (count, HD))
        hidden[group] = nn((preceding == symbols).astype(BF), table[...]) + jnp.where(
            preceding < 0, pad_embed[...].astype(F32).reshape(1, local_wide), 0.0
        )
    row_index = lax.broadcasted_iota(jnp.int32, (count, count), 0)
    column_index = lax.broadcasted_iota(jnp.int32, (count, count), 1)
    same = jnp.logical_and(
        lax.rem(row_index, share) == lax.rem(column_index, share), column_index <= row_index
    )
    lane = lax.broadcasted_iota(jnp.int32, (count, 2 * LHD), 1)
    halves = (lane < LHD, lane >= LHD)

    def pair_of(block, pair):
        low = block * local_wide + pair * 2 * LHD
        return mixed[:, low : low + 2 * LHD]

    def kept(values, side):
        return jnp.where(halves[side], values, jnp.zeros_like(values))

    def grad_copy(group, peer):
        mine = grad_all.at[core, part, pl.ds(pl.multiple_of(group * share, share), share)]
        return pb_copy(mine, mine, grad_s.at[group, peer], grad_r.at[group, part], peer)

    def grad_wait(group, peer):
        theirs = grad_all.at[core, peer, pl.ds(pl.multiple_of(group * share, share), share)]
        pb_copy(theirs, theirs, grad_s.at[group, peer], grad_r.at[group, peer], peer).wait_recv()

    def local_model(group):
        here = pl.ds(pl.multiple_of(group * share, share), share)
        each_part(lambda peer: glob_wait(group, peer))
        glob = glob_in[0, here, :].astype(F32)
        for index in range(1, npb):
            glob = glob + glob_in[index, here, :].astype(F32)
        glob = glob.astype(BF)
        pieces = jnp.concatenate(
            [glob[:, b * byte_wide : (b + 1) * byte_wide] for b in range(PATCH)], axis=0
        )
        hidden_one = hidden[group] + nn(pieces, w_link[...])
        hidden[group] = hidden_one
        inverse_one = rms_inverse(hidden_one)
        mixed[...] = nn((hidden_one * inverse_one).astype(BF), w_mix[...]).astype(BF)
        local_att = []
        for pair in range(pairs):
            summed = None
            for side in (0, 1):
                scores = nt(kept(pair_of(0, pair), side), pair_of(1, pair)) * LHD ** (-0.5)
                scores = jnp.where(same, scores, MASKED)
                exps = jnp.exp(scores - jnp.max(scores, axis=1, keepdims=True))
                soft = exps / jnp.sum(exps, axis=1, keepdims=True)
                weights[2 * pair + side] = soft
                term = nn(soft.astype(BF), kept(pair_of(2, pair), side))
                summed = term if summed is None else summed + term
            local_att.append(summed.astype(BF))
        hidden_two = hidden[group] + nn(jnp.concatenate(local_att, axis=1), w_local_out[...])
        inverse_two = rms_inverse(hidden_two)
        logits = nn((hidden_two * inverse_two).astype(BF), w_vocab[...])
        exps = jnp.exp(logits - jnp.max(logits, axis=1, keepdims=True))
        soft = exps / jnp.sum(exps, axis=1, keepdims=True)
        d_logits = (
            soft - jnp.where(targets_all[group, :, 0:1] == symbols, 1.0, 0.0)
        ) * (1.0 / (rows * nctx * PATCH))
        d_normed_two = nt(d_logits.astype(BF), w_vocab[...]).astype(BF).astype(F32)
        d_hidden = rms_back(hidden_two, inverse_two, d_normed_two)
        d_local_att = nt(d_hidden.astype(BF), w_local_out[...]).astype(BF)
        for pair in range(pairs):
            low = pair * 2 * LHD
            d_att = d_local_att[:, low : low + 2 * LHD]
            d_query = d_key = d_value = None
            for side in (0, 1):
                soft = weights[2 * pair + side]
                d_side = kept(d_att, side)
                d_soft = nt(d_side, pair_of(2, pair)).astype(BF).astype(F32)
                dots = jnp.sum(d_soft * soft, axis=1, keepdims=True)
                d_scores = (soft * (d_soft - dots) * LHD ** (-0.5)).astype(BF)
                value_term = tn(soft.astype(BF), d_side)
                query_term = nn(d_scores, kept(pair_of(1, pair), side))
                key_term = tn(d_scores, kept(pair_of(0, pair), side))
                if side == 0:
                    d_query, d_key, d_value = query_term, key_term, value_term
                else:
                    d_query, d_key, d_value = (
                        d_query + query_term,
                        d_key + key_term,
                        d_value + value_term,
                    )
            for block, term in enumerate((d_query, d_key, d_value)):
                at = block * local_wide + low
                d_mixed[:, at : at + 2 * LHD] = term.astype(BF)
        d_normed_one = nt(d_mixed[...], w_mix[...]).astype(BF).astype(F32)
        hidden_one = hidden[group]
        d_hidden = d_hidden + rms_back(hidden_one, rms_inverse(hidden_one), d_normed_one)
        d_pieces = nt(d_hidden.astype(BF), w_link[...]).astype(BF)
        for b in range(PATCH):
            grad_all[core, part, here, b * byte_wide : (b + 1) * byte_wide] = d_pieces[
                b * share : (b + 1) * share
            ]
        each_part(lambda peer: grad_copy(group, peer).start())

    loop(0, groups, local_model)
    for group in range(groups):
        each_part(lambda peer: grad_wait(group, peer))

    def full_copy(index):
        return ctx_copy(grad_all.at[index], grad_all.at[index], full_s, full_r, other)

    full_copy(core).start()
    product = nt(grad_all[core].reshape(rows, wide), w_out[...]).astype(BF)
    for head in (0, 1):
        d_att = product[:, head * HD : (head + 1) * HD]
        da_send[head, 0:rows] = d_att
        dots = jnp.sum(d_att.astype(F32) * att_pair[head].astype(F32), axis=1, keepdims=True)
        exact = row_form(dots, rows)
        high = exact.astype(BF)
        low = (exact - high.astype(F32)).astype(BF)
        spare = jnp.concatenate([high[0:1], low[0:1]], axis=0)
        tail = [spare[:, at : at + HD] for at in range(0, rows, HD)]
        filler = jnp.zeros((16 - 2 * len(tail), HD), BF)
        da_send[head, rows : rows + 16] = jnp.concatenate(tail + [filler], axis=0)

    def da_copy(peer):
        return ctx_copy(
            da_send.at[peer % 2], da_all.at[place], da_s.at[peer], da_r.at[place], peer
        )

    def da_wait(peer):
        ctx_copy(da_send.at[0], da_all.at[peer], da_s.at[peer], da_r.at[peer], peer).wait_recv()

    def grads_of(device):
        return da_all[device, 0:rows]

    def dots_of(device):
        tail = da_all[device, rows : rows + 16].astype(F32)
        pieces = [tail[2 * at : 2 * at + 1] + tail[2 * at + 1 : 2 * at + 2] for at in range(rows // HD)]
        return jnp.concatenate(pieces, axis=1)

    each_peer(earlier, lambda peer: da_copy(peer).start())
    da_all[place] = da_send[core]
    da_wait(other)

    dq_acc[...] = jnp.zeros(dq_acc.shape, F32)

    def query_back(half, at, on_diagonal):
        scores = nt(q_all[first + half], keys_of(at)) * scale
        probs = jnp.exp(scores - lse_col[half, :, 0:1])
        if on_diagonal:
            probs = jnp.where(diagonal(half, False), probs, 0.0)
        d_probs = nt(grads_of(first + half), values_of(at))
        d_scores = (probs * (d_probs - run_sum[half, :, 0:1]) * scale).astype(BF)
        dq_acc[half] += nn(d_scores, keys_of(at))

    for half in (0, 1):
        dots = jnp.sum(
            grads_of(first + half).astype(F32) * att_head[half].astype(F32), axis=1, keepdims=True
        )
        run_sum[half] = jnp.broadcast_to(dots, (rows, HD))
    for half in (0, 1):
        query_back(half, chip, True)

    def query_earlier(step):
        for half in (0, 1):
            query_back(half, chip - step, False)

    loop(1, chip + 1, query_earlier)

    block_wide = wide // nctx
    term_rows = min(512, wide)
    owners = term_rows // block_wide

    def wqo_copy(peer):
        return ctx_copy(wqo_send.at[peer], wqo_in.at[place], wqo_s.at[peer], wqo_r.at[place], peer)

    def wkv_copy(peer):
        return ctx_copy(wkv_send.at[peer], wkv_in.at[place], wkv_s.at[peer], wkv_r.at[place], peer)

    full_copy(1 - core).wait_recv()
    dq_ready = dq_acc[...].reshape(pair_rows, HD).astype(BF)
    att_turned = jnp.transpose(att_head[...].reshape(pair_rows, HD).astype(F32)).astype(BF)

    def wqo_block(step):
        here = pl.ds(pl.multiple_of(step * term_rows, term_rows), term_rows)
        terms = nn(normed_turned[here, :], dq_ready).astype(BF)
        wqo_send[pl.ds(step * owners, owners), 0] = terms.reshape(owners, block_wide, HD)
        grads = grad_all[:, :, :, here].reshape(pair_rows, term_rows)
        terms = nn(att_turned, grads).astype(BF)
        for index in range(owners):
            wqo_send[step * owners + index, 1] = terms[:, index * block_wide : (index + 1) * block_wide]

    loop(0, wide // term_rows, wqo_block)
    each_peer(anyone, lambda peer: wqo_copy(peer).start())
    wqo_in[place] = wqo_send[place]

    dk_acc[...] = jnp.zeros(dk_acc.shape, F32)
    dv_acc[...] = jnp.zeros(dv_acc.shape, F32)

    def key_back(half, at, on_diagonal):
        queries = q_all[pl.ds(2 * at, 2)].reshape(pair_rows, HD)
        grads = jnp.concatenate([grads_of(2 * at), grads_of(2 * at + 1)], axis=0)
        log_total = jnp.concatenate([lse_all[at, 0, 0:1, :], lse_all[at, 1, 0:1, :]], axis=1)
        dots = jnp.concatenate([dots_of(2 * at), dots_of(2 * at + 1)], axis=1)
        scores = nt(kv_all[0, first + half], queries) * scale
        probs = jnp.exp(scores - log_total)
        if on_diagonal:
            probs = jnp.where(diagonal(half, True), probs, 0.0)
        d_probs = nt(kv_all[1, first + half], grads)
        d_scores = (probs * (d_probs - dots) * scale).astype(BF)
        dv_acc[half] += nn(probs.astype(BF), grads)
        dk_acc[half] += nn(d_scores, queries)

    for half in (0, 1):
        key_back(half, chip, True)

    def key_later(at):
        for peer in (2 * at, 2 * at + 1):
            q_wait(peer)
            da_wait(peer)
        ctx_copy(
            lse_all.at[at], lse_all.at[at], lse_s.at[at], lse_r.at[at], 2 * at + core
        ).wait_recv()
        for half in (0, 1):
            key_back(half, at, False)

    loop(chip + 1, chips, key_later)
    dkv_ready = jnp.concatenate(
        [dk_acc[...].reshape(pair_rows, HD), dv_acc[...].reshape(pair_rows, HD)], axis=1
    ).astype(BF)

    def wkv_block(step):
        here = pl.ds(pl.multiple_of(step * term_rows, term_rows), term_rows)
        terms = nn(normed_turned[here, :], dkv_ready).astype(BF)
        wkv_send[pl.ds(step * owners, owners)] = terms.reshape(owners, block_wide, 2 * HD)

    loop(0, wide // term_rows, wkv_block)
    each_peer(anyone, lambda peer: wkv_copy(peer).start())
    wkv_in[place] = wkv_send[place]

    def total_of(pick, head):
        total = pick(head).astype(F32)
        for index in range(1, chips):
            total = total + pick(2 * index + head).astype(F32)
        return total.astype(BF)

    def wqo_wait(peer):
        ctx_copy(wqo_send.at[0], wqo_in.at[peer], wqo_s.at[peer], wqo_r.at[peer], peer).wait_recv()

    def wkv_wait(peer):
        ctx_copy(wkv_send.at[0], wkv_in.at[peer], wkv_s.at[peer], wkv_r.at[peer], peer).wait_recv()

    each_peer(anyone, wqo_wait)
    for head in (0, 1):
        at = head * HD
        tall_sums[0, :, at : at + HD] = total_of(lambda index: wqo_in[index, 0], head)
        wide_sums[at : at + HD, :] = total_of(lambda index: wqo_in[index, 1], head)
    each_peer(anyone, wkv_wait)
    for head in (0, 1):
        at = head * HD
        total = total_of(lambda index: wkv_in[index], head)
        tall_sums[1, :, at : at + HD] = total[:, :HD]
        tall_sums[2, :, at : at + HD] = total[:, HD:]

    each_peer(later, lambda peer: kv_copy(peer).wait_send())

    def sent_earlier(peer):
        q_copy(peer).wait_send()
        da_copy(peer).wait_send()

    each_peer(earlier, sent_earlier)
    loop(0, chip, lambda at: lse_copy(at).wait_send())
    norm_copy(core).wait_send()
    att_copy().wait_send()
    full_copy(core).wait_send()

    for group in range(groups):

        def sent_part(peer):
            glob_copy(group, peer).wait_send()
            grad_copy(group, peer).wait_send()

        each_part(sent_part)

    def sent_all(peer):
        wqo_copy(peer).wait_send()
        wkv_copy(peer).wait_send()

    each_peer(anyone, sent_all)


def split_kernel(tall_sums, wide_sums, grad_query, grad_key, grad_value, grad_out):
    grad_query[...] = tall_sums[0]
    grad_key[...] = tall_sums[1]
    grad_value[...] = tall_sums[2]
    grad_out[...] = wide_sums[...]


def per_device(nctx, npb, *args):
    embed, w_query, w_key, w_value, w_out, ids, pad_embed, table, w_link, w_mix, w_lo, w_vocab = args
    rows, wide = embed.shape
    patches = rows // npb
    groups = 2
    local_rows = patches // groups * PATCH
    local_wide = w_link.shape[1]
    chips = nctx // 2
    block = wide // nctx
    vmem = pltpu.VMEM
    dma = pltpu.SemaphoreType.DMA
    near = [embed, w_query, w_key, w_value, w_out, table, w_link, w_mix, w_lo, w_vocab]
    scratch = [vmem(array.shape, BF) for array in near]
    scratch += [
        dma((len(near),)),
        vmem((2, rows, wide), BF),
        vmem((wide, 2 * rows), BF),
        vmem((2, 2, rows, HD), BF),
        vmem((2, nctx, rows, HD), BF),
        vmem((2, rows, HD), BF),
        vmem((nctx, rows, HD), BF),
        vmem((2, rows, HD), F32),
        vmem((2, rows, HD), F32),
        vmem((2, rows, HD), F32),
        vmem((2, rows, HD), BF),
        vmem((2, rows, HD), BF),
        vmem((2, rows, HD), F32),
        vmem((chips, 2, 8, rows), F32),
        vmem((npb, patches, wide), BF),
        vmem((npb, patches, wide), BF),
        vmem((groups, local_rows, local_wide), F32),
        vmem((local_rows, 3 * local_wide), BF),
        vmem((local_wide // LHD, local_rows, local_rows), F32),
        vmem((local_rows, 3 * local_wide), BF),
        vmem((PATCH, HD), jnp.int32),
        vmem((groups, local_rows, HD), jnp.int32),
        vmem((2, npb, patches, wide), BF),
        vmem((2, rows + 16, HD), BF),
        vmem((nctx, rows + 16, HD), BF),
        vmem((2, rows, HD), F32),
        vmem((2, rows, HD), F32),
        vmem((2, rows, HD), F32),
        vmem((nctx, 2, HD, block), BF),
        vmem((nctx, block, 2 * HD), BF),
        vmem((nctx, 2, HD, block), BF),
        vmem((nctx, block, 2 * HD), BF),
    ]
    scratch += [dma((nctx,))] * 10
    scratch += [dma((chips,))] * 2
    scratch += [dma((groups, npb))] * 4
    scratch += [dma] * 6
    whole = pl.BlockSpec(memory_space=pltpu.VMEM)
    far = pl.BlockSpec(memory_space=pl.ANY)
    tall = jax.ShapeDtypeStruct((block, 2 * HD), BF)
    sums = pl.pallas_call(
        functools.partial(step_kernel, (nctx, npb)),
        out_shape=(
            jax.ShapeDtypeStruct((3, block, 2 * HD), BF),
            jax.ShapeDtypeStruct((2 * HD, block), BF),
        ),
        in_specs=[far] * 5 + [whole] * 2 + [far] * 5,
        out_specs=(whole,) * 2,
        scratch_shapes=scratch,
        compiler_params=pltpu.CompilerParams(
            collective_id=0, has_side_effects=True, vmem_limit_bytes=56 * 1024 * 1024
        ),
        name="step",
    )(
        embed, w_query, w_key, w_value, w_out, ids.T, pad_embed, table, w_link, w_mix,
        w_lo, w_vocab,
    )
    return pl.pallas_call(
        split_kernel,
        out_shape=(tall, tall, tall, jax.ShapeDtypeStruct((2 * HD, block), BF)),
        in_specs=[whole] * 2,
        out_specs=(whole,) * 4,
        name="split",
    )(*sums)


def solution(mesh):
    in_specs = (
        P("ctx", None),
        P(None, "pb"),
        P(None, "pb"),
        P(None, "pb"),
        P("pb", None),
        P(("ctx", "pb"), None),
        P(),
        P(),
        P(),
        P(),
        P(),
        P(),
    )
    out_specs = (P("ctx", "pb"), P("ctx", "pb"), P("ctx", "pb"), P("pb", "ctx"))
    return jax.shard_map(
        functools.partial(per_device, mesh.shape["ctx"], mesh.shape["pb"]),
        mesh=mesh,
        in_specs=in_specs,
        out_specs=out_specs,
        check_vma=False,
    )
```

```python
import functools

import jax
import jax.numpy as jnp
from jax import lax
from jax.experimental import pallas as pl
from jax.experimental.pallas import tpu as pltpu
from jax.sharding import PartitionSpec as P

HD = 128
LHD = 64
PATCH = 8
EPSILON = 1e-06
MASKED = -1e30
MESH = pl.DeviceIdType.MESH
BF = jnp.bfloat16
F32 = jnp.float32


def nn(left, right):
    return lax.dot_general(left, right, (((1,), (0,)), ((), ())), preferred_element_type=F32)


def nt(left, right):
    return lax.dot_general(left, right, (((1,), (1,)), ((), ())), preferred_element_type=F32)


def tn(left, right):
    return lax.dot_general(left, right, (((0,), (0,)), ((), ())), preferred_element_type=F32)


def loop(low, high, body):
    def step(index, unused):
        body(index)
        return unused

    lax.fori_loop(low, high, step, 0)


def row_form(column, rows):
    return jnp.transpose(jnp.broadcast_to(column, (rows, HD)))[0:8]


def rms_inverse(values):
    return lax.rsqrt(jnp.mean(values * values, axis=1, keepdims=True) + EPSILON)


def rms_back(values, inverse, grad):
    width = values.shape[1]
    dots = jnp.sum(grad * values, axis=1, keepdims=True)
    return inverse * grad - values * (inverse * inverse * inverse * dots * (1.0 / width))


def step_kernel(
    sizes,
    embed_far,
    w_query_far,
    w_key_far,
    w_value_far,
    w_out_far,
    ids,
    pad_embed,
    table_far,
    w_link_far,
    w_mix_far,
    w_local_out_far,
    w_vocab_far,
    tall_sums,
    wide_sums,
    embed,
    w_query,
    w_key,
    w_value,
    w_out,
    table,
    w_link,
    w_mix,
    w_local_out,
    w_vocab,
    load_s,
    normed,
    normed_turned,
    kv_send,
    kv_all,
    q_send,
    q_all,
    run_max,
    run_sum,
    run_out,
    att_head,
    att_pair,
    lse_col,
    lse_all,
    glob_part,
    glob_in,
    hidden,
    mixed,
    weights,
    d_weights,
    d_mixed,
    ids_wide,
    targets_all,
    grad_all,
    da_send,
    da_all,
    dq_acc,
    dk_acc,
    dv_acc,
    wo_send,
    wq_send,
    wkv_send,
    wo_in,
    wq_in,
    wkv_in,
    kv_s,
    kv_r,
    q_s,
    q_r,
    wo_s,
    wo_r,
    wq_s,
    wq_r,
    wkv_s,
    wkv_r,
    lse_s,
    lse_r,
    glob_s,
    glob_r,
    grad_s,
    grad_r,
    norm_s,
    norm_r,
    att_s,
    att_r,
    full_s,
    full_r,
    da_s,
    da_r,
    kv_forward_s,
    da_forward_s,
):
    nctx, npb = sizes
    chips = nctx // 2
    rows, wide = embed.shape
    patches = rows // npb
    bytes_here = patches * PATCH
    scale = HD ** (-0.5)
    place = lax.axis_index("ctx")
    part = lax.axis_index("pb")
    chip = place // 2
    core = place % 2
    other = place + 1 - 2 * core

    def ctx_copy(src, dst, send, recv, peer):
        return pltpu.make_async_remote_copy(
            src_ref=src,
            dst_ref=dst,
            send_sem=send,
            recv_sem=recv,
            device_id=(peer, part),
            device_id_type=MESH,
        )

    def pb_copy(src, dst, send, recv, peer):
        return pltpu.make_async_remote_copy(
            src_ref=src,
            dst_ref=dst,
            send_sem=send,
            recv_sem=recv,
            device_id=(place, peer),
            device_id_type=MESH,
        )

    def each_peer(wanted, action):
        def one(step):
            peer = (place + nctx - step) % nctx

            @pl.when(wanted(peer // 2))
            def _():
                action(peer)

        loop(1, nctx, one)

    def each_part(action):
        loop(1, npb, lambda step: action((part + step) % npb))

    pairs_in = (
        (embed_far, embed),
        (w_key_far, w_key),
        (w_value_far, w_value),
        (w_query_far, w_query),
        (w_out_far, w_out),
        (table_far, table),
        (w_link_far, w_link),
        (w_mix_far, w_mix),
        (w_local_out_far, w_local_out),
        (w_vocab_far, w_vocab),
    )
    half_rows = rows // 2
    first_load = pltpu.make_async_copy(
        embed_far.at[0:half_rows], embed.at[0:half_rows], load_s.at[len(pairs_in)]
    )
    pairs_in = ((embed_far.at[half_rows:rows], embed.at[half_rows:rows]),) + pairs_in[1:]
    loads = [
        pltpu.make_async_copy(far, near, load_s.at[index])
        for index, (far, near) in enumerate(pairs_in)
    ]
    first_load.start()
    for load in loads:
        load.start()

    later = lambda at: at >= chip
    earlier = lambda at: at <= chip
    anyone = lambda at: at >= 0

    def crossing(at, rows_away):
        return jnp.logical_and(at // 2 - chip // 2 == rows_away, at % 2 != chip % 2)

    later_direct = lambda at: jnp.logical_and(later(at), jnp.logical_not(crossing(at, 2)))
    earlier_direct = lambda at: jnp.logical_and(earlier(at), jnp.logical_not(crossing(at, -2)))
    neighbour = 2 * (chip + 1 - 2 * (chip % 2)) + core

    barrier = pltpu.get_barrier_semaphore()

    def greet_ctx(peer):
        pl.semaphore_signal(barrier, inc=1, device_id=(peer, part), device_id_type=MESH)

    def greet_part(peer):
        pl.semaphore_signal(barrier, inc=1, device_id=(place, peer), device_id_type=MESH)

    each_peer(anyone, greet_ctx)
    each_part(greet_part)

    tile_rows = min(32, rows)
    first_load.wait()
    for low in range(0, rows, tile_rows):
        if low == half_rows:
            loads[0].wait()
        values = embed[low : low + tile_rows, :].astype(F32)
        normed[core, low : low + tile_rows, :] = (values * rms_inverse(values)).astype(BF)
    own_normed = normed[core]
    for slot, weight in ((0, w_key), (1, w_value)):
        loads[1 + slot].wait()
        product = nn(own_normed, weight[...]).astype(BF)
        kv_send[0, slot] = product[:, :HD]
        kv_send[1, slot] = product[:, HD:]
    pl.semaphore_wait(barrier, nctx + npb - 2)

    def kv_copy(peer):
        return ctx_copy(
            kv_send.at[peer % 2], kv_all.at[:, place], kv_s.at[peer], kv_r.at[place], peer
        )

    each_peer(later_direct, lambda peer: kv_copy(peer).start())
    kv_all[:, place] = kv_send[core]
    loads[3].wait()
    product = nn(own_normed, w_query[...]).astype(BF)
    q_send[0] = product[:, :HD]
    q_send[1] = product[:, HD:]

    def q_copy(peer):
        return ctx_copy(q_send.at[peer % 2], q_all.at[place], q_s.at[peer], q_r.at[place], peer)

    q_copy(other).start()
    q_all[place] = q_send[core]

    def norm_copy(index):
        return ctx_copy(normed.at[index], normed.at[index], norm_s, norm_r, other)

    norm_copy(core).start()
    strictly_earlier = lambda at: at < chip
    each_peer(strictly_earlier, lambda peer: q_copy(peer).start())

    def kv_wait(peer):
        ctx_copy(kv_send.at[0], kv_all.at[:, peer], kv_s.at[peer], kv_r.at[peer], peer).wait_recv()

    def q_wait(peer):
        ctx_copy(q_send.at[0], q_all.at[peer], q_s.at[peer], q_r.at[peer], peer).wait_recv()

    first = 2 * chip
    pair_rows = 2 * rows

    def keys_of(at):
        return kv_all[0, pl.ds(2 * at, 2)].reshape(pair_rows, HD)

    def values_of(at):
        return kv_all[1, pl.ds(2 * at, 2)].reshape(pair_rows, HD)

    def diagonal(half, keys_down):
        shape = (rows, pair_rows)
        here = lax.broadcasted_iota(jnp.int32, shape, 0) + half * rows
        there = lax.broadcasted_iota(jnp.int32, shape, 1)
        return (there >= here) if keys_down else (there <= here)

    run_max[...] = jnp.full(run_max.shape, MASKED, F32)
    run_sum[...] = jnp.zeros(run_sum.shape, F32)
    run_out[...] = jnp.zeros(run_out.shape, F32)

    def attend(half, at, on_diagonal):
        scores = nt(q_all[first + half], keys_of(at)) * scale
        if on_diagonal:
            scores = jnp.where(diagonal(half, False), scores, MASKED)
        before = run_max[half, :, 0:1]
        highest = jnp.maximum(before, jnp.max(scores, axis=1, keepdims=True))
        exps = jnp.exp(scores - highest)
        factor = jnp.exp(before - highest)
        total = run_sum[half, :, 0:1] * factor + jnp.sum(exps, axis=1, keepdims=True)
        run_out[half] = run_out[half] * factor + nn(exps.astype(BF), values_of(at))
        run_max[half] = jnp.broadcast_to(highest, (rows, HD))
        run_sum[half] = jnp.broadcast_to(total, (rows, HD))

    kv_wait(other)
    q_wait(other)
    for half in (0, 1):
        attend(half, chip, True)
    norm_copy(1 - core).wait_recv()
    turn_tile = min(128, wide)

    def turn_columns(step):
        here = pl.ds(pl.multiple_of(step * turn_tile, turn_tile), turn_tile)
        block = normed[:, :, here].reshape(pair_rows, turn_tile)
        normed_turned[here, :] = jnp.transpose(block.astype(F32)).astype(BF)

    loop(0, wide // turn_tile, turn_columns)
    for load in loads[4:]:
        load.wait()

    def kv_forward(side):
        source = 2 * (chip - 4) + side
        block = kv_all.at[:, source]
        return ctx_copy(block, block, kv_forward_s.at[side], kv_r.at[source], neighbour)

    @pl.when(chip >= 4)
    def _():
        for side in (0, 1):
            kv_wait(2 * (chip - 4) + side)
            kv_forward(side).start()
        for half in (0, 1):
            attend(half, chip - 4, False)

    def attend_earlier(step):
        at = chip - step

        @pl.when(step != 4)
        def _():
            kv_wait(2 * at)
            kv_wait(2 * at + 1)
            for half in (0, 1):
                attend(half, at, False)

    loop(1, chip + 1, attend_earlier)
    for half in (0, 1):
        att_head[half] = (run_out[half] / run_sum[half]).astype(BF)
        log_total = run_max[half] + jnp.log(run_sum[half])
        lse_col[half] = log_total
        lse_all[chip, half] = jnp.transpose(log_total)[0:8]

    def att_copy():
        return ctx_copy(att_head.at[1 - core], att_pair.at[core], att_s, att_r, other)

    att_copy().start()
    att_pair[core] = att_head[core]

    def lse_copy(at):
        return ctx_copy(
            lse_all.at[chip], lse_all.at[chip], lse_s.at[at], lse_r.at[chip], 2 * at + core
        )

    loop(0, chip, lambda at: lse_copy(at).start())
    ctx_copy(att_head.at[0], att_pair.at[1 - core], att_s, att_r, other).wait_recv()

    both_heads = jnp.concatenate([att_pair[0], att_pair[1]], axis=1)
    out_tile = min(512, wide)

    def out_columns(step):
        here = pl.ds(pl.multiple_of(step * out_tile, out_tile), out_tile)
        product = nn(both_heads, w_out[:, here]).astype(BF)
        glob_part[:, :, here] = product.reshape(npb, patches, out_tile)

    loop(0, wide // out_tile, out_columns)

    groups = 2
    share = patches // groups

    def glob_copy(group, peer):
        here = pl.ds(pl.multiple_of(group * share, share), share)
        return pb_copy(
            glob_part.at[peer, here],
            glob_in.at[part, here],
            glob_s.at[group, peer],
            glob_r.at[group, part],
            peer,
        )

    def glob_wait(group, peer):
        here = pl.ds(pl.multiple_of(group * share, share), share)
        pb_copy(
            glob_part.at[0, here],
            glob_in.at[peer, here],
            glob_s.at[group, peer],
            glob_r.at[group, peer],
            peer,
        ).wait_recv()

    for group in range(groups):
        each_part(lambda peer: glob_copy(group, peer).start())
    glob_in[part] = glob_part[part]

    count = share * PATCH
    byte_wide = wide // PATCH
    local_wide = w_link.shape[1]
    pairs = local_wide // (2 * LHD)
    symbols = lax.broadcasted_iota(jnp.int32, (count, table.shape[0]), 1)
    nothing = jnp.full((share, 1), -1, jnp.int32)
    ids_wide[:, 0:patches] = ids[...]
    for group in range(groups):
        columns = []
        for b in range(PATCH):
            line = jnp.broadcast_to(ids_wide[b : b + 1, :], (HD, HD))
            columns.append(jnp.transpose(line)[group * share : (group + 1) * share, 0:1])
        preceding = jnp.concatenate([nothing] + columns[:-1], axis=0)
        targets_all[group] = jnp.broadcast_to(jnp.concatenate(columns, axis=0), (count, HD))
        hidden[group] = nn((preceding == symbols).astype(BF), table[...]) + jnp.where(
            preceding < 0, pad_embed[...].astype(F32).reshape(1, local_wide), 0.0
        )
    row_index = lax.broadcasted_iota(jnp.int32, (count, count), 0)
    column_index = lax.broadcasted_iota(jnp.int32, (count, count), 1)
    same = jnp.logical_and(
        lax.rem(row_index, share) == lax.rem(column_index, share), column_index <= row_index
    )
    lane = lax.broadcasted_iota(jnp.int32, (count, 2 * LHD), 1)
    halves = (lane < LHD, lane >= LHD)

    def pair_of(block, pair):
        low = block * local_wide + pair * 2 * LHD
        return mixed[:, low : low + 2 * LHD]

    def kept(values, side):
        return jnp.where(halves[side], values, jnp.zeros_like(values))

    def grad_copy(group, peer):
        mine = grad_all.at[core, part, pl.ds(pl.multiple_of(group * share, share), share)]
        return pb_copy(mine, mine, grad_s.at[group, peer], grad_r.at[group, part], peer)

    def grad_wait(group, peer):
        theirs = grad_all.at[core, peer, pl.ds(pl.multiple_of(group * share, share), share)]
        pb_copy(theirs, theirs, grad_s.at[group, peer], grad_r.at[group, peer], peer).wait_recv()

    def local_model(group):
        here = pl.ds(pl.multiple_of(group * share, share), share)
        each_part(lambda peer: glob_wait(group, peer))
        glob = glob_in[0, here, :].astype(F32)
        for index in range(1, npb):
            glob = glob + glob_in[index, here, :].astype(F32)
        glob = glob.astype(BF)
        pieces = jnp.concatenate(
            [glob[:, b * byte_wide : (b + 1) * byte_wide] for b in range(PATCH)], axis=0
        )
        hidden_one = hidden[group] + nn(pieces, w_link[...])
        hidden[group] = hidden_one
        inverse_one = rms_inverse(hidden_one)
        mixed[...] = nn((hidden_one * inverse_one).astype(BF), w_mix[...]).astype(BF)
        heads = 2 * pairs
        for head in range(heads):
            query = kept(pair_of(0, head // 2), head % 2)
            weights[head] = nt(query, pair_of(1, head // 2))
        scores = jnp.where(same[None], weights[...] * LHD ** (-0.5), MASKED)
        exps = jnp.exp(scores - jnp.max(scores, axis=2, keepdims=True))
        weights[...] = exps / jnp.sum(exps, axis=2, keepdims=True)
        local_att = []
        for pair in range(pairs):
            terms = [
                nn(weights[2 * pair + side].astype(BF), kept(pair_of(2, pair), side))
                for side in (0, 1)
            ]
            local_att.append((terms[0] + terms[1]).astype(BF))
        hidden_two = hidden[group] + nn(jnp.concatenate(local_att, axis=1), w_local_out[...])
        inverse_two = rms_inverse(hidden_two)
        logits = nn((hidden_two * inverse_two).astype(BF), w_vocab[...])
        exps = jnp.exp(logits - jnp.max(logits, axis=1, keepdims=True))
        soft = exps / jnp.sum(exps, axis=1, keepdims=True)
        d_logits = (
            soft - jnp.where(targets_all[group, :, 0:1] == symbols, 1.0, 0.0)
        ) * (1.0 / (rows * nctx * PATCH))
        d_normed_two = nt(d_logits.astype(BF), w_vocab[...]).astype(BF).astype(F32)
        d_hidden = rms_back(hidden_two, inverse_two, d_normed_two)
        d_local_att = nt(d_hidden.astype(BF), w_local_out[...]).astype(BF)
        d_heads = [
            kept(d_local_att[:, pair * 2 * LHD : (pair + 1) * 2 * LHD], side)
            for pair in range(pairs)
            for side in (0, 1)
        ]
        for head in range(heads):
            d_weights[head] = nt(d_heads[head], pair_of(2, head // 2))
        d_soft = d_weights[...].astype(BF).astype(F32)
        soft = weights[...]
        dots = jnp.sum(d_soft * soft, axis=2, keepdims=True)
        d_weights[...] = soft * (d_soft - dots) * LHD ** (-0.5)
        for pair in range(pairs):
            terms = [[], [], []]
            for side in (0, 1):
                head = 2 * pair + side
                d_scores = d_weights[head].astype(BF)
                terms[0].append(nn(d_scores, kept(pair_of(1, pair), side)))
                terms[1].append(tn(d_scores, kept(pair_of(0, pair), side)))
                terms[2].append(tn(weights[head].astype(BF), d_heads[head]))
            for block in range(3):
                at = block * local_wide + pair * 2 * LHD
                d_mixed[:, at : at + 2 * LHD] = (terms[block][0] + terms[block][1]).astype(BF)
        d_normed_one = nt(d_mixed[...], w_mix[...]).astype(BF).astype(F32)
        hidden_one = hidden[group]
        d_hidden = d_hidden + rms_back(hidden_one, rms_inverse(hidden_one), d_normed_one)
        d_pieces = nt(d_hidden.astype(BF), w_link[...]).astype(BF)
        for b in range(PATCH):
            grad_all[core, part, here, b * byte_wide : (b + 1) * byte_wide] = d_pieces[
                b * share : (b + 1) * share
            ]
        each_part(lambda peer: grad_copy(group, peer).start())

    loop(0, groups, local_model)
    def full_copy(group, index):
        here = pl.ds(group * share, share)
        block = grad_all.at[index, :, here]
        return ctx_copy(block, block, full_s.at[group], full_r.at[group], other)

    last = groups - 1

    def da_parts(group, whole):
        return whole.at[0 : npb + 1 if group == last else npb, group * share : (group + 1) * share]

    def da_copy(group, peer):
        return ctx_copy(
            da_parts(group, da_send.at[peer % 2]),
            da_parts(group, da_all.at[place]),
            da_s.at[group, peer],
            da_r.at[group, place],
            peer,
        )

    def da_wait_part(group, peer):
        ctx_copy(
            da_parts(group, da_send.at[0]),
            da_parts(group, da_all.at[peer]),
            da_s.at[group, peer],
            da_r.at[group, peer],
            peer,
        ).wait_recv()

    def da_wait(peer):
        for group in range(groups):
            da_wait_part(group, peer)

    def da_forward(group, side):
        source = 2 * (chip + 4) + side
        block = da_parts(group, da_all.at[source])
        return ctx_copy(
            block, block, da_forward_s.at[group, side], da_r.at[group, source], neighbour
        )

    for group in range(groups):
        each_part(lambda peer: grad_wait(group, peer))
        full_copy(group, core).start()
        here = slice(group * share, (group + 1) * share)
        grads = grad_all[core, :, here, :].reshape(npb * share, wide)
        product = nt(grads, w_out[...]).astype(BF)
        for head in (0, 1):
            d_att = product[:, head * HD : (head + 1) * HD]
            da_send[head, 0:npb, here, :] = d_att.reshape(npb, share, HD)
        if group == last:
            for head in (0, 1):
                d_att = da_send[head, 0:npb].reshape(rows, HD).astype(F32)
                dots = jnp.sum(d_att * att_pair[head].astype(F32), axis=1, keepdims=True)
                exact = row_form(dots, rows)
                high = exact.astype(BF)
                low = (exact - high.astype(F32)).astype(BF)
                spare = jnp.concatenate([high[0:1], low[0:1]], axis=0)
                tail = [spare[:, at : at + HD] for at in range(0, rows, HD)]
                filler = jnp.zeros((share - 2 * len(tail), HD), BF)
                da_send[head, npb, here, :] = jnp.concatenate(tail + [filler], axis=0)
        each_peer(earlier_direct, lambda peer: da_copy(group, peer).start())

    def grads_of(device):
        return da_all[device, 0:npb].reshape(rows, HD)

    def dots_of(device):
        tail = da_all[device, npb, last * share : (last + 1) * share].astype(F32)
        pieces = [
            tail[2 * at : 2 * at + 1] + tail[2 * at + 1 : 2 * at + 2] for at in range(rows // HD)
        ]
        return jnp.concatenate(pieces, axis=1)

    da_all[place] = da_send[core]

    block_wide = wide // nctx
    term_rows = min(512, wide)
    owners = term_rows // block_wide

    def wo_copy(peer):
        return ctx_copy(wo_send.at[peer], wo_in.at[place], wo_s.at[peer], wo_r.at[place], peer)

    def wq_copy(peer):
        return ctx_copy(wq_send.at[peer], wq_in.at[place], wq_s.at[peer], wq_r.at[place], peer)

    def wkv_copy(peer):
        return ctx_copy(wkv_send.at[peer], wkv_in.at[place], wkv_s.at[peer], wkv_r.at[place], peer)

    for group in range(groups):
        full_copy(group, 1 - core).wait_recv()
    att_turned = jnp.transpose(att_head[...].reshape(pair_rows, HD).astype(F32)).astype(BF)

    def wo_block(step):
        here = pl.ds(pl.multiple_of(step * term_rows, term_rows), term_rows)
        grads = grad_all[:, :, :, here].reshape(pair_rows, term_rows)
        terms = nn(att_turned, grads).astype(BF)
        for index in range(owners):
            wo_send[step * owners + index] = terms[:, index * block_wide : (index + 1) * block_wide]

    loop(0, wide // term_rows, wo_block)
    each_peer(anyone, lambda peer: wo_copy(peer).start())
    wo_in[place] = wo_send[place]
    da_wait(other)

    dq_acc[...] = jnp.zeros(dq_acc.shape, F32)

    def query_back(half, at, on_diagonal):
        scores = nt(q_all[first + half], keys_of(at)) * scale
        probs = jnp.exp(scores - lse_col[half, :, 0:1])
        if on_diagonal:
            probs = jnp.where(diagonal(half, False), probs, 0.0)
        d_probs = nt(grads_of(first + half), values_of(at))
        d_scores = (probs * (d_probs - run_sum[half, :, 0:1]) * scale).astype(BF)
        dq_acc[half] += nn(d_scores, keys_of(at))

    for half in (0, 1):
        dots = jnp.sum(
            grads_of(first + half).astype(F32) * att_head[half].astype(F32), axis=1, keepdims=True
        )
        run_sum[half] = jnp.broadcast_to(dots, (rows, HD))
    for half in (0, 1):
        query_back(half, chip, True)

    def query_earlier(step):
        for half in (0, 1):
            query_back(half, chip - step, False)

    loop(1, chip + 1, query_earlier)

    dq_ready = dq_acc[...].reshape(pair_rows, HD).astype(BF)

    def wq_block(step):
        here = pl.ds(pl.multiple_of(step * term_rows, term_rows), term_rows)
        terms = nn(normed_turned[here, :], dq_ready).astype(BF)
        wq_send[pl.ds(step * owners, owners)] = terms.reshape(owners, block_wide, HD)

    loop(0, wide // term_rows, wq_block)
    each_peer(anyone, lambda peer: wq_copy(peer).start())
    wq_in[place] = wq_send[place]

    dk_acc[...] = jnp.zeros(dk_acc.shape, F32)
    dv_acc[...] = jnp.zeros(dv_acc.shape, F32)

    def key_back(half, at, on_diagonal):
        queries = q_all[pl.ds(2 * at, 2)].reshape(pair_rows, HD)
        grads = da_all[pl.ds(2 * at, 2), 0:npb].reshape(pair_rows, HD)
        log_total = jnp.concatenate([lse_all[at, 0, 0:1, :], lse_all[at, 1, 0:1, :]], axis=1)
        dots = jnp.concatenate([dots_of(2 * at), dots_of(2 * at + 1)], axis=1)
        scores = nt(kv_all[0, first + half], queries) * scale
        probs = jnp.exp(scores - log_total)
        if on_diagonal:
            probs = jnp.where(diagonal(half, True), probs, 0.0)
        d_probs = nt(kv_all[1, first + half], grads)
        d_scores = (probs * (d_probs - dots) * scale).astype(BF)
        dv_acc[half] += nn(probs.astype(BF), grads)
        dk_acc[half] += nn(d_scores, queries)

    for half in (0, 1):
        key_back(half, chip, True)

    def rest_wait(at):
        q_wait(2 * at)
        q_wait(2 * at + 1)
        ctx_copy(
            lse_all.at[at], lse_all.at[at], lse_s.at[at], lse_r.at[at], 2 * at + core
        ).wait_recv()

    @pl.when(chip < chips - 4)
    def _():
        for group in range(groups):
            for side in (0, 1):
                da_wait_part(group, 2 * (chip + 4) + side)
                da_forward(group, side).start()
        rest_wait(chip + 4)
        for half in (0, 1):
            key_back(half, chip + 4, False)

    def key_later(at):
        @pl.when(at != chip + 4)
        def _():
            da_wait(2 * at)
            da_wait(2 * at + 1)
            rest_wait(at)
            for half in (0, 1):
                key_back(half, at, False)

    loop(chip + 1, chips, key_later)
    dkv_ready = jnp.concatenate(
        [dk_acc[...].reshape(pair_rows, HD), dv_acc[...].reshape(pair_rows, HD)], axis=1
    ).astype(BF)

    def wkv_block(step):
        here = pl.ds(pl.multiple_of(step * term_rows, term_rows), term_rows)
        terms = nn(normed_turned[here, :], dkv_ready).astype(BF)
        wkv_send[pl.ds(step * owners, owners)] = terms.reshape(owners, block_wide, 2 * HD)

    loop(0, wide // term_rows, wkv_block)
    each_peer(anyone, lambda peer: wkv_copy(peer).start())
    wkv_in[place] = wkv_send[place]

    def total_of(pick, head):
        total = pick(head).astype(F32)
        for index in range(1, chips):
            total = total + pick(2 * index + head).astype(F32)
        return total.astype(BF)

    def wo_wait(peer):
        ctx_copy(wo_send.at[0], wo_in.at[peer], wo_s.at[peer], wo_r.at[peer], peer).wait_recv()

    def wq_wait(peer):
        ctx_copy(wq_send.at[0], wq_in.at[peer], wq_s.at[peer], wq_r.at[peer], peer).wait_recv()

    def wkv_wait(peer):
        ctx_copy(wkv_send.at[0], wkv_in.at[peer], wkv_s.at[peer], wkv_r.at[peer], peer).wait_recv()

    each_peer(anyone, wo_wait)
    for head in (0, 1):
        wide_sums[head * HD : (head + 1) * HD, :] = total_of(lambda index: wo_in[index], head)
    each_peer(anyone, wq_wait)
    for head in (0, 1):
        at = head * HD
        tall_sums[0, :, at : at + HD] = total_of(lambda index: wq_in[index], head)
    each_peer(anyone, wkv_wait)
    for head in (0, 1):
        at = head * HD
        total = total_of(lambda index: wkv_in[index], head)
        tall_sums[1, :, at : at + HD] = total[:, :HD]
        tall_sums[2, :, at : at + HD] = total[:, HD:]

    each_peer(later_direct, lambda peer: kv_copy(peer).wait_send())

    @pl.when(chip >= 4)
    def _():
        for side in (0, 1):
            kv_forward(side).wait_send()

    @pl.when(chip < chips - 4)
    def _():
        for side in (0, 1):
            for group in range(groups):
                da_forward(group, side).wait_send()

    each_peer(earlier, lambda peer: q_copy(peer).wait_send())

    def sent_earlier(peer):
        for group in range(groups):
            da_copy(group, peer).wait_send()

    each_peer(earlier_direct, sent_earlier)
    loop(0, chip, lambda at: lse_copy(at).wait_send())
    norm_copy(core).wait_send()
    att_copy().wait_send()
    for group in range(groups):
        full_copy(group, core).wait_send()

    for group in range(groups):

        def sent_part(peer):
            glob_copy(group, peer).wait_send()
            grad_copy(group, peer).wait_send()

        each_part(sent_part)

    def sent_all(peer):
        wo_copy(peer).wait_send()
        wq_copy(peer).wait_send()
        wkv_copy(peer).wait_send()

    each_peer(anyone, sent_all)


def split_kernel(tall_sums, wide_sums, grad_query, grad_key, grad_value, grad_out):
    grad_query[...] = tall_sums[0]
    grad_key[...] = tall_sums[1]
    grad_value[...] = tall_sums[2]
    grad_out[...] = wide_sums[...]


def per_device(nctx, npb, *args):
    embed, w_query, w_key, w_value, w_out, ids, pad_embed, table, w_link, w_mix, w_lo, w_vocab = args
    rows, wide = embed.shape
    patches = rows // npb
    groups = 2
    local_rows = patches // groups * PATCH
    local_wide = w_link.shape[1]
    chips = nctx // 2
    block = wide // nctx
    vmem = pltpu.VMEM
    dma = pltpu.SemaphoreType.DMA
    near = [embed, w_query, w_key, w_value, w_out, table, w_link, w_mix, w_lo, w_vocab]
    scratch = [vmem(array.shape, BF) for array in near]
    scratch += [
        dma((len(near) + 1,)),
        vmem((2, rows, wide), BF),
        vmem((wide, 2 * rows), BF),
        vmem((2, 2, rows, HD), BF),
        vmem((2, nctx, rows, HD), BF),
        vmem((2, rows, HD), BF),
        vmem((nctx, rows, HD), BF),
        vmem((2, rows, HD), F32),
        vmem((2, rows, HD), F32),
        vmem((2, rows, HD), F32),
        vmem((2, rows, HD), BF),
        vmem((2, rows, HD), BF),
        vmem((2, rows, HD), F32),
        vmem((chips, 2, 8, rows), F32),
        vmem((npb, patches, wide), BF),
        vmem((npb, patches, wide), BF),
        vmem((groups, local_rows, local_wide), F32),
        vmem((local_rows, 3 * local_wide), BF),
        vmem((local_wide // LHD, local_rows, local_rows), F32),
        vmem((local_wide // LHD, local_rows, local_rows), F32),
        vmem((local_rows, 3 * local_wide), BF),
        vmem((PATCH, HD), jnp.int32),
        vmem((groups, local_rows, HD), jnp.int32),
        vmem((2, npb, patches, wide), BF),
        vmem((2, npb + 1, patches, HD), BF),
        vmem((nctx, npb + 1, patches, HD), BF),
        vmem((2, rows, HD), F32),
        vmem((2, rows, HD), F32),
        vmem((2, rows, HD), F32),
        vmem((nctx, HD, block), BF),
        vmem((nctx, block, HD), BF),
        vmem((nctx, block, 2 * HD), BF),
        vmem((nctx, HD, block), BF),
        vmem((nctx, block, HD), BF),
        vmem((nctx, block, 2 * HD), BF),
    ]
    scratch += [dma((nctx,))] * 10
    scratch += [dma((chips,))] * 2
    scratch += [dma((groups, npb))] * 4
    scratch += [dma] * 4 + [dma((groups,))] * 2 + [dma((groups, nctx))] * 2
    scratch += [dma((2,)), dma((groups, 2))]
    whole = pl.BlockSpec(memory_space=pltpu.VMEM)
    far = pl.BlockSpec(memory_space=pl.ANY)
    tall = jax.ShapeDtypeStruct((block, 2 * HD), BF)
    sums = pl.pallas_call(
        functools.partial(step_kernel, (nctx, npb)),
        out_shape=(
            jax.ShapeDtypeStruct((3, block, 2 * HD), BF),
            jax.ShapeDtypeStruct((2 * HD, block), BF),
        ),
        in_specs=[far] * 5 + [whole] * 2 + [far] * 5,
        out_specs=(whole,) * 2,
        scratch_shapes=scratch,
        compiler_params=pltpu.CompilerParams(
            collective_id=0, has_side_effects=True, vmem_limit_bytes=56 * 1024 * 1024
        ),
        name="step",
    )(
        embed, w_query, w_key, w_value, w_out, ids.T, pad_embed, table, w_link, w_mix,
        w_lo, w_vocab,
    )
    return pl.pallas_call(
        split_kernel,
        out_shape=(tall, tall, tall, jax.ShapeDtypeStruct((2 * HD, block), BF)),
        in_specs=[whole] * 2,
        out_specs=(whole,) * 4,
        name="split",
    )(*sums)


def solution(mesh):
    in_specs = (
        P("ctx", None),
        P(None, "pb"),
        P(None, "pb"),
        P(None, "pb"),
        P("pb", None),
        P(("ctx", "pb"), None),
        P(),
        P(),
        P(),
        P(),
        P(),
        P(),
    )
    out_specs = (P("ctx", "pb"), P("ctx", "pb"), P("ctx", "pb"), P("pb", "ctx"))
    return jax.shard_map(
        functools.partial(per_device, mesh.shape["ctx"], mesh.shape["pb"]),
        mesh=mesh,
        in_specs=in_specs,
        out_specs=out_specs,
        check_vma=False,
    )
```

```python
import functools

import jax
import jax.numpy as jnp
from jax import lax
from jax.experimental import pallas as pl
from jax.experimental.pallas import tpu as pltpu
from jax.sharding import PartitionSpec as P

HD = 128
LHD = 64
PATCH = 8
EPSILON = 1e-06
MASKED = -1e30
MESH = pl.DeviceIdType.MESH
BF = jnp.bfloat16
F32 = jnp.float32


def nn(left, right):
    return lax.dot_general(left, right, (((1,), (0,)), ((), ())), preferred_element_type=F32)


def nt(left, right):
    return lax.dot_general(left, right, (((1,), (1,)), ((), ())), preferred_element_type=F32)


def tn(left, right):
    return lax.dot_general(left, right, (((0,), (0,)), ((), ())), preferred_element_type=F32)


def loop(low, high, body):
    def step(index, unused):
        body(index)
        return unused

    lax.fori_loop(low, high, step, 0)


def row_form(column, rows):
    return jnp.transpose(jnp.broadcast_to(column, (rows, HD)))[0:8]


def rms_inverse(values):
    return lax.rsqrt(jnp.mean(values * values, axis=1, keepdims=True) + EPSILON)


def rms_back(values, inverse, grad):
    width = values.shape[1]
    dots = jnp.sum(grad * values, axis=1, keepdims=True)
    return inverse * grad - values * (inverse * inverse * inverse * dots * (1.0 / width))


def step_kernel(
    sizes,
    embed_far,
    w_query_far,
    w_key_far,
    w_value_far,
    w_out_far,
    ids,
    pad_embed,
    table_far,
    w_link_far,
    w_mix_far,
    w_local_out_far,
    w_vocab_far,
    tall_sums,
    wide_sums,
    w_query,
    w_key,
    w_value,
    w_out,
    table,
    w_link,
    w_mix,
    w_local_out,
    w_vocab,
    load_s,
    inputs,
    row_scale,
    inputs_turned,
    kv_send,
    kv_all,
    q_send,
    q_all,
    run_max,
    run_sum,
    run_out,
    att_head,
    att_pair,
    lse_col,
    lse_all,
    glob_part,
    glob_in,
    hidden,
    mixed,
    weights,
    d_weights,
    d_mixed,
    ids_wide,
    targets_all,
    grad_all,
    da_send,
    da_all,
    dq_acc,
    dk_acc,
    dv_acc,
    wo_send,
    wq_send,
    wkv_send,
    wo_in,
    wq_in,
    wkv_in,
    kv_s,
    kv_r,
    q_s,
    q_r,
    wo_s,
    wo_r,
    wq_s,
    wq_r,
    wkv_s,
    wkv_r,
    lse_s,
    lse_r,
    glob_s,
    glob_r,
    grad_s,
    grad_r,
    norm_s,
    norm_r,
    att_s,
    att_r,
    full_s,
    full_r,
    da_s,
    da_r,
    kv_forward_s,
    da_forward_s,
):
    nctx, npb = sizes
    chips = nctx // 2
    rows, wide = embed_far.shape
    patches = rows // npb
    bytes_here = patches * PATCH
    scale = HD ** (-0.5)
    place = lax.axis_index("ctx")
    part = lax.axis_index("pb")
    chip = lax.div(place, 2)
    core = lax.rem(place, 2)
    other = place + 1 - 2 * core

    def ctx_copy(src, dst, send, recv, peer):
        return pltpu.make_async_remote_copy(
            src_ref=src,
            dst_ref=dst,
            send_sem=send,
            recv_sem=recv,
            device_id=(peer, part),
            device_id_type=MESH,
        )

    def pb_copy(src, dst, send, recv, peer):
        return pltpu.make_async_remote_copy(
            src_ref=src,
            dst_ref=dst,
            send_sem=send,
            recv_sem=recv,
            device_id=(place, peer),
            device_id_type=MESH,
        )

    def each_peer(wanted, action):
        def one(step):
            peer = lax.rem(place + nctx - step, nctx)

            @pl.when(wanted(lax.div(peer, 2)))
            def _():
                action(peer)

        loop(1, nctx, one)

    def each_part(action):
        loop(1, npb, lambda step: action(lax.rem(part + step, npb)))

    half_rows = rows // 2
    pairs_in = (
        (embed_far.at[0:half_rows], inputs.at[core, 0:half_rows]),
        (embed_far.at[half_rows:rows], inputs.at[core, half_rows:rows]),
        (w_key_far, w_key),
        (w_value_far, w_value),
        (w_query_far, w_query),
        (w_out_far, w_out),
        (table_far, table),
        (w_link_far, w_link),
        (w_mix_far, w_mix),
        (w_local_out_far, w_local_out),
        (w_vocab_far, w_vocab),
    )
    loads = [
        pltpu.make_async_copy(far, near, load_s.at[index])
        for index, (far, near) in enumerate(pairs_in)
    ]
    for load in loads[:4]:
        load.start()

    later = lambda at: at >= chip
    earlier = lambda at: at <= chip
    anyone = lambda at: at >= 0

    def crossing(at, rows_away):
        return jnp.logical_and(lax.div(at, 2) - lax.div(chip, 2) == rows_away, lax.rem(at, 2) != lax.rem(chip, 2))

    later_direct = lambda at: jnp.logical_and(later(at), jnp.logical_not(crossing(at, 2)))
    earlier_direct = lambda at: jnp.logical_and(earlier(at), jnp.logical_not(crossing(at, -2)))
    neighbour = 2 * (chip + 1 - 2 * lax.rem(chip, 2)) + core

    barrier = pltpu.get_barrier_semaphore()

    def greet_ctx(peer):
        pl.semaphore_signal(barrier, inc=1, device_id=(peer, part), device_id_type=MESH)

    def greet_part(peer):
        pl.semaphore_signal(barrier, inc=1, device_id=(place, peer), device_id_type=MESH)

    each_peer(anyone, greet_ctx)
    each_part(greet_part)

    tile_rows = min(32, rows)

    def scale_rows(index):
        for low in range(0, rows, tile_rows):
            values = inputs[index, low : low + tile_rows, :].astype(F32)
            row_scale[index, low : low + tile_rows] = jnp.broadcast_to(
                rms_inverse(values), (tile_rows, HD)
            )

    loads[0].wait()
    loads[1].wait()
    loads[4].start()
    scale_rows(core)
    own_inputs = inputs[core]

    def scaled(product):
        return (product * row_scale[core, :, 0:1]).astype(BF)

    for slot, weight in ((0, w_key), (1, w_value)):
        loads[2 + slot].wait()
        product = scaled(nn(own_inputs, weight[...]))
        kv_send[0, slot] = product[:, :HD]
        kv_send[1, slot] = product[:, HD:]
    pl.semaphore_wait(barrier, nctx + npb - 2)

    def kv_copy(peer):
        return ctx_copy(
            kv_send.at[lax.rem(peer, 2)], kv_all.at[:, place], kv_s.at[peer], kv_r.at[place], peer
        )

    def kv_start(step):
        peer = lax.rem(place + step, nctx)

        @pl.when(later_direct(lax.div(peer, 2)))
        def _():
            kv_copy(peer).start()

    loop(1, nctx, kv_start)
    for load in loads[5:]:
        load.start()
    kv_all[:, place] = kv_send[core]
    loads[4].wait()
    product = scaled(nn(own_inputs, w_query[...]))
    q_send[0] = product[:, :HD]
    q_send[1] = product[:, HD:]

    def q_copy(peer):
        return ctx_copy(q_send.at[lax.rem(peer, 2)], q_all.at[place], q_s.at[peer], q_r.at[place], peer)

    q_copy(other).start()
    q_all[place] = q_send[core]

    def norm_copy(index):
        return ctx_copy(inputs.at[index], inputs.at[index], norm_s, norm_r, other)

    norm_copy(core).start()
    strictly_earlier = lambda at: at < chip
    each_peer(strictly_earlier, lambda peer: q_copy(peer).start())

    def kv_wait(peer):
        ctx_copy(kv_send.at[0], kv_all.at[:, peer], kv_s.at[peer], kv_r.at[peer], peer).wait_recv()

    def q_wait(peer):
        ctx_copy(q_send.at[0], q_all.at[peer], q_s.at[peer], q_r.at[peer], peer).wait_recv()

    first = 2 * chip
    pair_rows = 2 * rows

    def keys_of(at):
        return kv_all[0, pl.ds(2 * at, 2)].reshape(pair_rows, HD)

    def values_of(at):
        return kv_all[1, pl.ds(2 * at, 2)].reshape(pair_rows, HD)

    def diagonal(half, keys_down):
        shape = (rows, pair_rows)
        here = lax.broadcasted_iota(jnp.int32, shape, 0) + half * rows
        there = lax.broadcasted_iota(jnp.int32, shape, 1)
        return (there >= here) if keys_down else (there <= here)

    run_max[...] = jnp.full(run_max.shape, MASKED, F32)
    run_sum[...] = jnp.zeros(run_sum.shape, F32)
    run_out[...] = jnp.zeros(run_out.shape, F32)

    def attend(half, at, on_diagonal):
        scores = nt(q_all[first + half], keys_of(at)) * scale
        if on_diagonal:
            scores = jnp.where(diagonal(half, False), scores, MASKED)
        before = run_max[half, :, 0:1]
        highest = jnp.maximum(before, jnp.max(scores, axis=1, keepdims=True))
        exps = jnp.exp(scores - highest)
        factor = jnp.exp(before - highest)
        total = run_sum[half, :, 0:1] * factor + jnp.sum(exps, axis=1, keepdims=True)
        run_out[half] = run_out[half] * factor + nn(exps.astype(BF), values_of(at))
        run_max[half] = jnp.broadcast_to(highest, (rows, HD))
        run_sum[half] = jnp.broadcast_to(total, (rows, HD))

    kv_wait(other)
    q_wait(other)
    for half in (0, 1):
        attend(half, chip, True)
    norm_copy(1 - core).wait_recv()
    scale_rows(1 - core)
    turn_tile = min(128, wide)

    def turn_columns(step):
        here = pl.ds(pl.multiple_of(step * turn_tile, turn_tile), turn_tile)
        block = inputs[:, :, here].reshape(pair_rows, turn_tile)
        inputs_turned[here, :] = jnp.transpose(block.astype(F32)).astype(BF)

    loop(0, wide // turn_tile, turn_columns)
    for load in loads[5:]:
        load.wait()

    def kv_forward(side):
        source = 2 * (chip - 4) + side
        block = kv_all.at[:, source]
        return ctx_copy(block, block, kv_forward_s.at[side], kv_r.at[source], neighbour)

    @pl.when(chip >= 4)
    def _():
        for side in (0, 1):
            kv_wait(2 * (chip - 4) + side)
            kv_forward(side).start()
        for half in (0, 1):
            attend(half, chip - 4, False)

    def attend_earlier(step):
        at = chip - step

        @pl.when(step != 4)
        def _():
            kv_wait(2 * at)
            kv_wait(2 * at + 1)
            for half in (0, 1):
                attend(half, at, False)

    loop(1, chip + 1, attend_earlier)
    for half in (0, 1):
        att_head[half] = (run_out[half] / run_sum[half]).astype(BF)
        log_total = run_max[half] + jnp.log(run_sum[half])
        lse_col[half] = log_total
        lse_all[chip, half] = jnp.transpose(log_total)[0:8]

    def att_copy():
        return ctx_copy(att_head.at[1 - core], att_pair.at[core], att_s, att_r, other)

    att_copy().start()
    att_pair[core] = att_head[core]

    def lse_copy(at):
        return ctx_copy(
            lse_all.at[chip], lse_all.at[chip], lse_s.at[at], lse_r.at[chip], 2 * at + core
        )

    loop(0, chip, lambda at: lse_copy(at).start())
    ctx_copy(att_head.at[0], att_pair.at[1 - core], att_s, att_r, other).wait_recv()

    both_heads = jnp.concatenate([att_pair[0], att_pair[1]], axis=1)
    out_tile = min(512, wide)

    def out_columns(step):
        here = pl.ds(pl.multiple_of(step * out_tile, out_tile), out_tile)
        product = nn(both_heads, w_out[:, here]).astype(BF)
        glob_part[:, :, here] = product.reshape(npb, patches, out_tile)

    loop(0, wide // out_tile, out_columns)

    groups = 2
    share = patches // groups

    def glob_copy(group, peer):
        here = pl.ds(pl.multiple_of(group * share, share), share)
        return pb_copy(
            glob_part.at[peer, here],
            glob_in.at[part, here],
            glob_s.at[group, peer],
            glob_r.at[group, part],
            peer,
        )

    def glob_wait(group, peer):
        here = pl.ds(pl.multiple_of(group * share, share), share)
        pb_copy(
            glob_part.at[0, here],
            glob_in.at[peer, here],
            glob_s.at[group, peer],
            glob_r.at[group, peer],
            peer,
        ).wait_recv()

    for group in range(groups):
        each_part(lambda peer: glob_copy(group, peer).start())
    glob_in[part] = glob_part[part]

    count = share * PATCH
    byte_wide = wide // PATCH
    local_wide = w_link.shape[1]
    pairs = local_wide // (2 * LHD)
    symbols = lax.broadcasted_iota(jnp.int32, (count, table.shape[0]), 1)
    nothing = jnp.full((share, 1), -1, jnp.int32)
    ids_wide[:, 0:patches] = ids[...]
    for group in range(groups):
        columns = []
        for b in range(PATCH):
            line = jnp.broadcast_to(ids_wide[b : b + 1, :], (HD, HD))
            columns.append(jnp.transpose(line)[group * share : (group + 1) * share, 0:1])
        preceding = jnp.concatenate([nothing] + columns[:-1], axis=0)
        targets_all[group] = jnp.broadcast_to(jnp.concatenate(columns, axis=0), (count, HD))
        hidden[group] = nn((preceding == symbols).astype(BF), table[...]) + jnp.where(
            preceding < 0, pad_embed[...].astype(F32).reshape(1, local_wide), 0.0
        )
    row_index = lax.broadcasted_iota(jnp.int32, (count, count), 0)
    column_index = lax.broadcasted_iota(jnp.int32, (count, count), 1)
    same = jnp.logical_and(
        lax.rem(row_index, share) == lax.rem(column_index, share), column_index <= row_index
    )
    lane = lax.broadcasted_iota(jnp.int32, (count, 2 * LHD), 1)
    halves = (lane < LHD, lane >= LHD)

    def pair_of(block, pair):
        low = block * local_wide + pair * 2 * LHD
        return mixed[:, low : low + 2 * LHD]

    def kept(values, side):
        return jnp.where(halves[side], values, jnp.zeros_like(values))

    def grad_copy(group, peer):
        mine = grad_all.at[core, part, pl.ds(pl.multiple_of(group * share, share), share)]
        return pb_copy(mine, mine, grad_s.at[group, peer], grad_r.at[group, part], peer)

    def grad_wait(group, peer):
        theirs = grad_all.at[core, peer, pl.ds(pl.multiple_of(group * share, share), share)]
        pb_copy(theirs, theirs, grad_s.at[group, peer], grad_r.at[group, peer], peer).wait_recv()

    def local_model(group):
        here = pl.ds(pl.multiple_of(group * share, share), share)
        each_part(lambda peer: glob_wait(group, peer))
        glob = glob_in[0, here, :].astype(F32)
        for index in range(1, npb):
            glob = glob + glob_in[index, here, :].astype(F32)
        glob = glob.astype(BF)
        pieces = jnp.concatenate(
            [glob[:, b * byte_wide : (b + 1) * byte_wide] for b in range(PATCH)], axis=0
        )
        hidden_one = hidden[group] + nn(pieces, w_link[...])
        hidden[group] = hidden_one
        inverse_one = rms_inverse(hidden_one)
        mixed[...] = nn((hidden_one * inverse_one).astype(BF), w_mix[...]).astype(BF)
        heads = 2 * pairs
        for head in range(heads):
            query = kept(pair_of(0, head // 2), head % 2)
            weights[head] = nt(query, pair_of(1, head // 2))
        scores = jnp.where(same[None], weights[...] * LHD ** (-0.5), MASKED)
        exps = jnp.exp(scores - jnp.max(scores, axis=2, keepdims=True))
        weights[...] = exps / jnp.sum(exps, axis=2, keepdims=True)
        local_att = []
        for pair in range(pairs):
            terms = [
                nn(weights[2 * pair + side].astype(BF), kept(pair_of(2, pair), side))
                for side in (0, 1)
            ]
            local_att.append((terms[0] + terms[1]).astype(BF))
        hidden_two = hidden[group] + nn(jnp.concatenate(local_att, axis=1), w_local_out[...])
        inverse_two = rms_inverse(hidden_two)
        logits = nn((hidden_two * inverse_two).astype(BF), w_vocab[...])
        exps = jnp.exp(logits - jnp.max(logits, axis=1, keepdims=True))
        soft = exps / jnp.sum(exps, axis=1, keepdims=True)
        d_logits = (
            soft - jnp.where(targets_all[group, :, 0:1] == symbols, 1.0, 0.0)
        ) * (1.0 / (rows * nctx * PATCH))
        d_normed_two = nt(d_logits.astype(BF), w_vocab[...]).astype(BF).astype(F32)
        d_hidden = rms_back(hidden_two, inverse_two, d_normed_two)
        d_local_att = nt(d_hidden.astype(BF), w_local_out[...]).astype(BF)
        d_heads = [
            kept(d_local_att[:, pair * 2 * LHD : (pair + 1) * 2 * LHD], side)
            for pair in range(pairs)
            for side in (0, 1)
        ]
        for head in range(heads):
            d_weights[head] = nt(d_heads[head], pair_of(2, head // 2))
        d_soft = d_weights[...].astype(BF).astype(F32)
        soft = weights[...]
        dots = jnp.sum(d_soft * soft, axis=2, keepdims=True)
        d_weights[...] = soft * (d_soft - dots) * LHD ** (-0.5)
        for pair in range(pairs):
            terms = [[], [], []]
            for side in (0, 1):
                head = 2 * pair + side
                d_scores = d_weights[head].astype(BF)
                terms[0].append(nn(d_scores, kept(pair_of(1, pair), side)))
                terms[1].append(tn(d_scores, kept(pair_of(0, pair), side)))
                terms[2].append(tn(weights[head].astype(BF), d_heads[head]))
            for block in range(3):
                at = block * local_wide + pair * 2 * LHD
                d_mixed[:, at : at + 2 * LHD] = (terms[block][0] + terms[block][1]).astype(BF)
        d_normed_one = nt(d_mixed[...], w_mix[...]).astype(BF).astype(F32)
        hidden_one = hidden[group]
        d_hidden = d_hidden + rms_back(hidden_one, rms_inverse(hidden_one), d_normed_one)
        d_pieces = nt(d_hidden.astype(BF), w_link[...]).astype(BF)
        for b in range(PATCH):
            grad_all[core, part, here, b * byte_wide : (b + 1) * byte_wide] = d_pieces[
                b * share : (b + 1) * share
            ]
        each_part(lambda peer: grad_copy(group, peer).start())

    each_peer(later_direct, lambda peer: kv_copy(peer).wait_send())

    @pl.when(chip >= 4)
    def _():
        for side in (0, 1):
            kv_forward(side).wait_send()

    each_peer(earlier, lambda peer: q_copy(peer).wait_send())
    loop(0, chip, lambda at: lse_copy(at).wait_send())
    norm_copy(core).wait_send()
    att_copy().wait_send()

    loop(0, groups, local_model)
    def full_copy(group, index):
        here = pl.ds(group * share, share)
        block = grad_all.at[index, :, here]
        return ctx_copy(block, block, full_s.at[group], full_r.at[group], other)

    last = groups - 1

    def da_parts(group, whole):
        return whole.at[0 : npb + 1 if group == last else npb, group * share : (group + 1) * share]

    def da_copy(group, peer):
        return ctx_copy(
            da_parts(group, da_send.at[lax.rem(peer, 2)]),
            da_parts(group, da_all.at[place]),
            da_s.at[group, peer],
            da_r.at[group, place],
            peer,
        )

    def da_wait_part(group, peer):
        ctx_copy(
            da_parts(group, da_send.at[0]),
            da_parts(group, da_all.at[peer]),
            da_s.at[group, peer],
            da_r.at[group, peer],
            peer,
        ).wait_recv()

    def da_wait(peer):
        for group in range(groups):
            da_wait_part(group, peer)

    def da_forward(group, side):
        source = 2 * (chip + 4) + side
        block = da_parts(group, da_all.at[source])
        return ctx_copy(
            block, block, da_forward_s.at[group, side], da_r.at[group, source], neighbour
        )

    for group in range(groups):
        each_part(lambda peer: grad_wait(group, peer))
        full_copy(group, core).start()
        here = slice(group * share, (group + 1) * share)
        grads = grad_all[core, :, here, :].reshape(npb * share, wide)
        product = nt(grads, w_out[...]).astype(BF)
        for head in (0, 1):
            d_att = product[:, head * HD : (head + 1) * HD]
            da_send[head, 0:npb, here, :] = d_att.reshape(npb, share, HD)
        if group == last:
            for head in (0, 1):
                d_att = da_send[head, 0:npb].reshape(rows, HD).astype(F32)
                dots = jnp.sum(d_att * att_pair[head].astype(F32), axis=1, keepdims=True)
                exact = row_form(dots, rows)
                high = exact.astype(BF)
                low = (exact - high.astype(F32)).astype(BF)
                spare = jnp.concatenate([high[0:1], low[0:1]], axis=0)
                tail = [spare[:, at : at + HD] for at in range(0, rows, HD)]
                filler = jnp.zeros((share - 2 * len(tail), HD), BF)
                da_send[head, npb, here, :] = jnp.concatenate(tail + [filler], axis=0)
        each_peer(earlier_direct, lambda peer: da_copy(group, peer).start())

    def grads_of(device):
        return da_all[device, 0:npb].reshape(rows, HD)

    def dots_of(device):
        tail = da_all[device, npb, last * share : (last + 1) * share].astype(F32)
        pieces = [
            tail[2 * at : 2 * at + 1] + tail[2 * at + 1 : 2 * at + 2] for at in range(rows // HD)
        ]
        return jnp.concatenate(pieces, axis=1)

    da_all[place] = da_send[core]

    block_wide = wide // nctx
    term_rows = min(512, wide)
    owners = term_rows // block_wide

    def wo_copy(peer):
        return ctx_copy(wo_send.at[peer], wo_in.at[place], wo_s.at[peer], wo_r.at[place], peer)

    def wq_copy(peer):
        return ctx_copy(wq_send.at[peer], wq_in.at[place], wq_s.at[peer], wq_r.at[place], peer)

    def wkv_copy(peer):
        return ctx_copy(wkv_send.at[peer], wkv_in.at[place], wkv_s.at[peer], wkv_r.at[place], peer)

    for group in range(groups):
        full_copy(group, 1 - core).wait_recv()
    att_turned = jnp.transpose(att_head[...].reshape(pair_rows, HD).astype(F32)).astype(BF)

    def wo_block(step):
        here = pl.ds(pl.multiple_of(step * term_rows, term_rows), term_rows)
        grads = grad_all[:, :, :, here].reshape(pair_rows, term_rows)
        terms = nn(att_turned, grads).astype(BF)
        for index in range(owners):
            wo_send[step * owners + index] = terms[:, index * block_wide : (index + 1) * block_wide]

    loop(0, wide // term_rows, wo_block)
    each_peer(anyone, lambda peer: wo_copy(peer).start())
    wo_in[place] = wo_send[place]
    da_wait(other)

    dq_acc[...] = jnp.zeros(dq_acc.shape, F32)

    def query_back(half, at, on_diagonal):
        scores = nt(q_all[first + half], keys_of(at)) * scale
        probs = jnp.exp(scores - lse_col[half, :, 0:1])
        if on_diagonal:
            probs = jnp.where(diagonal(half, False), probs, 0.0)
        d_probs = nt(grads_of(first + half), values_of(at))
        d_scores = (probs * (d_probs - run_sum[half, :, 0:1]) * scale).astype(BF)
        dq_acc[half] += nn(d_scores, keys_of(at))

    for half in (0, 1):
        dots = jnp.sum(
            grads_of(first + half).astype(F32) * att_head[half].astype(F32), axis=1, keepdims=True
        )
        run_sum[half] = jnp.broadcast_to(dots, (rows, HD))
    for half in (0, 1):
        query_back(half, chip, True)

    def query_earlier(step):
        for half in (0, 1):
            query_back(half, chip - step, False)

    loop(1, chip + 1, query_earlier)

    dq_ready = (dq_acc[...] * row_scale[...]).reshape(pair_rows, HD).astype(BF)

    def wq_block(step):
        here = pl.ds(pl.multiple_of(step * term_rows, term_rows), term_rows)
        terms = nn(inputs_turned[here, :], dq_ready).astype(BF)
        wq_send[pl.ds(step * owners, owners)] = terms.reshape(owners, block_wide, HD)

    loop(0, wide // term_rows, wq_block)
    each_peer(anyone, lambda peer: wq_copy(peer).start())
    wq_in[place] = wq_send[place]

    dk_acc[...] = jnp.zeros(dk_acc.shape, F32)
    dv_acc[...] = jnp.zeros(dv_acc.shape, F32)

    def key_back(half, at, on_diagonal):
        queries = q_all[pl.ds(2 * at, 2)].reshape(pair_rows, HD)
        grads = da_all[pl.ds(2 * at, 2), 0:npb].reshape(pair_rows, HD)
        log_total = jnp.concatenate([lse_all[at, 0, 0:1, :], lse_all[at, 1, 0:1, :]], axis=1)
        dots = jnp.concatenate([dots_of(2 * at), dots_of(2 * at + 1)], axis=1)
        scores = nt(kv_all[0, first + half], queries) * scale
        probs = jnp.exp(scores - log_total)
        if on_diagonal:
            probs = jnp.where(diagonal(half, True), probs, 0.0)
        d_probs = nt(kv_all[1, first + half], grads)
        d_scores = (probs * (d_probs - dots) * scale).astype(BF)
        dv_acc[half] += nn(probs.astype(BF), grads)
        dk_acc[half] += nn(d_scores, queries)

    for half in (0, 1):
        key_back(half, chip, True)

    def rest_wait(at):
        q_wait(2 * at)
        q_wait(2 * at + 1)
        ctx_copy(
            lse_all.at[at], lse_all.at[at], lse_s.at[at], lse_r.at[at], 2 * at + core
        ).wait_recv()

    @pl.when(chip < chips - 4)
    def _():
        for group in range(groups):
            for side in (0, 1):
                da_wait_part(group, 2 * (chip + 4) + side)
                da_forward(group, side).start()
        rest_wait(chip + 4)
        for half in (0, 1):
            key_back(half, chip + 4, False)

    def key_later(at):
        @pl.when(at != chip + 4)
        def _():
            da_wait(2 * at)
            da_wait(2 * at + 1)
            rest_wait(at)
            for half in (0, 1):
                key_back(half, at, False)

    loop(chip + 1, chips, key_later)
    dkv_ready = jnp.concatenate(
        [
            (total[...] * row_scale[...]).reshape(pair_rows, HD).astype(BF)
            for total in (dk_acc, dv_acc)
        ],
        axis=1,
    )

    def wkv_block(step):
        here = pl.ds(pl.multiple_of(step * term_rows, term_rows), term_rows)
        terms = nn(inputs_turned[here, :], dkv_ready).astype(BF)
        wkv_send[pl.ds(step * owners, owners)] = terms.reshape(owners, block_wide, 2 * HD)

    loop(0, wide // term_rows, wkv_block)
    each_peer(anyone, lambda peer: wkv_copy(peer).start())
    wkv_in[place] = wkv_send[place]

    def sent_part(peer):
        for group in range(groups):
            glob_copy(group, peer).wait_send()
            grad_copy(group, peer).wait_send()

    each_part(sent_part)

    def sent_earlier(peer):
        for group in range(groups):
            da_copy(group, peer).wait_send()

    each_peer(earlier_direct, sent_earlier)

    @pl.when(chip < chips - 4)
    def _():
        for side in (0, 1):
            for group in range(groups):
                da_forward(group, side).wait_send()

    for group in range(groups):
        full_copy(group, core).wait_send()

    def sent_all(peer):
        wo_copy(peer).wait_send()
        wq_copy(peer).wait_send()
        wkv_copy(peer).wait_send()

    def total_of(pick, head):
        total = pick(head).astype(F32)
        for index in range(1, chips):
            total = total + pick(2 * index + head).astype(F32)
        return total.astype(BF)

    def wo_wait(peer):
        ctx_copy(wo_send.at[0], wo_in.at[peer], wo_s.at[peer], wo_r.at[peer], peer).wait_recv()

    def wq_wait(peer):
        ctx_copy(wq_send.at[0], wq_in.at[peer], wq_s.at[peer], wq_r.at[peer], peer).wait_recv()

    def wkv_wait(peer):
        ctx_copy(wkv_send.at[0], wkv_in.at[peer], wkv_s.at[peer], wkv_r.at[peer], peer).wait_recv()

    each_peer(anyone, wo_wait)
    for head in (0, 1):
        wide_sums[head * HD : (head + 1) * HD, :] = total_of(lambda index: wo_in[index], head)
    each_peer(anyone, wq_wait)
    for head in (0, 1):
        at = head * HD
        tall_sums[0, :, at : at + HD] = total_of(lambda index: wq_in[index], head)
    each_peer(anyone, sent_all)
    each_peer(anyone, wkv_wait)
    for head in (0, 1):
        at = head * HD
        total = total_of(lambda index: wkv_in[index], head)
        tall_sums[1, :, at : at + HD] = total[:, :HD]
        tall_sums[2, :, at : at + HD] = total[:, HD:]


def split_kernel(tall_sums, wide_sums, grad_query, grad_key, grad_value, grad_out):
    grad_query[...] = tall_sums[0]
    grad_key[...] = tall_sums[1]
    grad_value[...] = tall_sums[2]
    grad_out[...] = wide_sums[...]


def per_device(nctx, npb, *args):
    embed, w_query, w_key, w_value, w_out, ids, pad_embed, table, w_link, w_mix, w_lo, w_vocab = args
    rows, wide = embed.shape
    patches = rows // npb
    groups = 2
    local_rows = patches // groups * PATCH
    local_wide = w_link.shape[1]
    chips = nctx // 2
    block = wide // nctx
    vmem = pltpu.VMEM
    dma = pltpu.SemaphoreType.DMA
    near = [w_query, w_key, w_value, w_out, table, w_link, w_mix, w_lo, w_vocab]
    scratch = [vmem(array.shape, BF) for array in near]
    scratch += [
        dma((len(near) + 2,)),
        vmem((2, rows, wide), BF),
        vmem((2, rows, HD), F32),
        vmem((wide, 2 * rows), BF),
        vmem((2, 2, rows, HD), BF),
        vmem((2, nctx, rows, HD), BF),
        vmem((2, rows, HD), BF),
        vmem((nctx, rows, HD), BF),
        vmem((2, rows, HD), F32),
        vmem((2, rows, HD), F32),
        vmem((2, rows, HD), F32),
        vmem((2, rows, HD), BF),
        vmem((2, rows, HD), BF),
        vmem((2, rows, HD), F32),
        vmem((chips, 2, 8, rows), F32),
        vmem((npb, patches, wide), BF),
        vmem((npb, patches, wide), BF),
        vmem((groups, local_rows, local_wide), F32),
        vmem((local_rows, 3 * local_wide), BF),
        vmem((local_wide // LHD, local_rows, local_rows), F32),
        vmem((local_wide // LHD, local_rows, local_rows), F32),
        vmem((local_rows, 3 * local_wide), BF),
        vmem((PATCH, HD), jnp.int32),
        vmem((groups, local_rows, HD), jnp.int32),
        vmem((2, npb, patches, wide), BF),
        vmem((2, npb + 1, patches, HD), BF),
        vmem((nctx, npb + 1, patches, HD), BF),
        vmem((2, rows, HD), F32),
        vmem((2, rows, HD), F32),
        vmem((2, rows, HD), F32),
        vmem((nctx, HD, block), BF),
        vmem((nctx, block, HD), BF),
        vmem((nctx, block, 2 * HD), BF),
        vmem((nctx, HD, block), BF),
        vmem((nctx, block, HD), BF),
        vmem((nctx, block, 2 * HD), BF),
    ]
    scratch += [dma((nctx,))] * 10
    scratch += [dma((chips,))] * 2
    scratch += [dma((groups, npb))] * 4
    scratch += [dma] * 4 + [dma((groups,))] * 2 + [dma((groups, nctx))] * 2
    scratch += [dma((2,)), dma((groups, 2))]
    whole = pl.BlockSpec(memory_space=pltpu.VMEM)
    far = pl.BlockSpec(memory_space=pl.ANY)
    tall = jax.ShapeDtypeStruct((block, 2 * HD), BF)
    sums = pl.pallas_call(
        functools.partial(step_kernel, (nctx, npb)),
        out_shape=(
            jax.ShapeDtypeStruct((3, block, 2 * HD), BF),
            jax.ShapeDtypeStruct((2 * HD, block), BF),
        ),
        in_specs=[far] * 5 + [whole] * 2 + [far] * 5,
        out_specs=(whole,) * 2,
        scratch_shapes=scratch,
        compiler_params=pltpu.CompilerParams(
            collective_id=0, has_side_effects=True, vmem_limit_bytes=56 * 1024 * 1024
        ),
        name="step",
    )(
        embed, w_query, w_key, w_value, w_out, ids.T, pad_embed, table, w_link, w_mix,
        w_lo, w_vocab,
    )
    return pl.pallas_call(
        split_kernel,
        out_shape=(tall, tall, tall, jax.ShapeDtypeStruct((2 * HD, block), BF)),
        in_specs=[whole] * 2,
        out_specs=(whole,) * 4,
        name="split",
    )(*sums)


def solution(mesh):
    in_specs = (
        P("ctx", None),
        P(None, "pb"),
        P(None, "pb"),
        P(None, "pb"),
        P("pb", None),
        P(("ctx", "pb"), None),
        P(),
        P(),
        P(),
        P(),
        P(),
        P(),
    )
    out_specs = (P("ctx", "pb"), P("ctx", "pb"), P("ctx", "pb"), P("pb", "ctx"))
    return jax.shard_map(
        functools.partial(per_device, mesh.shape["ctx"], mesh.shape["pb"]),
        mesh=mesh,
        in_specs=in_specs,
        out_specs=out_specs,
        check_vma=False,
    )
```

```python
import functools

import jax
import jax.numpy as jnp
from jax import lax
from jax.experimental import pallas as pl
from jax.experimental.pallas import tpu as pltpu
from jax.sharding import PartitionSpec as P

HD = 128
LHD = 64
PATCH = 8
EPSILON = 1e-06
MASKED = -1e30
MESH = pl.DeviceIdType.MESH
BF = jnp.bfloat16
F32 = jnp.float32


def nn(left, right):
    return lax.dot_general(left, right, (((1,), (0,)), ((), ())), preferred_element_type=F32)


def nt(left, right):
    return lax.dot_general(left, right, (((1,), (1,)), ((), ())), preferred_element_type=F32)


def tn(left, right):
    return lax.dot_general(left, right, (((0,), (0,)), ((), ())), preferred_element_type=F32)


def loop(low, high, body):
    def step(index, unused):
        body(index)
        return unused

    lax.fori_loop(low, high, step, 0)


def row_form(column, rows):
    return jnp.transpose(jnp.broadcast_to(column, (rows, HD)))[0:8]


def rms_inverse(values):
    return lax.rsqrt(jnp.mean(values * values, axis=1, keepdims=True) + EPSILON)


def rms_back(values, inverse, grad):
    width = values.shape[1]
    dots = jnp.sum(grad * values, axis=1, keepdims=True)
    return inverse * grad - values * (inverse * inverse * inverse * dots * (1.0 / width))


def step_kernel(
    sizes,
    embed_far,
    w_query_far,
    w_key_far,
    w_value_far,
    w_out_far,
    ids,
    pad_embed,
    table_far,
    w_link_far,
    w_mix_far,
    w_local_out_far,
    w_vocab_far,
    tall_sums,
    wide_sums,
    w_query,
    w_key,
    w_value,
    w_out,
    table,
    w_link,
    w_mix,
    w_local_out,
    w_vocab,
    load_s,
    inputs,
    row_scale,
    inputs_turned,
    kv_send,
    kv_all,
    q_send,
    q_all,
    run_max,
    run_sum,
    run_out,
    att_head,
    att_pair,
    lse_col,
    lse_all,
    glob_part,
    glob_in,
    hidden,
    mixed,
    weights,
    d_weights,
    d_mixed,
    ids_wide,
    targets_all,
    grad_all,
    da_send,
    da_all,
    dq_acc,
    dk_acc,
    dv_acc,
    wo_send,
    wq_send,
    wkv_send,
    wo_in,
    wq_in,
    wkv_in,
    kv_s,
    kv_r,
    q_s,
    q_r,
    wo_s,
    wo_r,
    wq_s,
    wq_r,
    wkv_s,
    wkv_r,
    lse_s,
    lse_r,
    glob_s,
    glob_r,
    grad_s,
    grad_r,
    norm_s,
    norm_r,
    att_s,
    att_r,
    full_s,
    full_r,
    da_s,
    da_r,
    kv_forward_s,
    da_forward_s,
):
    nctx, npb = sizes
    chips = nctx // 2
    rows, wide = embed_far.shape
    patches = rows // npb
    bytes_here = patches * PATCH
    scale = HD ** (-0.5)
    place = lax.axis_index("ctx")
    part = lax.axis_index("pb")
    chip = lax.div(place, 2)
    core = lax.rem(place, 2)
    other = place + 1 - 2 * core

    def ctx_copy(src, dst, send, recv, peer):
        return pltpu.make_async_remote_copy(
            src_ref=src,
            dst_ref=dst,
            send_sem=send,
            recv_sem=recv,
            device_id=(peer, part),
            device_id_type=MESH,
        )

    def pb_copy(src, dst, send, recv, peer):
        return pltpu.make_async_remote_copy(
            src_ref=src,
            dst_ref=dst,
            send_sem=send,
            recv_sem=recv,
            device_id=(place, peer),
            device_id_type=MESH,
        )

    def each_peer(wanted, action):
        def one(step):
            peer = lax.rem(place + nctx - step, nctx)

            @pl.when(wanted(lax.div(peer, 2)))
            def _():
                action(peer)

        loop(1, nctx, one)

    def each_part(action):
        loop(1, npb, lambda step: action(lax.rem(part + step, npb)))

    half_rows = rows // 2
    pairs_in = (
        (embed_far.at[0:half_rows], inputs.at[core, 0:half_rows]),
        (embed_far.at[half_rows:rows], inputs.at[core, half_rows:rows]),
        (w_key_far, w_key),
        (w_value_far, w_value),
        (w_query_far, w_query),
        (w_out_far, w_out),
        (table_far, table),
        (w_link_far, w_link),
        (w_mix_far, w_mix),
        (w_local_out_far, w_local_out),
        (w_vocab_far, w_vocab),
    )
    loads = [
        pltpu.make_async_copy(far, near, load_s.at[index])
        for index, (far, near) in enumerate(pairs_in)
    ]
    for load in loads[:4]:
        load.start()

    later = lambda at: at >= chip
    earlier = lambda at: at <= chip
    anyone = lambda at: at >= 0

    def crossing(at, rows_away):
        return jnp.logical_and(lax.div(at, 2) - lax.div(chip, 2) == rows_away, lax.rem(at, 2) != lax.rem(chip, 2))

    later_direct = lambda at: jnp.logical_and(later(at), jnp.logical_not(crossing(at, 2)))
    earlier_direct = lambda at: jnp.logical_and(earlier(at), jnp.logical_not(crossing(at, -2)))
    neighbour = 2 * (chip + 1 - 2 * lax.rem(chip, 2)) + core

    barrier = pltpu.get_barrier_semaphore()

    def greet_ctx(peer):
        pl.semaphore_signal(barrier, inc=1, device_id=(peer, part), device_id_type=MESH)

    def greet_part(peer):
        pl.semaphore_signal(barrier, inc=1, device_id=(place, peer), device_id_type=MESH)

    each_peer(anyone, greet_ctx)
    each_part(greet_part)

    tile_rows = min(32, rows)

    def scale_rows(index):
        for low in range(0, rows, tile_rows):
            values = inputs[index, low : low + tile_rows, :].astype(F32)
            row_scale[index, low : low + tile_rows] = jnp.broadcast_to(
                rms_inverse(values), (tile_rows, HD)
            )

    loads[0].wait()
    loads[1].wait()
    loads[4].start()
    scale_rows(core)
    own_inputs = inputs[core]

    def scaled(product):
        return (product * row_scale[core, :, 0:1]).astype(BF)

    for slot, weight in ((0, w_key), (1, w_value)):
        loads[2 + slot].wait()
        product = scaled(nn(own_inputs, weight[...]))
        kv_send[0, slot] = product[:, :HD]
        kv_send[1, slot] = product[:, HD:]
    pl.semaphore_wait(barrier, nctx + npb - 2)

    def kv_copy(peer):
        return ctx_copy(
            kv_send.at[lax.rem(peer, 2)], kv_all.at[:, place], kv_s.at[peer], kv_r.at[place], peer
        )

    def kv_start(step):
        peer = lax.rem(place + step, nctx)

        @pl.when(later_direct(lax.div(peer, 2)))
        def _():
            kv_copy(peer).start()

    loop(1, nctx, kv_start)
    for load in loads[5:]:
        load.start()
    kv_all[:, place] = kv_send[core]
    loads[4].wait()
    product = scaled(nn(own_inputs, w_query[...]))
    q_send[0] = product[:, :HD]
    q_send[1] = product[:, HD:]

    def q_copy(peer):
        return ctx_copy(q_send.at[lax.rem(peer, 2)], q_all.at[place], q_s.at[peer], q_r.at[place], peer)

    q_copy(other).start()
    q_all[place] = q_send[core]

    def norm_copy(index):
        return ctx_copy(inputs.at[index], inputs.at[index], norm_s, norm_r, other)

    norm_copy(core).start()
    strictly_earlier = lambda at: at < chip
    each_peer(strictly_earlier, lambda peer: q_copy(peer).start())

    def kv_wait(peer):
        ctx_copy(kv_send.at[0], kv_all.at[:, peer], kv_s.at[peer], kv_r.at[peer], peer).wait_recv()

    def q_wait(peer):
        ctx_copy(q_send.at[0], q_all.at[peer], q_s.at[peer], q_r.at[peer], peer).wait_recv()

    first = 2 * chip
    pair_rows = 2 * rows

    def keys_of(at):
        return kv_all[0, pl.ds(2 * at, 2)].reshape(pair_rows, HD)

    def values_of(at):
        return kv_all[1, pl.ds(2 * at, 2)].reshape(pair_rows, HD)

    def diagonal(half, keys_down):
        shape = (rows, pair_rows)
        here = lax.broadcasted_iota(jnp.int32, shape, 0) + half * rows
        there = lax.broadcasted_iota(jnp.int32, shape, 1)
        return (there >= here) if keys_down else (there <= here)

    run_max[...] = jnp.full(run_max.shape, MASKED, F32)
    run_sum[...] = jnp.zeros(run_sum.shape, F32)
    run_out[...] = jnp.zeros(run_out.shape, F32)

    def attend(half, at, on_diagonal):
        scores = nt(q_all[first + half], keys_of(at)) * scale
        if on_diagonal:
            scores = jnp.where(diagonal(half, False), scores, MASKED)
        before = run_max[half, :, 0:1]
        highest = jnp.maximum(before, jnp.max(scores, axis=1, keepdims=True))
        exps = jnp.exp(scores - highest)
        factor = jnp.exp(before - highest)
        total = run_sum[half, :, 0:1] * factor + jnp.sum(exps, axis=1, keepdims=True)
        run_out[half] = run_out[half] * factor + nn(exps.astype(BF), values_of(at))
        run_max[half] = jnp.broadcast_to(highest, (rows, HD))
        run_sum[half] = jnp.broadcast_to(total, (rows, HD))

    kv_wait(other)
    q_wait(other)
    for half in (0, 1):
        attend(half, chip, True)
    norm_copy(1 - core).wait_recv()
    scale_rows(1 - core)
    turn_tile = min(128, wide)

    def turn_columns(step):
        here = pl.ds(pl.multiple_of(step * turn_tile, turn_tile), turn_tile)
        block = inputs[:, :, here].reshape(pair_rows, turn_tile)
        inputs_turned[here, :] = jnp.transpose(block.astype(F32)).astype(BF)

    loop(0, wide // turn_tile, turn_columns)
    for load in loads[5:]:
        load.wait()

    def kv_forward(side):
        source = 2 * (chip - 4) + side
        block = kv_all.at[:, source]
        return ctx_copy(block, block, kv_forward_s.at[side], kv_r.at[source], neighbour)

    @pl.when(chip >= 4)
    def _():
        for side in (0, 1):
            kv_wait(2 * (chip - 4) + side)
            kv_forward(side).start()
        for half in (0, 1):
            attend(half, chip - 4, False)

    def attend_earlier(step):
        at = chip - step

        @pl.when(step != 4)
        def _():
            kv_wait(2 * at)
            kv_wait(2 * at + 1)
            for half in (0, 1):
                attend(half, at, False)

    loop(1, chip + 1, attend_earlier)
    for half in (0, 1):
        att_head[half] = (run_out[half] / run_sum[half]).astype(BF)
        log_total = run_max[half] + jnp.log(run_sum[half])
        lse_col[half] = log_total
        lse_all[chip, half] = jnp.transpose(log_total)[0:8]

    def att_copy():
        return ctx_copy(att_head.at[1 - core], att_pair.at[core], att_s, att_r, other)

    att_copy().start()
    att_pair[core] = att_head[core]

    def lse_copy(at):
        return ctx_copy(
            lse_all.at[chip], lse_all.at[chip], lse_s.at[at], lse_r.at[chip], 2 * at + core
        )

    loop(0, chip, lambda at: lse_copy(at).start())
    ctx_copy(att_head.at[0], att_pair.at[1 - core], att_s, att_r, other).wait_recv()

    both_heads = jnp.concatenate([att_pair[0], att_pair[1]], axis=1)
    out_tile = min(512, wide)

    def out_columns(step):
        here = pl.ds(pl.multiple_of(step * out_tile, out_tile), out_tile)
        product = nn(both_heads, w_out[:, here]).astype(BF)
        glob_part[:, :, here] = product.reshape(npb, patches, out_tile)

    loop(0, wide // out_tile, out_columns)

    groups = 2
    share = patches // groups

    def glob_copy(group, peer):
        here = pl.ds(pl.multiple_of(group * share, share), share)
        return pb_copy(
            glob_part.at[peer, here],
            glob_in.at[part, here],
            glob_s.at[group, peer],
            glob_r.at[group, part],
            peer,
        )

    def glob_wait(group, peer):
        here = pl.ds(pl.multiple_of(group * share, share), share)
        pb_copy(
            glob_part.at[0, here],
            glob_in.at[peer, here],
            glob_s.at[group, peer],
            glob_r.at[group, peer],
            peer,
        ).wait_recv()

    for group in range(groups):
        each_part(lambda peer: glob_copy(group, peer).start())
    glob_in[part] = glob_part[part]

    count = share * PATCH
    byte_wide = wide // PATCH
    local_wide = w_link.shape[1]
    pairs = local_wide // (2 * LHD)
    symbols = lax.broadcasted_iota(jnp.int32, (count, table.shape[0]), 1)
    nothing = jnp.full((share, 1), -1, jnp.int32)
    ids_wide[:, 0:patches] = ids[...]
    for group in range(groups):
        columns = []
        for b in range(PATCH):
            line = jnp.broadcast_to(ids_wide[b : b + 1, :], (HD, HD))
            columns.append(jnp.transpose(line)[group * share : (group + 1) * share, 0:1])
        preceding = jnp.concatenate([nothing] + columns[:-1], axis=0)
        targets_all[group] = jnp.broadcast_to(jnp.concatenate(columns, axis=0), (count, HD))
        hidden[group] = nn((preceding == symbols).astype(BF), table[...]) + jnp.where(
            preceding < 0, pad_embed[...].astype(F32).reshape(1, local_wide), 0.0
        )
    row_index = lax.broadcasted_iota(jnp.int32, (count, count), 0)
    column_index = lax.broadcasted_iota(jnp.int32, (count, count), 1)
    same = jnp.logical_and(
        lax.rem(row_index, share) == lax.rem(column_index, share), column_index <= row_index
    )
    lane = lax.broadcasted_iota(jnp.int32, (count, 2 * LHD), 1)
    halves = (lane < LHD, lane >= LHD)

    def pair_of(block, pair):
        low = block * local_wide + pair * 2 * LHD
        return mixed[:, low : low + 2 * LHD]

    def kept(values, side):
        return jnp.where(halves[side], values, jnp.zeros_like(values))

    def grad_copy(group, peer):
        mine = grad_all.at[core, part, pl.ds(pl.multiple_of(group * share, share), share)]
        return pb_copy(mine, mine, grad_s.at[group, peer], grad_r.at[group, part], peer)

    def grad_wait(group, peer):
        theirs = grad_all.at[core, peer, pl.ds(pl.multiple_of(group * share, share), share)]
        pb_copy(theirs, theirs, grad_s.at[group, peer], grad_r.at[group, peer], peer).wait_recv()

    def local_model(group):
        here = pl.ds(pl.multiple_of(group * share, share), share)
        each_part(lambda peer: glob_wait(group, peer))
        glob = glob_in[0, here, :].astype(F32)
        for index in range(1, npb):
            glob = glob + glob_in[index, here, :].astype(F32)
        glob = glob.astype(BF)
        pieces = jnp.concatenate(
            [glob[:, b * byte_wide : (b + 1) * byte_wide] for b in range(PATCH)], axis=0
        )
        hidden_one = hidden[group] + nn(pieces, w_link[...])
        hidden[group] = hidden_one
        inverse_one = rms_inverse(hidden_one)
        mixed[...] = nn((hidden_one * inverse_one).astype(BF), w_mix[...]).astype(BF)
        heads = 2 * pairs
        for head in range(heads):
            query = kept(pair_of(0, head // 2), head % 2)
            weights[head] = nt(query, pair_of(1, head // 2))
        scores = jnp.where(same[None], weights[...] * LHD ** (-0.5), MASKED)
        exps = jnp.exp(scores - jnp.max(scores, axis=2, keepdims=True))
        weights[...] = exps / jnp.sum(exps, axis=2, keepdims=True)
        local_att = []
        for pair in range(pairs):
            terms = [
                nn(weights[2 * pair + side].astype(BF), kept(pair_of(2, pair), side))
                for side in (0, 1)
            ]
            local_att.append((terms[0] + terms[1]).astype(BF))
        hidden_two = hidden[group] + nn(jnp.concatenate(local_att, axis=1), w_local_out[...])
        inverse_two = rms_inverse(hidden_two)
        logits = nn((hidden_two * inverse_two).astype(BF), w_vocab[...])
        exps = jnp.exp(logits - jnp.max(logits, axis=1, keepdims=True))
        soft = exps / jnp.sum(exps, axis=1, keepdims=True)
        d_logits = (
            soft - jnp.where(targets_all[group, :, 0:1] == symbols, 1.0, 0.0)
        ) * (1.0 / (rows * nctx * PATCH))
        d_normed_two = nt(d_logits.astype(BF), w_vocab[...]).astype(BF).astype(F32)
        d_hidden = rms_back(hidden_two, inverse_two, d_normed_two)
        d_local_att = nt(d_hidden.astype(BF), w_local_out[...]).astype(BF)
        d_heads = [
            kept(d_local_att[:, pair * 2 * LHD : (pair + 1) * 2 * LHD], side)
            for pair in range(pairs)
            for side in (0, 1)
        ]
        for head in range(heads):
            d_weights[head] = nt(d_heads[head], pair_of(2, head // 2))
        d_soft = d_weights[...].astype(BF).astype(F32)
        soft = weights[...]
        dots = jnp.sum(d_soft * soft, axis=2, keepdims=True)
        d_weights[...] = soft * (d_soft - dots) * LHD ** (-0.5)
        for pair in range(pairs):
            terms = [[], [], []]
            for side in (0, 1):
                head = 2 * pair + side
                d_scores = d_weights[head].astype(BF)
                terms[0].append(nn(d_scores, kept(pair_of(1, pair), side)))
                terms[1].append(tn(d_scores, kept(pair_of(0, pair), side)))
                terms[2].append(tn(weights[head].astype(BF), d_heads[head]))
            for block in range(3):
                at = block * local_wide + pair * 2 * LHD
                d_mixed[:, at : at + 2 * LHD] = (terms[block][0] + terms[block][1]).astype(BF)
        d_normed_one = nt(d_mixed[...], w_mix[...]).astype(BF).astype(F32)
        hidden_one = hidden[group]
        d_hidden = d_hidden + rms_back(hidden_one, rms_inverse(hidden_one), d_normed_one)
        d_pieces = nt(d_hidden.astype(BF), w_link[...]).astype(BF)
        for b in range(PATCH):
            grad_all[core, part, here, b * byte_wide : (b + 1) * byte_wide] = d_pieces[
                b * share : (b + 1) * share
            ]
        each_part(lambda peer: grad_copy(group, peer).start())

    each_peer(later_direct, lambda peer: kv_copy(peer).wait_send())

    @pl.when(chip >= 4)
    def _():
        for side in (0, 1):
            kv_forward(side).wait_send()

    each_peer(earlier, lambda peer: q_copy(peer).wait_send())
    loop(0, chip, lambda at: lse_copy(at).wait_send())
    norm_copy(core).wait_send()
    att_copy().wait_send()

    loop(0, groups, local_model)
    def full_copy(group, index):
        here = pl.ds(group * share, share)
        block = grad_all.at[index, :, here]
        return ctx_copy(block, block, full_s.at[group], full_r.at[group], other)

    last = groups - 1

    def da_parts(group, whole):
        return whole.at[0 : npb + 1 if group == last else npb, group * share : (group + 1) * share]

    def da_copy(group, peer):
        return ctx_copy(
            da_parts(group, da_send.at[lax.rem(peer, 2)]),
            da_parts(group, da_all.at[place]),
            da_s.at[group, peer],
            da_r.at[group, place],
            peer,
        )

    def da_wait_part(group, peer):
        ctx_copy(
            da_parts(group, da_send.at[0]),
            da_parts(group, da_all.at[peer]),
            da_s.at[group, peer],
            da_r.at[group, peer],
            peer,
        ).wait_recv()

    def da_wait(peer):
        for group in range(groups):
            da_wait_part(group, peer)

    def da_forward(group, side):
        source = 2 * (chip + 4) + side
        block = da_parts(group, da_all.at[source])
        return ctx_copy(
            block, block, da_forward_s.at[group, side], da_r.at[group, source], neighbour
        )

    for group in range(groups):
        each_part(lambda peer: grad_wait(group, peer))
        full_copy(group, core).start()
        here = slice(group * share, (group + 1) * share)
        grads = grad_all[core, :, here, :].reshape(npb * share, wide)
        product = nt(grads, w_out[...]).astype(BF)
        for head in (0, 1):
            d_att = product[:, head * HD : (head + 1) * HD]
            da_send[head, 0:npb, here, :] = d_att.reshape(npb, share, HD)
        if group == last:
            for head in (0, 1):
                d_att = da_send[head, 0:npb].reshape(rows, HD).astype(F32)
                dots = jnp.sum(d_att * att_pair[head].astype(F32), axis=1, keepdims=True)
                exact = row_form(dots, rows)
                high = exact.astype(BF)
                low = (exact - high.astype(F32)).astype(BF)
                spare = jnp.concatenate([high[0:1], low[0:1]], axis=0)
                tail = [spare[:, at : at + HD] for at in range(0, rows, HD)]
                filler = jnp.zeros((share - 2 * len(tail), HD), BF)
                da_send[head, npb, here, :] = jnp.concatenate(tail + [filler], axis=0)
        da_copy(group, other).start()

        def da_start(peer):
            @pl.when(earlier_direct(lax.div(peer, 2)))
            def _():
                da_copy(group, peer).start()

        loop(0, 2 * chip, da_start)

    def grads_of(device):
        return da_all[device, 0:npb].reshape(rows, HD)

    def dots_of(device):
        tail = da_all[device, npb, last * share : (last + 1) * share].astype(F32)
        pieces = [
            tail[2 * at : 2 * at + 1] + tail[2 * at + 1 : 2 * at + 2] for at in range(rows // HD)
        ]
        return jnp.concatenate(pieces, axis=1)

    da_all[place] = da_send[core]

    block_wide = wide // nctx
    term_rows = min(512, wide)
    owners = term_rows // block_wide

    def wo_copy(peer):
        return ctx_copy(wo_send.at[peer], wo_in.at[place], wo_s.at[peer], wo_r.at[place], peer)

    def wq_copy(peer):
        return ctx_copy(wq_send.at[peer], wq_in.at[place], wq_s.at[peer], wq_r.at[place], peer)

    def wkv_copy(peer):
        return ctx_copy(wkv_send.at[peer], wkv_in.at[place], wkv_s.at[peer], wkv_r.at[place], peer)

    def in_turn(make, copy):
        steps = wide // term_rows

        def one(step):
            block = lax.rem(lax.div(place, owners) + step, steps)
            make(block)
            for index in range(owners):
                peer = block * owners + index

                @pl.when(peer != place)
                def _():
                    copy(peer).start()

        loop(0, steps, one)

    for group in range(groups):
        full_copy(group, 1 - core).wait_recv()
    att_turned = jnp.transpose(att_head[...].reshape(pair_rows, HD).astype(F32)).astype(BF)

    def wo_block(step):
        here = pl.ds(pl.multiple_of(step * term_rows, term_rows), term_rows)
        grads = grad_all[:, :, :, here].reshape(pair_rows, term_rows)
        terms = nn(att_turned, grads).astype(BF)
        for index in range(owners):
            wo_send[step * owners + index] = terms[:, index * block_wide : (index + 1) * block_wide]

    in_turn(wo_block, wo_copy)
    wo_in[place] = wo_send[place]
    da_wait(other)

    dq_acc[...] = jnp.zeros(dq_acc.shape, F32)

    def query_back(half, at, on_diagonal):
        scores = nt(q_all[first + half], keys_of(at)) * scale
        probs = jnp.exp(scores - lse_col[half, :, 0:1])
        if on_diagonal:
            probs = jnp.where(diagonal(half, False), probs, 0.0)
        d_probs = nt(grads_of(first + half), values_of(at))
        d_scores = (probs * (d_probs - run_sum[half, :, 0:1]) * scale).astype(BF)
        dq_acc[half] += nn(d_scores, keys_of(at))

    for half in (0, 1):
        dots = jnp.sum(
            grads_of(first + half).astype(F32) * att_head[half].astype(F32), axis=1, keepdims=True
        )
        run_sum[half] = jnp.broadcast_to(dots, (rows, HD))
    for half in (0, 1):
        query_back(half, chip, True)

    def query_earlier(step):
        for half in (0, 1):
            query_back(half, chip - step, False)

    loop(1, chip + 1, query_earlier)

    dq_ready = (dq_acc[...] * row_scale[...]).reshape(pair_rows, HD).astype(BF)

    def wq_block(step):
        here = pl.ds(pl.multiple_of(step * term_rows, term_rows), term_rows)
        terms = nn(inputs_turned[here, :], dq_ready).astype(BF)
        wq_send[pl.ds(step * owners, owners)] = terms.reshape(owners, block_wide, HD)

    in_turn(wq_block, wq_copy)
    wq_in[place] = wq_send[place]

    dk_acc[...] = jnp.zeros(dk_acc.shape, F32)
    dv_acc[...] = jnp.zeros(dv_acc.shape, F32)

    def key_back(half, at, on_diagonal):
        queries = q_all[pl.ds(2 * at, 2)].reshape(pair_rows, HD)
        grads = da_all[pl.ds(2 * at, 2), 0:npb].reshape(pair_rows, HD)
        log_total = jnp.concatenate([lse_all[at, 0, 0:1, :], lse_all[at, 1, 0:1, :]], axis=1)
        dots = jnp.concatenate([dots_of(2 * at), dots_of(2 * at + 1)], axis=1)
        scores = nt(kv_all[0, first + half], queries) * scale
        probs = jnp.exp(scores - log_total)
        if on_diagonal:
            probs = jnp.where(diagonal(half, True), probs, 0.0)
        d_probs = nt(kv_all[1, first + half], grads)
        d_scores = (probs * (d_probs - dots) * scale).astype(BF)
        dv_acc[half] += nn(probs.astype(BF), grads)
        dk_acc[half] += nn(d_scores, queries)

    for half in (0, 1):
        key_back(half, chip, True)

    def rest_wait(at):
        q_wait(2 * at)
        q_wait(2 * at + 1)
        ctx_copy(
            lse_all.at[at], lse_all.at[at], lse_s.at[at], lse_r.at[at], 2 * at + core
        ).wait_recv()

    @pl.when(chip < chips - 4)
    def _():
        for group in range(groups):
            for side in (0, 1):
                da_wait_part(group, 2 * (chip + 4) + side)
                da_forward(group, side).start()
        rest_wait(chip + 4)
        for half in (0, 1):
            key_back(half, chip + 4, False)

    def key_later(at):
        @pl.when(at != chip + 4)
        def _():
            da_wait(2 * at)
            da_wait(2 * at + 1)
            rest_wait(at)
            for half in (0, 1):
                key_back(half, at, False)

    loop(chip + 1, chips, key_later)
    dkv_ready = jnp.concatenate(
        [
            (total[...] * row_scale[...]).reshape(pair_rows, HD).astype(BF)
            for total in (dk_acc, dv_acc)
        ],
        axis=1,
    )

    def wkv_block(step):
        here = pl.ds(pl.multiple_of(step * term_rows, term_rows), term_rows)
        terms = nn(inputs_turned[here, :], dkv_ready).astype(BF)
        wkv_send[pl.ds(step * owners, owners)] = terms.reshape(owners, block_wide, 2 * HD)

    in_turn(wkv_block, wkv_copy)
    wkv_in[place] = wkv_send[place]

    def sent_part(peer):
        for group in range(groups):
            glob_copy(group, peer).wait_send()
            grad_copy(group, peer).wait_send()

    each_part(sent_part)

    def sent_earlier(peer):
        for group in range(groups):
            da_copy(group, peer).wait_send()

    each_peer(earlier_direct, sent_earlier)

    @pl.when(chip < chips - 4)
    def _():
        for side in (0, 1):
            for group in range(groups):
                da_forward(group, side).wait_send()

    for group in range(groups):
        full_copy(group, core).wait_send()

    def sent_all(peer):
        wo_copy(peer).wait_send()
        wq_copy(peer).wait_send()
        wkv_copy(peer).wait_send()

    def total_of(pick, head):
        total = pick(head).astype(F32)
        for index in range(1, chips):
            total = total + pick(2 * index + head).astype(F32)
        return total.astype(BF)

    def wo_wait(peer):
        ctx_copy(wo_send.at[0], wo_in.at[peer], wo_s.at[peer], wo_r.at[peer], peer).wait_recv()

    def wq_wait(peer):
        ctx_copy(wq_send.at[0], wq_in.at[peer], wq_s.at[peer], wq_r.at[peer], peer).wait_recv()

    def wkv_wait(peer):
        ctx_copy(wkv_send.at[0], wkv_in.at[peer], wkv_s.at[peer], wkv_r.at[peer], peer).wait_recv()

    each_peer(anyone, wo_wait)
    for head in (0, 1):
        wide_sums[head * HD : (head + 1) * HD, :] = total_of(lambda index: wo_in[index], head)
    each_peer(anyone, wq_wait)
    for head in (0, 1):
        at = head * HD
        tall_sums[0, :, at : at + HD] = total_of(lambda index: wq_in[index], head)
    each_peer(anyone, sent_all)
    each_peer(anyone, wkv_wait)
    for head in (0, 1):
        at = head * HD
        total = total_of(lambda index: wkv_in[index], head)
        tall_sums[1, :, at : at + HD] = total[:, :HD]
        tall_sums[2, :, at : at + HD] = total[:, HD:]


def split_kernel(tall_sums, wide_sums, grad_query, grad_key, grad_value, grad_out):
    grad_query[...] = tall_sums[0]
    grad_key[...] = tall_sums[1]
    grad_value[...] = tall_sums[2]
    grad_out[...] = wide_sums[...]


def per_device(nctx, npb, *args):
    embed, w_query, w_key, w_value, w_out, ids, pad_embed, table, w_link, w_mix, w_lo, w_vocab = args
    rows, wide = embed.shape
    patches = rows // npb
    groups = 2
    local_rows = patches // groups * PATCH
    local_wide = w_link.shape[1]
    chips = nctx // 2
    block = wide // nctx
    vmem = pltpu.VMEM
    dma = pltpu.SemaphoreType.DMA
    near = [w_query, w_key, w_value, w_out, table, w_link, w_mix, w_lo, w_vocab]
    scratch = [vmem(array.shape, BF) for array in near]
    scratch += [
        dma((len(near) + 2,)),
        vmem((2, rows, wide), BF),
        vmem((2, rows, HD), F32),
        vmem((wide, 2 * rows), BF),
        vmem((2, 2, rows, HD), BF),
        vmem((2, nctx, rows, HD), BF),
        vmem((2, rows, HD), BF),
        vmem((nctx, rows, HD), BF),
        vmem((2, rows, HD), F32),
        vmem((2, rows, HD), F32),
        vmem((2, rows, HD), F32),
        vmem((2, rows, HD), BF),
        vmem((2, rows, HD), BF),
        vmem((2, rows, HD), F32),
        vmem((chips, 2, 8, rows), F32),
        vmem((npb, patches, wide), BF),
        vmem((npb, patches, wide), BF),
        vmem((groups, local_rows, local_wide), F32),
        vmem((local_rows, 3 * local_wide), BF),
        vmem((local_wide // LHD, local_rows, local_rows), F32),
        vmem((local_wide // LHD, local_rows, local_rows), F32),
        vmem((local_rows, 3 * local_wide), BF),
        vmem((PATCH, HD), jnp.int32),
        vmem((groups, local_rows, HD), jnp.int32),
        vmem((2, npb, patches, wide), BF),
        vmem((2, npb + 1, patches, HD), BF),
        vmem((nctx, npb + 1, patches, HD), BF),
        vmem((2, rows, HD), F32),
        vmem((2, rows, HD), F32),
        vmem((2, rows, HD), F32),
        vmem((nctx, HD, block), BF),
        vmem((nctx, block, HD), BF),
        vmem((nctx, block, 2 * HD), BF),
        vmem((nctx, HD, block), BF),
        vmem((nctx, block, HD), BF),
        vmem((nctx, block, 2 * HD), BF),
    ]
    scratch += [dma((nctx,))] * 10
    scratch += [dma((chips,))] * 2
    scratch += [dma((groups, npb))] * 4
    scratch += [dma] * 4 + [dma((groups,))] * 2 + [dma((groups, nctx))] * 2
    scratch += [dma((2,)), dma((groups, 2))]
    whole = pl.BlockSpec(memory_space=pltpu.VMEM)
    far = pl.BlockSpec(memory_space=pl.ANY)
    tall = jax.ShapeDtypeStruct((block, 2 * HD), BF)
    sums = pl.pallas_call(
        functools.partial(step_kernel, (nctx, npb)),
        out_shape=(
            jax.ShapeDtypeStruct((3, block, 2 * HD), BF),
            jax.ShapeDtypeStruct((2 * HD, block), BF),
        ),
        in_specs=[far] * 5 + [whole] * 2 + [far] * 5,
        out_specs=(whole,) * 2,
        scratch_shapes=scratch,
        compiler_params=pltpu.CompilerParams(
            collective_id=0, has_side_effects=True, vmem_limit_bytes=56 * 1024 * 1024
        ),
        name="step",
    )(
        embed, w_query, w_key, w_value, w_out, ids.T, pad_embed, table, w_link, w_mix,
        w_lo, w_vocab,
    )
    return pl.pallas_call(
        split_kernel,
        out_shape=(tall, tall, tall, jax.ShapeDtypeStruct((2 * HD, block), BF)),
        in_specs=[whole] * 2,
        out_specs=(whole,) * 4,
        name="split",
    )(*sums)


def solution(mesh):
    in_specs = (
        P("ctx", None),
        P(None, "pb"),
        P(None, "pb"),
        P(None, "pb"),
        P("pb", None),
        P(("ctx", "pb"), None),
        P(),
        P(),
        P(),
        P(),
        P(),
        P(),
    )
    out_specs = (P("ctx", "pb"), P("ctx", "pb"), P("ctx", "pb"), P("pb", "ctx"))
    return jax.shard_map(
        functools.partial(per_device, mesh.shape["ctx"], mesh.shape["pb"]),
        mesh=mesh,
        in_specs=in_specs,
        out_specs=out_specs,
        check_vma=False,
    )
```

```python
import functools

import jax
import jax.numpy as jnp
from jax import lax
from jax.experimental import pallas as pl
from jax.experimental.pallas import tpu as pltpu
from jax.sharding import PartitionSpec as P

HD = 128
LHD = 64
PATCH = 8
EPSILON = 1e-06
MASKED = -1e30
MESH = pl.DeviceIdType.MESH
BF = jnp.bfloat16
F32 = jnp.float32


def nn(left, right):
    return lax.dot_general(left, right, (((1,), (0,)), ((), ())), preferred_element_type=F32)


def nt(left, right):
    return lax.dot_general(left, right, (((1,), (1,)), ((), ())), preferred_element_type=F32)


def tn(left, right):
    return lax.dot_general(left, right, (((0,), (0,)), ((), ())), preferred_element_type=F32)


def loop(low, high, body):
    def step(index, unused):
        body(index)
        return unused

    lax.fori_loop(low, high, step, 0)


def row_form(column, rows):
    return jnp.transpose(jnp.broadcast_to(column, (rows, HD)))[0:8]


def rms_inverse(values):
    return lax.rsqrt(jnp.mean(values * values, axis=1, keepdims=True) + EPSILON)


def rms_back(values, inverse, grad):
    width = values.shape[1]
    dots = jnp.sum(grad * values, axis=1, keepdims=True)
    return inverse * grad - values * (inverse * inverse * inverse * dots * (1.0 / width))


def step_kernel(
    sizes,
    embed_far,
    w_query_far,
    w_key_far,
    w_value_far,
    w_out_far,
    ids,
    pad_embed,
    table_far,
    w_link_far,
    w_mix_far,
    w_local_out_far,
    w_vocab_far,
    tall_sums,
    wide_sums,
    w_query,
    w_key,
    w_value,
    w_out,
    table,
    w_link,
    w_mix,
    w_local_out,
    w_vocab,
    load_s,
    inputs,
    row_scale,
    inputs_turned,
    kv_send,
    kv_all,
    q_send,
    q_all,
    run_max,
    run_sum,
    run_out,
    att_head,
    att_pair,
    lse_col,
    lse_all,
    glob_part,
    glob_in,
    hidden,
    mixed,
    weights,
    d_weights,
    d_mixed,
    ids_wide,
    targets_all,
    grad_all,
    da_send,
    da_all,
    dq_acc,
    dk_acc,
    dv_acc,
    wo_send,
    wq_send,
    wkv_send,
    wo_in,
    wq_in,
    wkv_in,
    kv_s,
    kv_r,
    q_s,
    q_r,
    wo_s,
    wo_r,
    wq_s,
    wq_r,
    wkv_s,
    wkv_r,
    lse_s,
    lse_r,
    glob_s,
    glob_r,
    grad_s,
    grad_r,
    norm_s,
    norm_r,
    att_s,
    att_r,
    full_s,
    full_r,
    da_s,
    da_r,
    kv_forward_s,
    da_forward_s,
):
    nctx, npb = sizes
    chips = nctx // 2
    rows, wide = embed_far.shape
    patches = rows // npb
    bytes_here = patches * PATCH
    scale = HD ** (-0.5)
    place = lax.axis_index("ctx")
    part = lax.axis_index("pb")
    chip = lax.div(place, 2)
    core = lax.rem(place, 2)
    other = place + 1 - 2 * core

    def ctx_copy(src, dst, send, recv, peer):
        return pltpu.make_async_remote_copy(
            src_ref=src,
            dst_ref=dst,
            send_sem=send,
            recv_sem=recv,
            device_id=(peer, part),
            device_id_type=MESH,
        )

    def pb_copy(src, dst, send, recv, peer):
        return pltpu.make_async_remote_copy(
            src_ref=src,
            dst_ref=dst,
            send_sem=send,
            recv_sem=recv,
            device_id=(place, peer),
            device_id_type=MESH,
        )

    def each_peer(wanted, action):
        def one(step):
            peer = lax.rem(place + nctx - step, nctx)

            @pl.when(wanted(lax.div(peer, 2)))
            def _():
                action(peer)

        loop(1, nctx, one)

    def each_part(action):
        loop(1, npb, lambda step: action(lax.rem(part + step, npb)))

    half_rows = rows // 2
    pairs_in = (
        (embed_far.at[0:half_rows], inputs.at[core, 0:half_rows]),
        (embed_far.at[half_rows:rows], inputs.at[core, half_rows:rows]),
        (w_key_far, w_key),
        (w_value_far, w_value),
        (w_query_far, w_query),
        (w_out_far, w_out),
        (table_far, table),
        (w_link_far, w_link),
        (w_mix_far, w_mix),
        (w_local_out_far, w_local_out),
        (w_vocab_far, w_vocab),
    )
    loads = [
        pltpu.make_async_copy(far, near, load_s.at[index])
        for index, (far, near) in enumerate(pairs_in)
    ]
    for load in loads[:4]:
        load.start()

    later = lambda at: at >= chip
    earlier = lambda at: at <= chip
    anyone = lambda at: at >= 0

    def crossing(at, rows_away):
        return jnp.logical_and(lax.div(at, 2) - lax.div(chip, 2) == rows_away, lax.rem(at, 2) != lax.rem(chip, 2))

    later_direct = lambda at: jnp.logical_and(later(at), jnp.logical_not(crossing(at, 2)))
    earlier_direct = lambda at: jnp.logical_and(earlier(at), jnp.logical_not(crossing(at, -2)))
    neighbour = 2 * (chip + 1 - 2 * lax.rem(chip, 2)) + core

    barrier = pltpu.get_barrier_semaphore()

    def greet_ctx(peer):
        pl.semaphore_signal(barrier, inc=1, device_id=(peer, part), device_id_type=MESH)

    def greet_part(peer):
        pl.semaphore_signal(barrier, inc=1, device_id=(place, peer), device_id_type=MESH)

    each_peer(anyone, greet_ctx)
    each_part(greet_part)

    tile_rows = min(32, rows)

    def scale_rows(index):
        for low in range(0, rows, tile_rows):
            values = inputs[index, low : low + tile_rows, :].astype(F32)
            row_scale[index, low : low + tile_rows] = jnp.broadcast_to(
                rms_inverse(values), (tile_rows, HD)
            )

    loads[0].wait()
    loads[1].wait()
    loads[4].start()
    scale_rows(core)
    own_inputs = inputs[core]

    def scaled(product):
        return (product * row_scale[core, :, 0:1]).astype(BF)

    for slot, weight in ((0, w_key), (1, w_value)):
        loads[2 + slot].wait()
        product = scaled(nn(own_inputs, weight[...]))
        kv_send[0, slot] = product[:, :HD]
        kv_send[1, slot] = product[:, HD:]
    pl.semaphore_wait(barrier, nctx + npb - 2)

    def kv_copy(peer):
        return ctx_copy(
            kv_send.at[lax.rem(peer, 2)], kv_all.at[:, place], kv_s.at[peer], kv_r.at[place], peer
        )

    def kv_start(step):
        peer = lax.rem(place + step, nctx)
        at = lax.div(peer, 2)

        @pl.when(jnp.logical_and(later_direct(at), at != chip + 4))
        def _():
            kv_copy(peer).start()

    @pl.when(chip < chips - 4)
    def _():
        for side in (0, 1):
            kv_copy(2 * (chip + 4) + side).start()

    loop(1, nctx, kv_start)
    for load in loads[5:]:
        load.start()
    kv_all[:, place] = kv_send[core]
    loads[4].wait()
    product = scaled(nn(own_inputs, w_query[...]))
    q_send[0] = product[:, :HD]
    q_send[1] = product[:, HD:]

    def q_copy(peer):
        return ctx_copy(q_send.at[lax.rem(peer, 2)], q_all.at[place], q_s.at[peer], q_r.at[place], peer)

    q_copy(other).start()
    q_all[place] = q_send[core]

    def norm_copy(index):
        return ctx_copy(inputs.at[index], inputs.at[index], norm_s, norm_r, other)

    norm_copy(core).start()
    strictly_earlier = lambda at: at < chip
    each_peer(strictly_earlier, lambda peer: q_copy(peer).start())

    def kv_wait(peer):
        ctx_copy(kv_send.at[0], kv_all.at[:, peer], kv_s.at[peer], kv_r.at[peer], peer).wait_recv()

    def q_wait(peer):
        ctx_copy(q_send.at[0], q_all.at[peer], q_s.at[peer], q_r.at[peer], peer).wait_recv()

    first = 2 * chip
    pair_rows = 2 * rows

    def keys_of(at):
        return kv_all[0, pl.ds(2 * at, 2)].reshape(pair_rows, HD)

    def values_of(at):
        return kv_all[1, pl.ds(2 * at, 2)].reshape(pair_rows, HD)

    def diagonal(half, keys_down):
        shape = (rows, pair_rows)
        here = lax.broadcasted_iota(jnp.int32, shape, 0) + half * rows
        there = lax.broadcasted_iota(jnp.int32, shape, 1)
        return (there >= here) if keys_down else (there <= here)

    run_max[...] = jnp.full(run_max.shape, MASKED, F32)
    run_sum[...] = jnp.zeros(run_sum.shape, F32)
    run_out[...] = jnp.zeros(run_out.shape, F32)

    def attend(half, at, on_diagonal):
        scores = nt(q_all[first + half], keys_of(at)) * scale
        if on_diagonal:
            scores = jnp.where(diagonal(half, False), scores, MASKED)
        before = run_max[half, :, 0:1]
        highest = jnp.maximum(before, jnp.max(scores, axis=1, keepdims=True))
        exps = jnp.exp(scores - highest)
        factor = jnp.exp(before - highest)
        total = run_sum[half, :, 0:1] * factor + jnp.sum(exps, axis=1, keepdims=True)
        run_out[half] = run_out[half] * factor + nn(exps.astype(BF), values_of(at))
        run_max[half] = jnp.broadcast_to(highest, (rows, HD))
        run_sum[half] = jnp.broadcast_to(total, (rows, HD))

    kv_wait(other)
    q_wait(other)
    for half in (0, 1):
        attend(half, chip, True)
    norm_copy(1 - core).wait_recv()
    scale_rows(1 - core)
    turn_tile = min(128, wide)

    def turn_columns(step):
        here = pl.ds(pl.multiple_of(step * turn_tile, turn_tile), turn_tile)
        block = inputs[:, :, here].reshape(pair_rows, turn_tile)
        inputs_turned[here, :] = jnp.transpose(block.astype(F32)).astype(BF)

    loop(0, wide // turn_tile, turn_columns)
    for load in loads[5:]:
        load.wait()

    def kv_forward(side):
        source = 2 * (chip - 4) + side
        block = kv_all.at[:, source]
        return ctx_copy(block, block, kv_forward_s.at[side], kv_r.at[source], neighbour)

    @pl.when(chip >= 4)
    def _():
        for side in (0, 1):
            kv_wait(2 * (chip - 4) + side)
            kv_forward(side).start()
        for half in (0, 1):
            attend(half, chip - 4, False)

    def attend_earlier(step):
        at = chip - step

        @pl.when(step != 4)
        def _():
            kv_wait(2 * at)
            kv_wait(2 * at + 1)
            for half in (0, 1):
                attend(half, at, False)

    loop(1, chip + 1, attend_earlier)
    for half in (0, 1):
        att_head[half] = (run_out[half] / run_sum[half]).astype(BF)
        log_total = run_max[half] + jnp.log(run_sum[half])
        lse_col[half] = log_total
        lse_all[chip, half] = jnp.transpose(log_total)[0:8]

    def att_copy():
        return ctx_copy(att_head.at[1 - core], att_pair.at[core], att_s, att_r, other)

    att_copy().start()
    att_pair[core] = att_head[core]

    def lse_copy(at):
        return ctx_copy(
            lse_all.at[chip], lse_all.at[chip], lse_s.at[at], lse_r.at[chip], 2 * at + core
        )

    loop(0, chip, lambda at: lse_copy(at).start())
    ctx_copy(att_head.at[0], att_pair.at[1 - core], att_s, att_r, other).wait_recv()

    both_heads = jnp.concatenate([att_pair[0], att_pair[1]], axis=1)
    out_tile = min(512, wide)

    def out_columns(step):
        here = pl.ds(pl.multiple_of(step * out_tile, out_tile), out_tile)
        product = nn(both_heads, w_out[:, here]).astype(BF)
        glob_part[:, :, here] = product.reshape(npb, patches, out_tile)

    loop(0, wide // out_tile, out_columns)

    groups = 2
    share = patches // groups

    def glob_copy(group, peer):
        here = pl.ds(pl.multiple_of(group * share, share), share)
        return pb_copy(
            glob_part.at[peer, here],
            glob_in.at[part, here],
            glob_s.at[group, peer],
            glob_r.at[group, part],
            peer,
        )

    def glob_wait(group, peer):
        here = pl.ds(pl.multiple_of(group * share, share), share)
        pb_copy(
            glob_part.at[0, here],
            glob_in.at[peer, here],
            glob_s.at[group, peer],
            glob_r.at[group, peer],
            peer,
        ).wait_recv()

    for group in range(groups):
        each_part(lambda peer: glob_copy(group, peer).start())
    glob_in[part] = glob_part[part]

    count = share * PATCH
    byte_wide = wide // PATCH
    local_wide = w_link.shape[1]
    pairs = local_wide // (2 * LHD)
    symbols = lax.broadcasted_iota(jnp.int32, (count, table.shape[0]), 1)
    nothing = jnp.full((share, 1), -1, jnp.int32)
    ids_wide[:, 0:patches] = ids[...]
    for group in range(groups):
        columns = []
        for b in range(PATCH):
            line = jnp.broadcast_to(ids_wide[b : b + 1, :], (HD, HD))
            columns.append(jnp.transpose(line)[group * share : (group + 1) * share, 0:1])
        preceding = jnp.concatenate([nothing] + columns[:-1], axis=0)
        targets_all[group] = jnp.broadcast_to(jnp.concatenate(columns, axis=0), (count, HD))
        hidden[group] = nn((preceding == symbols).astype(BF), table[...]) + jnp.where(
            preceding < 0, pad_embed[...].astype(F32).reshape(1, local_wide), 0.0
        )
    row_index = lax.broadcasted_iota(jnp.int32, (count, count), 0)
    column_index = lax.broadcasted_iota(jnp.int32, (count, count), 1)
    same = jnp.logical_and(
        lax.rem(row_index, share) == lax.rem(column_index, share), column_index <= row_index
    )
    lane = lax.broadcasted_iota(jnp.int32, (count, 2 * LHD), 1)
    halves = (lane < LHD, lane >= LHD)

    def pair_of(block, pair):
        low = block * local_wide + pair * 2 * LHD
        return mixed[:, low : low + 2 * LHD]

    def kept(values, side):
        return jnp.where(halves[side], values, jnp.zeros_like(values))

    def grad_copy(group, peer):
        mine = grad_all.at[core, part, pl.ds(pl.multiple_of(group * share, share), share)]
        return pb_copy(mine, mine, grad_s.at[group, peer], grad_r.at[group, part], peer)

    def grad_wait(group, peer):
        theirs = grad_all.at[core, peer, pl.ds(pl.multiple_of(group * share, share), share)]
        pb_copy(theirs, theirs, grad_s.at[group, peer], grad_r.at[group, peer], peer).wait_recv()

    def local_model(group):
        here = pl.ds(pl.multiple_of(group * share, share), share)
        each_part(lambda peer: glob_wait(group, peer))
        glob = glob_in[0, here, :].astype(F32)
        for index in range(1, npb):
            glob = glob + glob_in[index, here, :].astype(F32)
        glob = glob.astype(BF)
        pieces = jnp.concatenate(
            [glob[:, b * byte_wide : (b + 1) * byte_wide] for b in range(PATCH)], axis=0
        )
        hidden_one = hidden[group] + nn(pieces, w_link[...])
        hidden[group] = hidden_one
        inverse_one = rms_inverse(hidden_one)
        mixed[...] = nn((hidden_one * inverse_one).astype(BF), w_mix[...]).astype(BF)
        heads = 2 * pairs
        for head in range(heads):
            query = kept(pair_of(0, head // 2), head % 2)
            weights[head] = nt(query, pair_of(1, head // 2))
        scores = jnp.where(same[None], weights[...] * LHD ** (-0.5), MASKED)
        exps = jnp.exp(scores - jnp.max(scores, axis=2, keepdims=True))
        weights[...] = exps / jnp.sum(exps, axis=2, keepdims=True)
        local_att = []
        for pair in range(pairs):
            terms = [
                nn(weights[2 * pair + side].astype(BF), kept(pair_of(2, pair), side))
                for side in (0, 1)
            ]
            local_att.append((terms[0] + terms[1]).astype(BF))
        hidden_two = hidden[group] + nn(jnp.concatenate(local_att, axis=1), w_local_out[...])
        inverse_two = rms_inverse(hidden_two)
        logits = nn((hidden_two * inverse_two).astype(BF), w_vocab[...])
        exps = jnp.exp(logits - jnp.max(logits, axis=1, keepdims=True))
        soft = exps / jnp.sum(exps, axis=1, keepdims=True)
        d_logits = (
            soft - jnp.where(targets_all[group, :, 0:1] == symbols, 1.0, 0.0)
        ) * (1.0 / (rows * nctx * PATCH))
        d_normed_two = nt(d_logits.astype(BF), w_vocab[...]).astype(BF).astype(F32)
        d_hidden = rms_back(hidden_two, inverse_two, d_normed_two)
        d_local_att = nt(d_hidden.astype(BF), w_local_out[...]).astype(BF)
        d_heads = [
            kept(d_local_att[:, pair * 2 * LHD : (pair + 1) * 2 * LHD], side)
            for pair in range(pairs)
            for side in (0, 1)
        ]
        for head in range(heads):
            d_weights[head] = nt(d_heads[head], pair_of(2, head // 2))
        d_soft = d_weights[...].astype(BF).astype(F32)
        soft = weights[...]
        dots = jnp.sum(d_soft * soft, axis=2, keepdims=True)
        d_weights[...] = soft * (d_soft - dots) * LHD ** (-0.5)
        for pair in range(pairs):
            terms = [[], [], []]
            for side in (0, 1):
                head = 2 * pair + side
                d_scores = d_weights[head].astype(BF)
                terms[0].append(nn(d_scores, kept(pair_of(1, pair), side)))
                terms[1].append(tn(d_scores, kept(pair_of(0, pair), side)))
                terms[2].append(tn(weights[head].astype(BF), d_heads[head]))
            for block in range(3):
                at = block * local_wide + pair * 2 * LHD
                d_mixed[:, at : at + 2 * LHD] = (terms[block][0] + terms[block][1]).astype(BF)
        d_normed_one = nt(d_mixed[...], w_mix[...]).astype(BF).astype(F32)
        hidden_one = hidden[group]
        d_hidden = d_hidden + rms_back(hidden_one, rms_inverse(hidden_one), d_normed_one)
        d_pieces = nt(d_hidden.astype(BF), w_link[...]).astype(BF)
        for b in range(PATCH):
            grad_all[core, part, here, b * byte_wide : (b + 1) * byte_wide] = d_pieces[
                b * share : (b + 1) * share
            ]
        each_part(lambda peer: grad_copy(group, peer).start())

    each_peer(later_direct, lambda peer: kv_copy(peer).wait_send())

    @pl.when(chip >= 4)
    def _():
        for side in (0, 1):
            kv_forward(side).wait_send()

    each_peer(earlier, lambda peer: q_copy(peer).wait_send())
    loop(0, chip, lambda at: lse_copy(at).wait_send())
    norm_copy(core).wait_send()
    att_copy().wait_send()

    loop(0, groups, local_model)
    def full_copy(group, index):
        here = pl.ds(group * share, share)
        block = grad_all.at[index, :, here]
        return ctx_copy(block, block, full_s.at[group], full_r.at[group], other)

    last = groups - 1

    def da_parts(group, whole):
        return whole.at[0 : npb + 1 if group == last else npb, group * share : (group + 1) * share]

    def da_copy(group, peer):
        return ctx_copy(
            da_parts(group, da_send.at[lax.rem(peer, 2)]),
            da_parts(group, da_all.at[place]),
            da_s.at[group, peer],
            da_r.at[group, place],
            peer,
        )

    def da_wait_part(group, peer):
        ctx_copy(
            da_parts(group, da_send.at[0]),
            da_parts(group, da_all.at[peer]),
            da_s.at[group, peer],
            da_r.at[group, peer],
            peer,
        ).wait_recv()

    def da_wait(peer):
        for group in range(groups):
            da_wait_part(group, peer)

    def da_forward(group, side):
        source = 2 * (chip + 4) + side
        block = da_parts(group, da_all.at[source])
        return ctx_copy(
            block, block, da_forward_s.at[group, side], da_r.at[group, source], neighbour
        )

    for group in range(groups):
        each_part(lambda peer: grad_wait(group, peer))
        full_copy(group, core).start()
        here = slice(group * share, (group + 1) * share)
        grads = grad_all[core, :, here, :].reshape(npb * share, wide)
        product = nt(grads, w_out[...]).astype(BF)
        for head in (0, 1):
            d_att = product[:, head * HD : (head + 1) * HD]
            da_send[head, 0:npb, here, :] = d_att.reshape(npb, share, HD)
        if group == last:
            for head in (0, 1):
                d_att = da_send[head, 0:npb].reshape(rows, HD).astype(F32)
                dots = jnp.sum(d_att * att_pair[head].astype(F32), axis=1, keepdims=True)
                exact = row_form(dots, rows)
                high = exact.astype(BF)
                low = (exact - high.astype(F32)).astype(BF)
                spare = jnp.concatenate([high[0:1], low[0:1]], axis=0)
                tail = [spare[:, at : at + HD] for at in range(0, rows, HD)]
                filler = jnp.zeros((share - 2 * len(tail), HD), BF)
                da_send[head, npb, here, :] = jnp.concatenate(tail + [filler], axis=0)
        da_copy(group, other).start()

        def da_start(peer):
            @pl.when(earlier_direct(lax.div(peer, 2)))
            def _():
                da_copy(group, peer).start()

        loop(0, 2 * chip, da_start)

    def grads_of(device):
        return da_all[device, 0:npb].reshape(rows, HD)

    def dots_of(device):
        tail = da_all[device, npb, last * share : (last + 1) * share].astype(F32)
        pieces = [
            tail[2 * at : 2 * at + 1] + tail[2 * at + 1 : 2 * at + 2] for at in range(rows // HD)
        ]
        return jnp.concatenate(pieces, axis=1)

    da_all[place] = da_send[core]

    block_wide = wide // nctx
    term_rows = min(512, wide)
    owners = term_rows // block_wide

    def wo_copy(peer):
        return ctx_copy(wo_send.at[peer], wo_in.at[place], wo_s.at[peer], wo_r.at[place], peer)

    def wq_copy(peer):
        return ctx_copy(wq_send.at[peer], wq_in.at[place], wq_s.at[peer], wq_r.at[place], peer)

    def wkv_copy(peer):
        return ctx_copy(wkv_send.at[peer], wkv_in.at[place], wkv_s.at[peer], wkv_r.at[place], peer)

    def in_turn(make, copy):
        steps = wide // term_rows

        def one(step):
            block = lax.rem(lax.div(place, owners) + step, steps)
            make(block)
            for index in range(owners):
                peer = block * owners + index

                @pl.when(peer != place)
                def _():
                    copy(peer).start()

        loop(0, steps, one)

    for group in range(groups):
        full_copy(group, 1 - core).wait_recv()
    att_turned = jnp.transpose(att_head[...].reshape(pair_rows, HD).astype(F32)).astype(BF)

    def wo_block(step):
        here = pl.ds(pl.multiple_of(step * term_rows, term_rows), term_rows)
        grads = grad_all[:, :, :, here].reshape(pair_rows, term_rows)
        terms = nn(att_turned, grads).astype(BF)
        for index in range(owners):
            wo_send[step * owners + index] = terms[:, index * block_wide : (index + 1) * block_wide]

    in_turn(wo_block, wo_copy)
    wo_in[place] = wo_send[place]
    da_wait(other)

    dq_acc[...] = jnp.zeros(dq_acc.shape, F32)

    def query_back(half, at, on_diagonal):
        scores = nt(q_all[first + half], keys_of(at)) * scale
        probs = jnp.exp(scores - lse_col[half, :, 0:1])
        if on_diagonal:
            probs = jnp.where(diagonal(half, False), probs, 0.0)
        d_probs = nt(grads_of(first + half), values_of(at))
        d_scores = (probs * (d_probs - run_sum[half, :, 0:1]) * scale).astype(BF)
        dq_acc[half] += nn(d_scores, keys_of(at))

    for half in (0, 1):
        dots = jnp.sum(
            grads_of(first + half).astype(F32) * att_head[half].astype(F32), axis=1, keepdims=True
        )
        run_sum[half] = jnp.broadcast_to(dots, (rows, HD))
    for half in (0, 1):
        query_back(half, chip, True)

    def query_earlier(step):
        for half in (0, 1):
            query_back(half, chip - step, False)

    loop(1, chip + 1, query_earlier)

    dq_ready = (dq_acc[...] * row_scale[...]).reshape(pair_rows, HD).astype(BF)

    def wq_block(step):
        here = pl.ds(pl.multiple_of(step * term_rows, term_rows), term_rows)
        terms = nn(inputs_turned[here, :], dq_ready).astype(BF)
        wq_send[pl.ds(step * owners, owners)] = terms.reshape(owners, block_wide, HD)

    in_turn(wq_block, wq_copy)
    wq_in[place] = wq_send[place]

    dk_acc[...] = jnp.zeros(dk_acc.shape, F32)
    dv_acc[...] = jnp.zeros(dv_acc.shape, F32)

    def key_back(half, at, on_diagonal):
        queries = q_all[pl.ds(2 * at, 2)].reshape(pair_rows, HD)
        grads = da_all[pl.ds(2 * at, 2), 0:npb].reshape(pair_rows, HD)
        log_total = jnp.concatenate([lse_all[at, 0, 0:1, :], lse_all[at, 1, 0:1, :]], axis=1)
        dots = jnp.concatenate([dots_of(2 * at), dots_of(2 * at + 1)], axis=1)
        scores = nt(kv_all[0, first + half], queries) * scale
        probs = jnp.exp(scores - log_total)
        if on_diagonal:
            probs = jnp.where(diagonal(half, True), probs, 0.0)
        d_probs = nt(kv_all[1, first + half], grads)
        d_scores = (probs * (d_probs - dots) * scale).astype(BF)
        dv_acc[half] += nn(probs.astype(BF), grads)
        dk_acc[half] += nn(d_scores, queries)

    for half in (0, 1):
        key_back(half, chip, True)

    def rest_wait(at):
        q_wait(2 * at)
        q_wait(2 * at + 1)
        ctx_copy(
            lse_all.at[at], lse_all.at[at], lse_s.at[at], lse_r.at[at], 2 * at + core
        ).wait_recv()

    @pl.when(chip < chips - 4)
    def _():
        for group in range(groups):
            for side in (0, 1):
                da_wait_part(group, 2 * (chip + 4) + side)
                da_forward(group, side).start()
        rest_wait(chip + 4)
        for half in (0, 1):
            key_back(half, chip + 4, False)

    def key_later(at):
        @pl.when(at != chip + 4)
        def _():
            da_wait(2 * at)
            da_wait(2 * at + 1)
            rest_wait(at)
            for half in (0, 1):
                key_back(half, at, False)

    loop(chip + 1, chips, key_later)
    dkv_ready = jnp.concatenate(
        [
            (total[...] * row_scale[...]).reshape(pair_rows, HD).astype(BF)
            for total in (dk_acc, dv_acc)
        ],
        axis=1,
    )

    def wkv_block(step):
        here = pl.ds(pl.multiple_of(step * term_rows, term_rows), term_rows)
        terms = nn(inputs_turned[here, :], dkv_ready).astype(BF)
        wkv_send[pl.ds(step * owners, owners)] = terms.reshape(owners, block_wide, 2 * HD)

    in_turn(wkv_block, wkv_copy)
    wkv_in[place] = wkv_send[place]

    def sent_part(peer):
        for group in range(groups):
            glob_copy(group, peer).wait_send()
            grad_copy(group, peer).wait_send()

    each_part(sent_part)

    def sent_earlier(peer):
        for group in range(groups):
            da_copy(group, peer).wait_send()

    each_peer(earlier_direct, sent_earlier)

    @pl.when(chip < chips - 4)
    def _():
        for side in (0, 1):
            for group in range(groups):
                da_forward(group, side).wait_send()

    for group in range(groups):
        full_copy(group, core).wait_send()

    def sent_all(peer):
        wo_copy(peer).wait_send()
        wq_copy(peer).wait_send()
        wkv_copy(peer).wait_send()

    def total_of(pick, head):
        total = pick(head).astype(F32)
        for index in range(1, chips):
            total = total + pick(2 * index + head).astype(F32)
        return total.astype(BF)

    def wo_wait(peer):
        ctx_copy(wo_send.at[0], wo_in.at[peer], wo_s.at[peer], wo_r.at[peer], peer).wait_recv()

    def wq_wait(peer):
        ctx_copy(wq_send.at[0], wq_in.at[peer], wq_s.at[peer], wq_r.at[peer], peer).wait_recv()

    def wkv_wait(peer):
        ctx_copy(wkv_send.at[0], wkv_in.at[peer], wkv_s.at[peer], wkv_r.at[peer], peer).wait_recv()

    each_peer(anyone, wo_wait)
    for head in (0, 1):
        wide_sums[head * HD : (head + 1) * HD, :] = total_of(lambda index: wo_in[index], head)
    each_peer(anyone, wq_wait)
    for head in (0, 1):
        at = head * HD
        tall_sums[0, :, at : at + HD] = total_of(lambda index: wq_in[index], head)
    each_peer(anyone, sent_all)
    each_peer(anyone, wkv_wait)
    for head in (0, 1):
        at = head * HD
        total = total_of(lambda index: wkv_in[index], head)
        tall_sums[1, :, at : at + HD] = total[:, :HD]
        tall_sums[2, :, at : at + HD] = total[:, HD:]


def split_kernel(tall_sums, wide_sums, grad_query, grad_key, grad_value, grad_out):
    grad_query[...] = tall_sums[0]
    grad_key[...] = tall_sums[1]
    grad_value[...] = tall_sums[2]
    grad_out[...] = wide_sums[...]


def per_device(nctx, npb, *args):
    embed, w_query, w_key, w_value, w_out, ids, pad_embed, table, w_link, w_mix, w_lo, w_vocab = args
    rows, wide = embed.shape
    patches = rows // npb
    groups = 2
    local_rows = patches // groups * PATCH
    local_wide = w_link.shape[1]
    chips = nctx // 2
    block = wide // nctx
    vmem = pltpu.VMEM
    dma = pltpu.SemaphoreType.DMA
    near = [w_query, w_key, w_value, w_out, table, w_link, w_mix, w_lo, w_vocab]
    scratch = [vmem(array.shape, BF) for array in near]
    scratch += [
        dma((len(near) + 2,)),
        vmem((2, rows, wide), BF),
        vmem((2, rows, HD), F32),
        vmem((wide, 2 * rows), BF),
        vmem((2, 2, rows, HD), BF),
        vmem((2, nctx, rows, HD), BF),
        vmem((2, rows, HD), BF),
        vmem((nctx, rows, HD), BF),
        vmem((2, rows, HD), F32),
        vmem((2, rows, HD), F32),
        vmem((2, rows, HD), F32),
        vmem((2, rows, HD), BF),
        vmem((2, rows, HD), BF),
        vmem((2, rows, HD), F32),
        vmem((chips, 2, 8, rows), F32),
        vmem((npb, patches, wide), BF),
        vmem((npb, patches, wide), BF),
        vmem((groups, local_rows, local_wide), F32),
        vmem((local_rows, 3 * local_wide), BF),
        vmem((local_wide // LHD, local_rows, local_rows), F32),
        vmem((local_wide // LHD, local_rows, local_rows), F32),
        vmem((local_rows, 3 * local_wide), BF),
        vmem((PATCH, HD), jnp.int32),
        vmem((groups, local_rows, HD), jnp.int32),
        vmem((2, npb, patches, wide), BF),
        vmem((2, npb + 1, patches, HD), BF),
        vmem((nctx, npb + 1, patches, HD), BF),
        vmem((2, rows, HD), F32),
        vmem((2, rows, HD), F32),
        vmem((2, rows, HD), F32),
        vmem((nctx, HD, block), BF),
        vmem((nctx, block, HD), BF),
        vmem((nctx, block, 2 * HD), BF),
        vmem((nctx, HD, block), BF),
        vmem((nctx, block, HD), BF),
        vmem((nctx, block, 2 * HD), BF),
    ]
    scratch += [dma((nctx,))] * 10
    scratch += [dma((chips,))] * 2
    scratch += [dma((groups, npb))] * 4
    scratch += [dma] * 4 + [dma((groups,))] * 2 + [dma((groups, nctx))] * 2
    scratch += [dma((2,)), dma((groups, 2))]
    whole = pl.BlockSpec(memory_space=pltpu.VMEM)
    far = pl.BlockSpec(memory_space=pl.ANY)
    tall = jax.ShapeDtypeStruct((block, 2 * HD), BF)
    sums = pl.pallas_call(
        functools.partial(step_kernel, (nctx, npb)),
        out_shape=(
            jax.ShapeDtypeStruct((3, block, 2 * HD), BF),
            jax.ShapeDtypeStruct((2 * HD, block), BF),
        ),
        in_specs=[far] * 5 + [whole] * 2 + [far] * 5,
        out_specs=(whole,) * 2,
        scratch_shapes=scratch,
        compiler_params=pltpu.CompilerParams(
            collective_id=0, has_side_effects=True, vmem_limit_bytes=56 * 1024 * 1024
        ),
        name="step",
    )(
        embed, w_query, w_key, w_value, w_out, ids.T, pad_embed, table, w_link, w_mix,
        w_lo, w_vocab,
    )
    return pl.pallas_call(
        split_kernel,
        out_shape=(tall, tall, tall, jax.ShapeDtypeStruct((2 * HD, block), BF)),
        in_specs=[whole] * 2,
        out_specs=(whole,) * 4,
        name="split",
    )(*sums)


def solution(mesh):
    in_specs = (
        P("ctx", None),
        P(None, "pb"),
        P(None, "pb"),
        P(None, "pb"),
        P("pb", None),
        P(("ctx", "pb"), None),
        P(),
        P(),
        P(),
        P(),
        P(),
        P(),
    )
    out_specs = (P("ctx", "pb"), P("ctx", "pb"), P("ctx", "pb"), P("pb", "ctx"))
    return jax.shard_map(
        functools.partial(per_device, mesh.shape["ctx"], mesh.shape["pb"]),
        mesh=mesh,
        in_specs=in_specs,
        out_specs=out_specs,
        check_vma=False,
    )
```

```python
import functools

import jax
import jax.numpy as jnp
from jax import lax
from jax.experimental import pallas as pl
from jax.experimental.pallas import tpu as pltpu
from jax.sharding import PartitionSpec as P

HD = 128
LHD = 64
PATCH = 8
EPSILON = 1e-06
MASKED = -1e30
MESH = pl.DeviceIdType.MESH
BF = jnp.bfloat16
F32 = jnp.float32


def nn(left, right):
    return lax.dot_general(left, right, (((1,), (0,)), ((), ())), preferred_element_type=F32)


def nt(left, right):
    return lax.dot_general(left, right, (((1,), (1,)), ((), ())), preferred_element_type=F32)


def tn(left, right):
    return lax.dot_general(left, right, (((0,), (0,)), ((), ())), preferred_element_type=F32)


def loop(low, high, body):
    def step(index, unused):
        body(index)
        return unused

    lax.fori_loop(low, high, step, 0)


def row_form(column, rows):
    return jnp.transpose(jnp.broadcast_to(column, (rows, HD)))[0:8]


def rms_inverse(values):
    return lax.rsqrt(jnp.mean(values * values, axis=1, keepdims=True) + EPSILON)


def rms_back(values, inverse, grad):
    width = values.shape[1]
    dots = jnp.sum(grad * values, axis=1, keepdims=True)
    return inverse * grad - values * (inverse * inverse * inverse * dots * (1.0 / width))


def step_kernel(
    sizes,
    embed_far,
    w_query_far,
    w_key_far,
    w_value_far,
    w_out_far,
    ids,
    pad_embed,
    table_far,
    w_link_far,
    w_mix_far,
    w_local_out_far,
    w_vocab_far,
    tall_sums,
    wide_sums,
    w_query,
    w_key,
    w_value,
    w_out,
    table,
    w_link,
    w_mix,
    w_local_out,
    w_vocab,
    load_s,
    inputs,
    row_scale,
    inputs_turned,
    kv_send,
    kv_all,
    q_send,
    q_all,
    run_max,
    run_sum,
    run_out,
    att_head,
    att_pair,
    lse_col,
    lse_all,
    glob_part,
    glob_in,
    hidden,
    mixed,
    weights,
    d_weights,
    d_mixed,
    ids_wide,
    targets_all,
    grad_all,
    da_send,
    da_all,
    dq_acc,
    dk_acc,
    dv_acc,
    wo_send,
    wq_send,
    wkv_send,
    wo_in,
    wq_in,
    wkv_in,
    kv_s,
    kv_r,
    q_s,
    q_r,
    wo_s,
    wo_r,
    wq_s,
    wq_r,
    wkv_s,
    wkv_r,
    lse_s,
    lse_r,
    glob_s,
    glob_r,
    grad_s,
    grad_r,
    norm_s,
    norm_r,
    att_s,
    att_r,
    full_s,
    full_r,
    da_s,
    da_r,
    kv_forward_s,
    da_forward_s,
):
    nctx, npb = sizes
    chips = nctx // 2
    rows, wide = embed_far.shape
    patches = rows // npb
    bytes_here = patches * PATCH
    scale = HD ** (-0.5)
    place = lax.axis_index("ctx")
    part = lax.axis_index("pb")
    chip = lax.div(place, 2)
    core = lax.rem(place, 2)
    other = place + 1 - 2 * core

    def ctx_copy(src, dst, send, recv, peer):
        return pltpu.make_async_remote_copy(
            src_ref=src,
            dst_ref=dst,
            send_sem=send,
            recv_sem=recv,
            device_id=(peer, part),
            device_id_type=MESH,
        )

    def pb_copy(src, dst, send, recv, peer):
        return pltpu.make_async_remote_copy(
            src_ref=src,
            dst_ref=dst,
            send_sem=send,
            recv_sem=recv,
            device_id=(place, peer),
            device_id_type=MESH,
        )

    def each_peer(wanted, action):
        def one(step):
            peer = lax.rem(place + nctx - step, nctx)

            @pl.when(wanted(lax.div(peer, 2)))
            def _():
                action(peer)

        loop(1, nctx, one)

    def each_part(action):
        loop(1, npb, lambda step: action(lax.rem(part + step, npb)))

    half_rows = rows // 2
    pairs_in = (
        (embed_far.at[0:half_rows], inputs.at[core, 0:half_rows]),
        (embed_far.at[half_rows:rows], inputs.at[core, half_rows:rows]),
        (w_key_far, w_key),
        (w_value_far, w_value),
        (w_query_far, w_query),
        (w_out_far, w_out),
        (table_far, table),
        (w_link_far, w_link),
        (w_mix_far, w_mix),
        (w_local_out_far, w_local_out),
        (w_vocab_far, w_vocab),
    )
    loads = [
        pltpu.make_async_copy(far, near, load_s.at[index])
        for index, (far, near) in enumerate(pairs_in)
    ]
    for load in loads[:4]:
        load.start()

    later = lambda at: at >= chip
    earlier = lambda at: at <= chip
    anyone = lambda at: at >= 0

    def crossing(at, rows_away):
        return jnp.logical_and(lax.div(at, 2) - lax.div(chip, 2) == rows_away, lax.rem(at, 2) != lax.rem(chip, 2))

    later_direct = lambda at: jnp.logical_and(later(at), jnp.logical_not(crossing(at, 2)))
    earlier_direct = lambda at: jnp.logical_and(earlier(at), jnp.logical_not(crossing(at, -2)))
    neighbour = 2 * (chip + 1 - 2 * lax.rem(chip, 2)) + core

    barrier = pltpu.get_barrier_semaphore()

    def greet_ctx(peer):
        pl.semaphore_signal(barrier, inc=1, device_id=(peer, part), device_id_type=MESH)

    def greet_part(peer):
        pl.semaphore_signal(barrier, inc=1, device_id=(place, peer), device_id_type=MESH)

    each_peer(anyone, greet_ctx)
    each_part(greet_part)

    tile_rows = min(32, rows)

    def scale_rows(index):
        for low in range(0, rows, tile_rows):
            values = inputs[index, low : low + tile_rows, :].astype(F32)
            row_scale[index, low : low + tile_rows] = jnp.broadcast_to(
                rms_inverse(values), (tile_rows, HD)
            )

    loads[0].wait()
    loads[1].wait()
    loads[4].start()
    scale_rows(core)
    own_inputs = inputs[core]

    def scaled(product):
        return (product * row_scale[core, :, 0:1]).astype(BF)

    for slot, weight in ((0, w_key), (1, w_value)):
        loads[2 + slot].wait()
        product = scaled(nn(own_inputs, weight[...]))
        kv_send[0, slot] = product[:, :HD]
        kv_send[1, slot] = product[:, HD:]
    pl.semaphore_wait(barrier, nctx + npb - 2)

    def kv_copy(peer):
        return ctx_copy(
            kv_send.at[lax.rem(peer, 2)], kv_all.at[:, place], kv_s.at[peer], kv_r.at[place], peer
        )

    def kv_start(step):
        peer = lax.rem(place + step, nctx)
        at = lax.div(peer, 2)

        @pl.when(jnp.logical_and(later_direct(at), at != chip + 4))
        def _():
            kv_copy(peer).start()

    @pl.when(chip < chips - 4)
    def _():
        for side in (0, 1):
            kv_copy(2 * (chip + 4) + side).start()

    loop(1, nctx, kv_start)
    for load in loads[5:]:
        load.start()
    kv_all[:, place] = kv_send[core]
    loads[4].wait()
    product = scaled(nn(own_inputs, w_query[...]))
    q_send[0] = product[:, :HD]
    q_send[1] = product[:, HD:]

    def q_copy(peer):
        return ctx_copy(q_send.at[lax.rem(peer, 2)], q_all.at[place], q_s.at[peer], q_r.at[place], peer)

    q_copy(other).start()
    q_all[place] = q_send[core]

    def norm_copy(index):
        return ctx_copy(inputs.at[index], inputs.at[index], norm_s, norm_r, other)

    norm_copy(core).start()
    strictly_earlier = lambda at: at < chip
    each_peer(strictly_earlier, lambda peer: q_copy(peer).start())

    def kv_wait(peer):
        ctx_copy(kv_send.at[0], kv_all.at[:, peer], kv_s.at[peer], kv_r.at[peer], peer).wait_recv()

    def q_wait(peer):
        ctx_copy(q_send.at[0], q_all.at[peer], q_s.at[peer], q_r.at[peer], peer).wait_recv()

    first = 2 * chip
    pair_rows = 2 * rows

    def keys_of(at):
        return kv_all[0, pl.ds(2 * at, 2)].reshape(pair_rows, HD)

    def values_of(at):
        return kv_all[1, pl.ds(2 * at, 2)].reshape(pair_rows, HD)

    def diagonal(half, keys_down):
        shape = (rows, pair_rows)
        here = lax.broadcasted_iota(jnp.int32, shape, 0) + half * rows
        there = lax.broadcasted_iota(jnp.int32, shape, 1)
        return (there >= here) if keys_down else (there <= here)

    run_max[...] = jnp.full(run_max.shape, MASKED, F32)
    run_sum[...] = jnp.zeros(run_sum.shape, F32)
    run_out[...] = jnp.zeros(run_out.shape, F32)

    def attend(half, at, on_diagonal):
        scores = nt(q_all[first + half], keys_of(at)) * scale
        if on_diagonal:
            scores = jnp.where(diagonal(half, False), scores, MASKED)
        before = run_max[half, :, 0:1]
        highest = jnp.maximum(before, jnp.max(scores, axis=1, keepdims=True))
        exps = jnp.exp(scores - highest)
        factor = jnp.exp(before - highest)
        total = run_sum[half, :, 0:1] * factor + jnp.sum(exps, axis=1, keepdims=True)
        run_out[half] = run_out[half] * factor + nn(exps.astype(BF), values_of(at))
        run_max[half] = jnp.broadcast_to(highest, (rows, HD))
        run_sum[half] = jnp.broadcast_to(total, (rows, HD))

    kv_wait(other)
    q_wait(other)
    for half in (0, 1):
        attend(half, chip, True)
    for load in loads[5:]:
        load.wait()

    def kv_forward(side):
        source = 2 * (chip - 4) + side
        block = kv_all.at[:, source]
        return ctx_copy(block, block, kv_forward_s.at[side], kv_r.at[source], neighbour)

    @pl.when(chip >= 4)
    def _():
        for side in (0, 1):
            kv_wait(2 * (chip - 4) + side)
            kv_forward(side).start()
        for half in (0, 1):
            attend(half, chip - 4, False)

    def attend_earlier(step):
        at = chip - step

        @pl.when(step != 4)
        def _():
            kv_wait(2 * at)
            kv_wait(2 * at + 1)
            for half in (0, 1):
                attend(half, at, False)

    loop(1, chip + 1, attend_earlier)
    for half in (0, 1):
        att_head[half] = (run_out[half] / run_sum[half]).astype(BF)
        log_total = run_max[half] + jnp.log(run_sum[half])
        lse_col[half] = log_total
        lse_all[chip, half] = jnp.transpose(log_total)[0:8]

    def att_copy():
        return ctx_copy(att_head.at[1 - core], att_pair.at[core], att_s, att_r, other)

    att_copy().start()
    att_pair[core] = att_head[core]

    def lse_copy(at):
        return ctx_copy(
            lse_all.at[chip], lse_all.at[chip], lse_s.at[at], lse_r.at[chip], 2 * at + core
        )

    loop(0, chip, lambda at: lse_copy(at).start())
    ctx_copy(att_head.at[0], att_pair.at[1 - core], att_s, att_r, other).wait_recv()

    both_heads = jnp.concatenate([att_pair[0], att_pair[1]], axis=1)
    out_tile = min(512, wide)

    def out_columns(step):
        here = pl.ds(pl.multiple_of(step * out_tile, out_tile), out_tile)
        product = nn(both_heads, w_out[:, here]).astype(BF)
        glob_part[:, :, here] = product.reshape(npb, patches, out_tile)

    loop(0, wide // out_tile, out_columns)

    groups = 2
    share = patches // groups

    def glob_copy(group, peer):
        here = pl.ds(pl.multiple_of(group * share, share), share)
        return pb_copy(
            glob_part.at[peer, here],
            glob_in.at[part, here],
            glob_s.at[group, peer],
            glob_r.at[group, part],
            peer,
        )

    def glob_wait(group, peer):
        here = pl.ds(pl.multiple_of(group * share, share), share)
        pb_copy(
            glob_part.at[0, here],
            glob_in.at[peer, here],
            glob_s.at[group, peer],
            glob_r.at[group, peer],
            peer,
        ).wait_recv()

    for group in range(groups):
        each_part(lambda peer: glob_copy(group, peer).start())
    glob_in[part] = glob_part[part]

    count = share * PATCH
    byte_wide = wide // PATCH
    local_wide = w_link.shape[1]
    pairs = local_wide // (2 * LHD)
    symbols = lax.broadcasted_iota(jnp.int32, (count, table.shape[0]), 1)
    nothing = jnp.full((share, 1), -1, jnp.int32)
    ids_wide[:, 0:patches] = ids[...]
    for group in range(groups):
        columns = []
        for b in range(PATCH):
            line = jnp.broadcast_to(ids_wide[b : b + 1, :], (HD, HD))
            columns.append(jnp.transpose(line)[group * share : (group + 1) * share, 0:1])
        preceding = jnp.concatenate([nothing] + columns[:-1], axis=0)
        targets_all[group] = jnp.broadcast_to(jnp.concatenate(columns, axis=0), (count, HD))
        hidden[group] = nn((preceding == symbols).astype(BF), table[...]) + jnp.where(
            preceding < 0, pad_embed[...].astype(F32).reshape(1, local_wide), 0.0
        )
    row_index = lax.broadcasted_iota(jnp.int32, (count, count), 0)
    column_index = lax.broadcasted_iota(jnp.int32, (count, count), 1)
    same = jnp.logical_and(
        lax.rem(row_index, share) == lax.rem(column_index, share), column_index <= row_index
    )
    lane = lax.broadcasted_iota(jnp.int32, (count, 2 * LHD), 1)
    halves = (lane < LHD, lane >= LHD)

    def pair_of(block, pair):
        low = block * local_wide + pair * 2 * LHD
        return mixed[:, low : low + 2 * LHD]

    def kept(values, side):
        return jnp.where(halves[side], values, jnp.zeros_like(values))

    def grad_copy(group, peer):
        mine = grad_all.at[core, part, pl.ds(pl.multiple_of(group * share, share), share)]
        return pb_copy(mine, mine, grad_s.at[group, peer], grad_r.at[group, part], peer)

    def grad_wait(group, peer):
        theirs = grad_all.at[core, peer, pl.ds(pl.multiple_of(group * share, share), share)]
        pb_copy(theirs, theirs, grad_s.at[group, peer], grad_r.at[group, peer], peer).wait_recv()

    def local_model(group):
        here = pl.ds(pl.multiple_of(group * share, share), share)
        each_part(lambda peer: glob_wait(group, peer))
        glob = glob_in[0, here, :].astype(F32)
        for index in range(1, npb):
            glob = glob + glob_in[index, here, :].astype(F32)
        glob = glob.astype(BF)
        pieces = jnp.concatenate(
            [glob[:, b * byte_wide : (b + 1) * byte_wide] for b in range(PATCH)], axis=0
        )
        hidden_one = hidden[group] + nn(pieces, w_link[...])
        hidden[group] = hidden_one
        inverse_one = rms_inverse(hidden_one)
        mixed[...] = nn((hidden_one * inverse_one).astype(BF), w_mix[...]).astype(BF)
        heads = 2 * pairs
        for head in range(heads):
            query = kept(pair_of(0, head // 2), head % 2)
            weights[head] = nt(query, pair_of(1, head // 2))
        scores = jnp.where(same[None], weights[...] * LHD ** (-0.5), MASKED)
        exps = jnp.exp(scores - jnp.max(scores, axis=2, keepdims=True))
        weights[...] = exps / jnp.sum(exps, axis=2, keepdims=True)
        local_att = []
        for pair in range(pairs):
            terms = [
                nn(weights[2 * pair + side].astype(BF), kept(pair_of(2, pair), side))
                for side in (0, 1)
            ]
            local_att.append((terms[0] + terms[1]).astype(BF))
        hidden_two = hidden[group] + nn(jnp.concatenate(local_att, axis=1), w_local_out[...])
        inverse_two = rms_inverse(hidden_two)
        logits = nn((hidden_two * inverse_two).astype(BF), w_vocab[...])
        exps = jnp.exp(logits - jnp.max(logits, axis=1, keepdims=True))
        soft = exps / jnp.sum(exps, axis=1, keepdims=True)
        d_logits = (
            soft - jnp.where(targets_all[group, :, 0:1] == symbols, 1.0, 0.0)
        ) * (1.0 / (rows * nctx * PATCH))
        d_normed_two = nt(d_logits.astype(BF), w_vocab[...]).astype(BF).astype(F32)
        d_hidden = rms_back(hidden_two, inverse_two, d_normed_two)
        d_local_att = nt(d_hidden.astype(BF), w_local_out[...]).astype(BF)
        d_heads = [
            kept(d_local_att[:, pair * 2 * LHD : (pair + 1) * 2 * LHD], side)
            for pair in range(pairs)
            for side in (0, 1)
        ]
        for head in range(heads):
            d_weights[head] = nt(d_heads[head], pair_of(2, head // 2))
        d_soft = d_weights[...].astype(BF).astype(F32)
        soft = weights[...]
        dots = jnp.sum(d_soft * soft, axis=2, keepdims=True)
        d_weights[...] = soft * (d_soft - dots) * LHD ** (-0.5)
        for pair in range(pairs):
            terms = [[], [], []]
            for side in (0, 1):
                head = 2 * pair + side
                d_scores = d_weights[head].astype(BF)
                terms[0].append(nn(d_scores, kept(pair_of(1, pair), side)))
                terms[1].append(tn(d_scores, kept(pair_of(0, pair), side)))
                terms[2].append(tn(weights[head].astype(BF), d_heads[head]))
            for block in range(3):
                at = block * local_wide + pair * 2 * LHD
                d_mixed[:, at : at + 2 * LHD] = (terms[block][0] + terms[block][1]).astype(BF)
        d_normed_one = nt(d_mixed[...], w_mix[...]).astype(BF).astype(F32)
        hidden_one = hidden[group]
        d_hidden = d_hidden + rms_back(hidden_one, rms_inverse(hidden_one), d_normed_one)
        d_pieces = nt(d_hidden.astype(BF), w_link[...]).astype(BF)
        for b in range(PATCH):
            grad_all[core, part, here, b * byte_wide : (b + 1) * byte_wide] = d_pieces[
                b * share : (b + 1) * share
            ]
        each_part(lambda peer: grad_copy(group, peer).start())

    norm_copy(1 - core).wait_recv()
    scale_rows(1 - core)
    turn_tile = min(128, wide)

    def turn_columns(step):
        here = pl.ds(pl.multiple_of(step * turn_tile, turn_tile), turn_tile)
        block = inputs[:, :, here].reshape(pair_rows, turn_tile)
        inputs_turned[here, :] = jnp.transpose(block.astype(F32)).astype(BF)

    loop(0, wide // turn_tile, turn_columns)

    each_peer(later_direct, lambda peer: kv_copy(peer).wait_send())

    @pl.when(chip >= 4)
    def _():
        for side in (0, 1):
            kv_forward(side).wait_send()

    each_peer(earlier, lambda peer: q_copy(peer).wait_send())
    loop(0, chip, lambda at: lse_copy(at).wait_send())
    norm_copy(core).wait_send()
    att_copy().wait_send()

    loop(0, groups, local_model)
    def full_copy(group, index):
        here = pl.ds(group * share, share)
        block = grad_all.at[index, :, here]
        return ctx_copy(block, block, full_s.at[group], full_r.at[group], other)

    last = groups - 1

    def da_parts(group, whole):
        return whole.at[0 : npb + 1 if group == last else npb, group * share : (group + 1) * share]

    def da_copy(group, peer):
        return ctx_copy(
            da_parts(group, da_send.at[lax.rem(peer, 2)]),
            da_parts(group, da_all.at[place]),
            da_s.at[group, peer],
            da_r.at[group, place],
            peer,
        )

    def da_wait_part(group, peer):
        ctx_copy(
            da_parts(group, da_send.at[0]),
            da_parts(group, da_all.at[peer]),
            da_s.at[group, peer],
            da_r.at[group, peer],
            peer,
        ).wait_recv()

    def da_wait(peer):
        for group in range(groups):
            da_wait_part(group, peer)

    def da_forward(group, side):
        source = 2 * (chip + 4) + side
        block = da_parts(group, da_all.at[source])
        return ctx_copy(
            block, block, da_forward_s.at[group, side], da_r.at[group, source], neighbour
        )

    for group in range(groups):
        each_part(lambda peer: grad_wait(group, peer))
        full_copy(group, core).start()
        here = slice(group * share, (group + 1) * share)
        grads = grad_all[core, :, here, :].reshape(npb * share, wide)
        product = nt(grads, w_out[...]).astype(BF)
        for head in (0, 1):
            d_att = product[:, head * HD : (head + 1) * HD]
            da_send[head, 0:npb, here, :] = d_att.reshape(npb, share, HD)
        if group == last:
            for head in (0, 1):
                d_att = da_send[head, 0:npb].reshape(rows, HD).astype(F32)
                dots = jnp.sum(d_att * att_pair[head].astype(F32), axis=1, keepdims=True)
                exact = row_form(dots, rows)
                high = exact.astype(BF)
                low = (exact - high.astype(F32)).astype(BF)
                spare = jnp.concatenate([high[0:1], low[0:1]], axis=0)
                tail = [spare[:, at : at + HD] for at in range(0, rows, HD)]
                filler = jnp.zeros((share - 2 * len(tail), HD), BF)
                da_send[head, npb, here, :] = jnp.concatenate(tail + [filler], axis=0)
        da_copy(group, other).start()

        def da_start(peer):
            @pl.when(earlier_direct(lax.div(peer, 2)))
            def _():
                da_copy(group, peer).start()

        loop(0, 2 * chip, da_start)

    def grads_of(device):
        return da_all[device, 0:npb].reshape(rows, HD)

    def dots_of(device):
        tail = da_all[device, npb, last * share : (last + 1) * share].astype(F32)
        pieces = [
            tail[2 * at : 2 * at + 1] + tail[2 * at + 1 : 2 * at + 2] for at in range(rows // HD)
        ]
        return jnp.concatenate(pieces, axis=1)

    da_all[place] = da_send[core]

    block_wide = wide // nctx
    term_rows = min(512, wide)
    owners = term_rows // block_wide

    def wo_copy(peer):
        return ctx_copy(wo_send.at[peer], wo_in.at[place], wo_s.at[peer], wo_r.at[place], peer)

    def wq_copy(peer):
        return ctx_copy(wq_send.at[peer], wq_in.at[place], wq_s.at[peer], wq_r.at[place], peer)

    def wkv_copy(peer):
        return ctx_copy(wkv_send.at[peer], wkv_in.at[place], wkv_s.at[peer], wkv_r.at[place], peer)

    def in_turn(make, copy):
        steps = wide // term_rows

        def one(step):
            block = lax.rem(lax.div(place, owners) + step, steps)
            make(block)
            for index in range(owners):
                peer = block * owners + index

                @pl.when(peer != place)
                def _():
                    copy(peer).start()

        loop(0, steps, one)

    for group in range(groups):
        full_copy(group, 1 - core).wait_recv()
    att_turned = jnp.transpose(att_head[...].reshape(pair_rows, HD).astype(F32)).astype(BF)

    def wo_block(step):
        here = pl.ds(pl.multiple_of(step * term_rows, term_rows), term_rows)
        grads = grad_all[:, :, :, here].reshape(pair_rows, term_rows)
        terms = nn(att_turned, grads).astype(BF)
        for index in range(owners):
            wo_send[step * owners + index] = terms[:, index * block_wide : (index + 1) * block_wide]

    in_turn(wo_block, wo_copy)
    wo_in[place] = wo_send[place]
    da_wait(other)

    dq_acc[...] = jnp.zeros(dq_acc.shape, F32)

    def query_back(half, at, on_diagonal):
        scores = nt(q_all[first + half], keys_of(at)) * scale
        probs = jnp.exp(scores - lse_col[half, :, 0:1])
        if on_diagonal:
            probs = jnp.where(diagonal(half, False), probs, 0.0)
        d_probs = nt(grads_of(first + half), values_of(at))
        d_scores = (probs * (d_probs - run_sum[half, :, 0:1]) * scale).astype(BF)
        dq_acc[half] += nn(d_scores, keys_of(at))

    for half in (0, 1):
        dots = jnp.sum(
            grads_of(first + half).astype(F32) * att_head[half].astype(F32), axis=1, keepdims=True
        )
        run_sum[half] = jnp.broadcast_to(dots, (rows, HD))
    for half in (0, 1):
        query_back(half, chip, True)

    def query_earlier(step):
        for half in (0, 1):
            query_back(half, chip - step, False)

    loop(1, chip + 1, query_earlier)

    dq_ready = (dq_acc[...] * row_scale[...]).reshape(pair_rows, HD).astype(BF)

    def wq_block(step):
        here = pl.ds(pl.multiple_of(step * term_rows, term_rows), term_rows)
        terms = nn(inputs_turned[here, :], dq_ready).astype(BF)
        wq_send[pl.ds(step * owners, owners)] = terms.reshape(owners, block_wide, HD)

    in_turn(wq_block, wq_copy)
    wq_in[place] = wq_send[place]

    dk_acc[...] = jnp.zeros(dk_acc.shape, F32)
    dv_acc[...] = jnp.zeros(dv_acc.shape, F32)

    def key_back(half, at, on_diagonal):
        queries = q_all[pl.ds(2 * at, 2)].reshape(pair_rows, HD)
        grads = da_all[pl.ds(2 * at, 2), 0:npb].reshape(pair_rows, HD)
        log_total = jnp.concatenate([lse_all[at, 0, 0:1, :], lse_all[at, 1, 0:1, :]], axis=1)
        dots = jnp.concatenate([dots_of(2 * at), dots_of(2 * at + 1)], axis=1)
        scores = nt(kv_all[0, first + half], queries) * scale
        probs = jnp.exp(scores - log_total)
        if on_diagonal:
            probs = jnp.where(diagonal(half, True), probs, 0.0)
        d_probs = nt(kv_all[1, first + half], grads)
        d_scores = (probs * (d_probs - dots) * scale).astype(BF)
        dv_acc[half] += nn(probs.astype(BF), grads)
        dk_acc[half] += nn(d_scores, queries)

    for half in (0, 1):
        key_back(half, chip, True)

    def rest_wait(at):
        q_wait(2 * at)
        q_wait(2 * at + 1)
        ctx_copy(
            lse_all.at[at], lse_all.at[at], lse_s.at[at], lse_r.at[at], 2 * at + core
        ).wait_recv()

    @pl.when(chip < chips - 4)
    def _():
        for group in range(groups):
            for side in (0, 1):
                da_wait_part(group, 2 * (chip + 4) + side)
                da_forward(group, side).start()
        rest_wait(chip + 4)
        for half in (0, 1):
            key_back(half, chip + 4, False)

    def key_later(at):
        @pl.when(at != chip + 4)
        def _():
            da_wait(2 * at)
            da_wait(2 * at + 1)
            rest_wait(at)
            for half in (0, 1):
                key_back(half, at, False)

    loop(chip + 1, chips, key_later)
    dkv_ready = jnp.concatenate(
        [
            (total[...] * row_scale[...]).reshape(pair_rows, HD).astype(BF)
            for total in (dk_acc, dv_acc)
        ],
        axis=1,
    )

    def wkv_block(step):
        here = pl.ds(pl.multiple_of(step * term_rows, term_rows), term_rows)
        terms = nn(inputs_turned[here, :], dkv_ready).astype(BF)
        wkv_send[pl.ds(step * owners, owners)] = terms.reshape(owners, block_wide, 2 * HD)

    in_turn(wkv_block, wkv_copy)
    wkv_in[place] = wkv_send[place]

    def sent_part(peer):
        for group in range(groups):
            glob_copy(group, peer).wait_send()
            grad_copy(group, peer).wait_send()

    each_part(sent_part)

    def sent_earlier(peer):
        for group in range(groups):
            da_copy(group, peer).wait_send()

    each_peer(earlier_direct, sent_earlier)

    @pl.when(chip < chips - 4)
    def _():
        for side in (0, 1):
            for group in range(groups):
                da_forward(group, side).wait_send()

    for group in range(groups):
        full_copy(group, core).wait_send()

    def sent_all(peer):
        wo_copy(peer).wait_send()
        wq_copy(peer).wait_send()
        wkv_copy(peer).wait_send()

    def total_of(pick, head):
        total = pick(head).astype(F32)
        for index in range(1, chips):
            total = total + pick(2 * index + head).astype(F32)
        return total.astype(BF)

    def wo_wait(peer):
        ctx_copy(wo_send.at[0], wo_in.at[peer], wo_s.at[peer], wo_r.at[peer], peer).wait_recv()

    def wq_wait(peer):
        ctx_copy(wq_send.at[0], wq_in.at[peer], wq_s.at[peer], wq_r.at[peer], peer).wait_recv()

    def wkv_wait(peer):
        ctx_copy(wkv_send.at[0], wkv_in.at[peer], wkv_s.at[peer], wkv_r.at[peer], peer).wait_recv()

    each_peer(anyone, wo_wait)
    for head in (0, 1):
        wide_sums[head * HD : (head + 1) * HD, :] = total_of(lambda index: wo_in[index], head)
    each_peer(anyone, wq_wait)
    for head in (0, 1):
        at = head * HD
        tall_sums[0, :, at : at + HD] = total_of(lambda index: wq_in[index], head)
    each_peer(anyone, sent_all)
    each_peer(anyone, wkv_wait)
    for head in (0, 1):
        at = head * HD
        total = total_of(lambda index: wkv_in[index], head)
        tall_sums[1, :, at : at + HD] = total[:, :HD]
        tall_sums[2, :, at : at + HD] = total[:, HD:]


def split_kernel(tall_sums, wide_sums, grad_query, grad_key, grad_value, grad_out):
    grad_query[...] = tall_sums[0]
    grad_key[...] = tall_sums[1]
    grad_value[...] = tall_sums[2]
    grad_out[...] = wide_sums[...]


def per_device(nctx, npb, *args):
    embed, w_query, w_key, w_value, w_out, ids, pad_embed, table, w_link, w_mix, w_lo, w_vocab = args
    rows, wide = embed.shape
    patches = rows // npb
    groups = 2
    local_rows = patches // groups * PATCH
    local_wide = w_link.shape[1]
    chips = nctx // 2
    block = wide // nctx
    vmem = pltpu.VMEM
    dma = pltpu.SemaphoreType.DMA
    near = [w_query, w_key, w_value, w_out, table, w_link, w_mix, w_lo, w_vocab]
    scratch = [vmem(array.shape, BF) for array in near]
    scratch += [
        dma((len(near) + 2,)),
        vmem((2, rows, wide), BF),
        vmem((2, rows, HD), F32),
        vmem((wide, 2 * rows), BF),
        vmem((2, 2, rows, HD), BF),
        vmem((2, nctx, rows, HD), BF),
        vmem((2, rows, HD), BF),
        vmem((nctx, rows, HD), BF),
        vmem((2, rows, HD), F32),
        vmem((2, rows, HD), F32),
        vmem((2, rows, HD), F32),
        vmem((2, rows, HD), BF),
        vmem((2, rows, HD), BF),
        vmem((2, rows, HD), F32),
        vmem((chips, 2, 8, rows), F32),
        vmem((npb, patches, wide), BF),
        vmem((npb, patches, wide), BF),
        vmem((groups, local_rows, local_wide), F32),
        vmem((local_rows, 3 * local_wide), BF),
        vmem((local_wide // LHD, local_rows, local_rows), F32),
        vmem((local_wide // LHD, local_rows, local_rows), F32),
        vmem((local_rows, 3 * local_wide), BF),
        vmem((PATCH, HD), jnp.int32),
        vmem((groups, local_rows, HD), jnp.int32),
        vmem((2, npb, patches, wide), BF),
        vmem((2, npb + 1, patches, HD), BF),
        vmem((nctx, npb + 1, patches, HD), BF),
        vmem((2, rows, HD), F32),
        vmem((2, rows, HD), F32),
        vmem((2, rows, HD), F32),
        vmem((nctx, HD, block), BF),
        vmem((nctx, block, HD), BF),
        vmem((nctx, block, 2 * HD), BF),
        vmem((nctx, HD, block), BF),
        vmem((nctx, block, HD), BF),
        vmem((nctx, block, 2 * HD), BF),
    ]
    scratch += [dma((nctx,))] * 10
    scratch += [dma((chips,))] * 2
    scratch += [dma((groups, npb))] * 4
    scratch += [dma] * 4 + [dma((groups,))] * 2 + [dma((groups, nctx))] * 2
    scratch += [dma((2,)), dma((groups, 2))]
    whole = pl.BlockSpec(memory_space=pltpu.VMEM)
    far = pl.BlockSpec(memory_space=pl.ANY)
    tall = jax.ShapeDtypeStruct((block, 2 * HD), BF)
    sums = pl.pallas_call(
        functools.partial(step_kernel, (nctx, npb)),
        out_shape=(
            jax.ShapeDtypeStruct((3, block, 2 * HD), BF),
            jax.ShapeDtypeStruct((2 * HD, block), BF),
        ),
        in_specs=[far] * 5 + [whole] * 2 + [far] * 5,
        out_specs=(whole,) * 2,
        scratch_shapes=scratch,
        compiler_params=pltpu.CompilerParams(
            collective_id=0, has_side_effects=True, vmem_limit_bytes=56 * 1024 * 1024
        ),
        name="step",
    )(
        embed, w_query, w_key, w_value, w_out, ids.T, pad_embed, table, w_link, w_mix,
        w_lo, w_vocab,
    )
    return pl.pallas_call(
        split_kernel,
        out_shape=(tall, tall, tall, jax.ShapeDtypeStruct((2 * HD, block), BF)),
        in_specs=[whole] * 2,
        out_specs=(whole,) * 4,
        name="split",
    )(*sums)


def solution(mesh):
    in_specs = (
        P("ctx", None),
        P(None, "pb"),
        P(None, "pb"),
        P(None, "pb"),
        P("pb", None),
        P(("ctx", "pb"), None),
        P(),
        P(),
        P(),
        P(),
        P(),
        P(),
    )
    out_specs = (P("ctx", "pb"), P("ctx", "pb"), P("ctx", "pb"), P("pb", "ctx"))
    return jax.shard_map(
        functools.partial(per_device, mesh.shape["ctx"], mesh.shape["pb"]),
        mesh=mesh,
        in_specs=in_specs,
        out_specs=out_specs,
        check_vma=False,
    )
```
